128 devices in a mesh: fsdp: 4 (over x_lo, core), ctx: 32 (over z, y, x_hi).
Axes of the slice: x: 4 (x_hi: 2, x_lo: 2; x = x_hi * 2 + x_lo), y: 4, z: 4, core: 2. Of those that a mesh axis runs over, the one named last changes fastest.
Arguments:
- tokens: bfloat16 [16384, 1024], P(('fsdp', 'ctx')), may hold values from -6 to 6
- positions: int32 [16384], P(('fsdp', 'ctx')), may hold values from 0 to 4095, as said below
- attn_gain: bfloat16 [1024], P('fsdp'), may hold values from 0.5 to 1.5
- w_query: bfloat16 [1024, 2048], P('fsdp'), may hold values from -0.1875 to 0.1875
- w_key: bfloat16 [1024, 1024], P('fsdp'), may hold values from -0.1875 to 0.1875
- w_value: bfloat16 [1024, 1024], P('fsdp'), may hold values from -0.1875 to 0.1875
- query_gain: bfloat16 [128], P('fsdp'), may hold values from 0.5 to 1.5
- key_gain: bfloat16 [128], P('fsdp'), may hold values from 0.5 to 1.5
- w_out: bfloat16 [2048, 1024], P('fsdp'), may hold values from -4 to 4
- ffn_gain: bfloat16 [1024], P('fsdp'), may hold values from 0.5 to 1.5
- w_gate: bfloat16 [1024, 3072], P('fsdp'), may hold values from -0.1875 to 0.1875
- w_up: bfloat16 [1024, 3072], P('fsdp'), may hold values from -0.1875 to 0.1875
- w_down: bfloat16 [3072, 1024], P('fsdp'), may hold values from -0.109375 to 0.109375
- cotangent: bfloat16 [16384, 1024], P(('fsdp', 'ctx')), may hold values from -6 to 6
Outputs:
- output: bfloat16 [16384, 1024], P(('fsdp', 'ctx'))
- grad_tokens: float32 [16384, 1024], P(('fsdp', 'ctx'))
- grad_attn_gain: float32 [1024], P('fsdp')
- grad_w_query: float32 [1024, 2048], P('fsdp')
- grad_w_key: float32 [1024, 1024], P('fsdp')
- grad_w_value: float32 [1024, 1024], P('fsdp')
- grad_query_gain: float32 [128], P('fsdp')
- grad_key_gain: float32 [128], P('fsdp')
- grad_w_out: float32 [2048, 1024], P('fsdp')
- grad_ffn_gain: float32 [1024], P('fsdp')
- grad_w_gate: float32 [1024, 3072], P('fsdp')
- grad_w_up: float32 [1024, 3072], P('fsdp')
- grad_w_down: float32 [3072, 1024], P('fsdp')
The draws below stay inside these ranges and needn't reach their ends.
Inputs may be any that keep to these rules, and one draw needn't show every extreme that they name: Each sequence of 4096 tokens holds a first document of fewer than 128 tokens, possibly empty, and a second one from there to its end; positions count from 0 at each document's start; at least one sequence is a single document.
All inputs are finite; a program needn't handle non-finite values.
Results may differ from the reference program's by a relative error of at most 0.035.
Values may be sent and summed in bfloat16 or wider, within the bound.
No kernel may reach another device: no remote copies, remote signals or barrier semaphores. Data moves between devices by JAX's collectives and lax.ppermute only.
A program may use at most 192 MiB of HBM per device.

```python
import jax
import jax.numpy as jnp
from jax import lax

D = 1024
HQ = 16
HK = 8
DH = 128
FF = 3072
TOK_DEV = 128
LENGTH = 4096
SEQS = 4
TOKENS = 16384


def draw_positions(key, part):
    key = jax.random.fold_in(key, 11)
    first_key, pick_key = jax.random.split(key)
    starts = jax.random.randint(first_key, (SEQS,), 0, TOK_DEV)
    chosen = jax.random.randint(pick_key, (), 0, SEQS)
    starts = jnp.where(jnp.arange(SEQS) == chosen, 0, starts)
    index = jnp.arange(LENGTH, dtype=jnp.int32)
    within = jnp.where(index[None, :] < starts[:, None], index[None, :], index[None, :] - starts[:, None])
    return within.reshape(-1).astype(jnp.int32)


def shard_levels(stream_key, extent, cuts, low, high):
    factor_of, own = 1.0, jax.random.fold_in(stream_key, 6)
    for position, blocks in cuts:
        heights = jnp.exp(jax.random.uniform(jax.random.fold_in(own, position), (blocks,), jnp.float32, low / len(cuts), high / len(cuts)))
        factor_of = factor_of * jnp.repeat(heights, extent[position] // blocks).reshape([-1 if axis == position else 1 for axis in range(len(extent))])
    return factor_of


def gaussian(own_key, shape, width, most, shards=(), held_as=jnp.bfloat16):
    array = jax.random.normal(own_key, shape, jnp.float32) * width
    if len(shards) > 0:
        array = shard_levels(own_key, shape, shards, -0.22, 0.18) * array
    return jnp.clip(array, min=-most, max=most).astype(held_as)


def setup_inputs(seed: int = 0) -> dict:
    splits = jax.random.split(jax.random.key(seed), 15)
    tokens = gaussian(splits[0], (TOKENS, D), 1.0, 6.0, ((0, 128),))
    positions = draw_positions(jax.random.fold_in(splits[14], 71), 0)
    attn_gain = jnp.clip(1.0 + 0.1 * jax.random.normal(splits[2], (D,), jnp.float32), 0.5, 1.5).astype(jnp.bfloat16)
    w_query = gaussian(splits[3], (D, HQ * DH), D ** -0.5, 0.1875, ((0, 4),))
    w_key = gaussian(splits[4], (D, HK * DH), D ** -0.5, 0.1875, ((0, 4),))
    w_value = gaussian(splits[5], (D, HK * DH), D ** -0.5, 0.1875, ((0, 4),))
    query_gain = jnp.clip(1.0 + 0.1 * jax.random.normal(splits[6], (DH,), jnp.float32), 0.5, 1.5).astype(jnp.bfloat16)
    key_gain = jnp.clip(1.0 + 0.1 * jax.random.normal(splits[7], (DH,), jnp.float32), 0.5, 1.5).astype(jnp.bfloat16)
    w_out = gaussian(splits[8], (HQ * DH, D), (max(1, 4 * HQ * DH // LENGTH)) ** -0.5, 4.0, ((0, 4),))
    ffn_gain = jnp.clip(1.0 + 0.1 * jax.random.normal(splits[9], (D,), jnp.float32), 0.5, 1.5).astype(jnp.bfloat16)
    w_gate = gaussian(splits[10], (D, FF), D ** -0.5, 0.1875, ((0, 4),))
    w_up = gaussian(splits[11], (D, FF), D ** -0.5, 0.1875, ((0, 4),))
    w_down = gaussian(splits[12], (FF, D), FF ** -0.5, 0.109375, ((0, 4),))
    cotangent = gaussian(splits[13], (TOKENS, D), 1.0, 6.0, ((0, 128),))
    return {"tokens": tokens, "positions": positions, "attn_gain": attn_gain, "w_query": w_query, "w_key": w_key, "w_value": w_value, "query_gain": query_gain, "key_gain": key_gain, "w_out": w_out, "ffn_gain": ffn_gain, "w_gate": w_gate, "w_up": w_up, "w_down": w_down, "cotangent": cotangent}


EPSILON = 1e-06
THETA = 1000000.0
NEG_BIG = -1e+30

@jax.custom_vjp
def low(v):
    return lax.optimization_barrier(v.astype(jnp.bfloat16)).astype(jnp.float32)

@jax.custom_vjp
def low_back(v):
    return v

def low_keep(v):
    return (low(v), None)

def low_pass(kept, grad):
    return (grad,)

def back_keep(v):
    return (v, None)

def back_low(kept, grad):
    return (low(grad),)
low.defvjp(low_keep, low_pass)
low_back.defvjp(back_keep, back_low)

def precise_dot(left, right):
    return jnp.dot(left, right, precision=lax.Precision.HIGHEST)

def normalize(values_in, gain):
    return values_in * lax.rsqrt(lax.optimization_barrier(jnp.mean(values_in * values_in, axis=-1, keepdims=True)) + EPSILON) * gain

def rotary(values_in, where_at):
    feature_count = values_in.shape[-1]
    half_width = feature_count // 2
    frequency = THETA ** (-(jnp.arange(half_width, dtype=jnp.float32) * 2.0) / feature_count)
    angles = where_at.astype(jnp.float32)[:, None] * frequency[None, :]
    cosine = jnp.concatenate([jnp.cos(angles), jnp.cos(angles)], axis=-1)[:, None, :]
    sine = jnp.concatenate([jnp.sin(angles), jnp.sin(angles)], axis=-1)[:, None, :]
    front_half = values_in[..., :half_width]
    back_half = values_in[..., half_width:]
    turned = jnp.concatenate([-back_half, front_half], axis=-1)
    return values_in * cosine + turned * sine

def sequence_attention(packed):
    queries, key_heads, value_heads, where_at = packed
    length = queries.shape[0]
    heads_kv = key_heads.shape[1]
    group_size = queries.shape[1] // heads_kv
    block_size = min(512, length)
    block_total = length // block_size
    score_scale = queries.shape[-1] ** (-0.5)
    key_index = jnp.arange(length, dtype=jnp.int32)

    def one_block(block_number):
        first_index = (block_number * block_size).astype(jnp.int32)
        query_block = lax.dynamic_slice_in_dim(queries, first_index, block_size, 0)
        query_block = query_block.reshape(block_size, heads_kv, group_size, -1)
        where_block = lax.dynamic_slice_in_dim(where_at, first_index, block_size, 0)
        row_index = first_index + jnp.arange(block_size, dtype=jnp.int32)
        scores = jnp.einsum('qkgd,tkd->kgqt', query_block, key_heads, precision=lax.Precision.HIGHEST)
        scores = low_back(scores * score_scale)
        visible = (key_index[None, :] <= row_index[:, None]) & (key_index[None, :] >= (row_index - where_block)[:, None])
        scores = jnp.where(visible, scores, NEG_BIG)
        row_max = lax.optimization_barrier(jnp.max(scores, axis=-1, keepdims=True))
        weights = jnp.exp(scores - row_max)
        probability = low(weights / lax.optimization_barrier(jnp.sum(weights, axis=-1, keepdims=True)))
        mixed_out = jnp.einsum('kgqt,tkd->qkgd', probability, value_heads, precision=lax.Precision.HIGHEST)
        return mixed_out.reshape(block_size, heads_kv * group_size, -1)
    blocks = lax.map(jax.checkpoint(one_block), jnp.arange(block_total, dtype=jnp.int32))
    return blocks.reshape(length, heads_kv * group_size, -1)

def reference(tokens, positions, attn_gain, w_query, w_key, w_value, query_gain, key_gain, w_out, ffn_gain, w_gate, w_up, w_down, cotangent):
    floats = [member.astype(jnp.float32) for member in (tokens, attn_gain, w_query, w_key, w_value, query_gain, key_gain, w_out, ffn_gain, w_gate, w_up, w_down)]

    def layer(inputs, gain_one, query_weight, key_weight, value_weight, gain_query, gain_key, out_weight, gain_two, gate_weight, up_weight, down_weight):
        token_count = inputs.shape[0]
        normed_one = low(normalize(inputs, gain_one))
        query_raw = low_back(precise_dot(normed_one, query_weight)).reshape(token_count, HQ, DH)
        queries = low(rotary(normalize(query_raw, gain_query), positions))
        key_raw = low_back(precise_dot(normed_one, key_weight)).reshape(token_count, HK, DH)
        key_heads = low(rotary(normalize(key_raw, gain_key), positions))
        value_heads = low(low_back(precise_dot(normed_one, value_weight))).reshape(token_count, HK, DH)
        attended = lax.map(sequence_attention, (queries.reshape(SEQS, LENGTH, HQ, DH), key_heads.reshape(SEQS, LENGTH, HK, DH), value_heads.reshape(SEQS, LENGTH, HK, DH), positions.reshape(SEQS, LENGTH)))
        merged = low(low_back(attended.reshape(token_count, HQ * DH)))
        middle = inputs + low_back(precise_dot(merged, out_weight))
        normed_two = low(normalize(middle, gain_two))
        gate_value = low_back(precise_dot(normed_two, gate_weight))
        up_value = low_back(precise_dot(normed_two, up_weight))
        hidden = low(jax.nn.silu(gate_value) * up_value)
        return middle + low_back(precise_dot(hidden, down_weight))
    result, pullback = jax.vjp(layer, *floats)
    gradients = pullback(cotangent.astype(jnp.float32))
    return (result.astype(jnp.bfloat16), gradients[0], gradients[1], gradients[2], gradients[3], gradients[4], gradients[5], gradients[6], gradients[7], gradients[8], gradients[9], gradients[10], gradients[11])
```

```python
import jax
import jax.numpy as jnp
from jax import lax
from jax.experimental import pallas as pl
from jax.experimental.pallas import tpu as pltpu
from jax.sharding import Mesh
from jax.sharding import PartitionSpec as P

EPSILON = 1e-06
THETA = 1000000.0
HEAD = 128
ROWS = 128
CHUNK = 512
SCORE_SCALE = HEAD ** (-0.5)
LOG2_E = 1.4426950408889634
EXP_SCALE = SCORE_SCALE * LOG2_E
LOW = jnp.bfloat16
F32 = jnp.float32


def x_shift(value, step):
    pairs = []
    for x in range(4):
        to = (x + step) % 4
        pairs.append(((x % 2) * 2 + x // 2, (to % 2) * 2 + to // 2))
    return lax.ppermute(value, ("xl", "xh"), pairs)


def shift(value, axis, step):
    if axis == "x":
        return x_shift(value, step)
    return lax.ppermute(value, axis, [(i, (i + step) % 4) for i in range(4)])


def core_swap(value):
    return lax.ppermute(value, "co", [(0, 1), (1, 0)])


def place_on(axis):
    if axis == "x":
        return lax.axis_index("xh") * 2 + lax.axis_index("xl")
    return lax.axis_index(axis)


def pick(value, index, dim):
    return lax.dynamic_index_in_dim(value, index, dim, keepdims=False)


def reduce_over(value, axis, dim):
    me = place_on(axis)
    total = pick(value, me, dim).astype(F32)
    for step in (1, 3, 2):
        total = total + shift(pick(value, (me + step) % 4, dim), axis, step).astype(F32)
    return total.astype(LOW)


def gather_over(value, axis, dim, dtype=LOW):
    me = place_on(axis)
    shape = value.shape[:dim] + (4,) + value.shape[dim:]
    out = jnp.zeros(shape, dtype)
    out = lax.dynamic_update_index_in_dim(out, value.astype(dtype), me, dim)
    for step in (1, 3, 2):
        got = shift(value, axis, step).astype(dtype)
        out = lax.dynamic_update_index_in_dim(out, got, (me - step) % 4, dim)
    return out


def sum_everywhere(grads):
    cols = grads.shape[-1]
    half = cols // 2
    parts = grads.reshape(2, 4, 4, 16, cols)
    first, second = parts[..., :half], parts[..., half:]
    first = reduce_over(first, "y", 1)
    second = reduce_over(second, "z", 2)
    first = reduce_over(first, "z", 1)
    second = reduce_over(second, "y", 1)
    both = jnp.stack([first, second], axis=0)
    mine = reduce_over(both.reshape(4, 16, half), "x", 0)
    xh = lax.axis_index("xh")
    other = lax.ppermute(mine, "xh", [(0, 1), (1, 0)])
    first = jnp.where(xh == 0, mine, other)
    second = jnp.where(xh == 0, other, mine)
    first = gather_over(first, "z", 0)
    second = gather_over(second, "y", 0)
    first = gather_over(first, "y", 0, F32).reshape(256, half)
    second = gather_over(second, "z", 1, F32).reshape(256, half)
    return first, second


def gather_weight(shard):
    rows = shard.shape[0]
    half = rows // 2
    up = x_shift(shard[:half], 1)
    down = x_shift(shard[half:], -1)
    own_swapped = core_swap(shard)
    up_swapped = core_swap(up)
    down_swapped = core_swap(down)
    xl = lax.axis_index("xl")
    co = lax.axis_index("co")
    out = jnp.zeros((rows * 4, shard.shape[1]), shard.dtype)
    here = (xl * 2 + co) * rows
    there = ((1 - xl) * 2 + co) * rows
    here_other = (xl * 2 + 1 - co) * rows
    there_other = ((1 - xl) * 2 + 1 - co) * rows
    for piece, at in (
        (shard, here),
        (up, there),
        (down, there + half),
        (own_swapped, here_other),
        (up_swapped, there_other),
        (down_swapped, there_other + half),
    ):
        out = lax.dynamic_update_slice_in_dim(out, piece, at, 0)
    return out, (up, down)


def visible(first_key, query_block, start):
    key = first_key + lax.broadcasted_iota(jnp.int32, (CHUNK, 2 * ROWS), 0)
    query = query_block * ROWS + (lax.broadcasted_iota(jnp.int32, (CHUNK, 2 * ROWS), 1) & (ROWS - 1))
    return (key <= query) & ((key >= start) | (query < start))


def dot_t(left, right):
    return lax.dot_general(left, right, (((1,), (1,)), ((), ())), preferred_element_type=F32)


def dot_n(left, right):
    return lax.dot_general(left, right, (((1,), (0,)), ((), ())), preferred_element_type=F32)


def block_of(info):
    i = pl.program_id(0)
    return (i // 2) * 8 + info[1] * 2 + i % 2


def forward_kernel(info, q_ref, k_ref, vt_ref, o_ref, l_ref):
    block = block_of(info)
    start = info[0]
    q = q_ref[0]
    last = block // (CHUNK // ROWS)

    def step(c, carry, masked):
        total, mixed = carry
        keys = k_ref[pl.ds(pl.multiple_of(c * CHUNK, CHUNK), CHUNK), :]
        p = jnp.exp2(dot_t(keys, q) * EXP_SCALE)
        if masked:
            p = jnp.where(visible(c * CHUNK, block, start), p, 0.0)
        total = total + jnp.sum(p.reshape(CHUNK // 8, 8, 2 * ROWS), axis=0)
        mixed = mixed + dot_n(vt_ref[c], p.astype(LOW))
        return total, mixed

    carry = (jnp.zeros((8, 2 * ROWS), F32), jnp.zeros((HEAD, 2 * ROWS), F32))
    carry = step(last, carry, True)
    carry = lax.fori_loop(0, jnp.minimum(last, 1), lambda c, x: step(c, x, True), carry)
    carry = lax.fori_loop(1, last, lambda c, x: step(c, x, False), carry)
    total = jnp.sum(carry[0], axis=0, keepdims=True)
    o_ref[0] = carry[1] / total
    l_ref[0] = jnp.log2(total)


def backward_kernel(
    info, q_ref, do_ref, ot_ref, l_ref, k_ref, kt_ref, v_ref, dq_ref, dkv_ref, dk_acc, dv_acc
):
    i = pl.program_id(0)
    block = block_of(info)
    start = info[0]
    q = q_ref[0]
    do = do_ref[0]
    last = block // (CHUNK // ROWS)

    @pl.when(i == 0)
    def _():
        dk_acc[...] = jnp.zeros_like(dk_acc)
        dv_acc[...] = jnp.zeros_like(dv_acc)

    delta = jnp.sum(do.astype(F32).T * ot_ref[0], axis=0, keepdims=True)
    logs = l_ref[0]

    def step(c, dqt, masked):
        at = pl.ds(pl.multiple_of(c * CHUNK, CHUNK), CHUNK)
        p = jnp.exp2(dot_t(k_ref[at, :], q) * EXP_SCALE - logs)
        if masked:
            p = jnp.where(visible(c * CHUNK, block, start), p, 0.0)
        dp = dot_t(v_ref[at, :], do)
        ds = (p * (dp - delta)).astype(LOW)
        dv_acc[at, :] += dot_n(p.astype(LOW), do)
        dk_acc[at, :] += dot_n(ds, q)
        return dqt + dot_n(kt_ref[c], ds)

    dqt = step(last, jnp.zeros((HEAD, 2 * ROWS), F32), True)
    dqt = lax.fori_loop(0, jnp.minimum(last, 1), lambda c, x: step(c, x, True), dqt)
    dqt = lax.fori_loop(1, last, lambda c, x: step(c, x, False), dqt)
    dq_ref[0] = (dqt * SCORE_SCALE).T.astype(LOW)

    @pl.when(i == pl.num_programs(0) - 1)
    def _():
        dkv_ref[:, :HEAD] = (dk_acc[...] * SCORE_SCALE).astype(LOW)
        dkv_ref[:, HEAD:] = dv_acc[...].astype(LOW)


def whole(shape):
    return pl.BlockSpec(shape, lambda i: (0,) * len(shape))


def per_block(shape):
    return pl.BlockSpec((1,) + shape, lambda i: (i,) + (0,) * len(shape))


def smem():
    return pl.BlockSpec(memory_space=pltpu.SMEM)


def attention_forward(info, q, k, vt):
    length = k.shape[0]
    return pl.pallas_call(
        forward_kernel,
        grid=(8,),
        in_specs=[
            smem(),
            per_block((2 * ROWS, HEAD)),
            whole((length, HEAD)),
            whole((length // CHUNK, HEAD, CHUNK)),
        ],
        out_specs=[per_block((HEAD, 2 * ROWS)), per_block((1, 2 * ROWS))],
        out_shape=[
            jax.ShapeDtypeStruct((8, HEAD, 2 * ROWS), F32),
            jax.ShapeDtypeStruct((8, 1, 2 * ROWS), F32),
        ],
        compiler_params=pltpu.CompilerParams(vmem_limit_bytes=24 * 2**20),
        cost_estimate=pl.CostEstimate(
            flops=3 * 10**9, bytes_accessed=5 * 2**20, transcendentals=5 * 10**6
        ),
        name="attention_forward",
    )(info, q, k, vt)


def attention_backward(info, q, do, ot, logs, k, kt, v):
    length = k.shape[0]
    return pl.pallas_call(
        backward_kernel,
        grid=(8,),
        in_specs=[
            smem(),
            per_block((2 * ROWS, HEAD)),
            per_block((2 * ROWS, HEAD)),
            per_block((HEAD, 2 * ROWS)),
            per_block((1, 2 * ROWS)),
            whole((length, HEAD)),
            whole((length // CHUNK, HEAD, CHUNK)),
            whole((length, HEAD)),
        ],
        out_specs=[per_block((2 * ROWS, HEAD)), whole((length, 2 * HEAD))],
        out_shape=[
            jax.ShapeDtypeStruct((8, 2 * ROWS, HEAD), LOW),
            jax.ShapeDtypeStruct((length, 2 * HEAD), LOW),
        ],
        scratch_shapes=[pltpu.VMEM((length, HEAD), F32), pltpu.VMEM((length, HEAD), F32)],
        compiler_params=pltpu.CompilerParams(vmem_limit_bytes=32 * 2**20),
        cost_estimate=pl.CostEstimate(
            flops=8 * 10**9, bytes_accessed=10 * 2**20, transcendentals=5 * 10**6
        ),
        name="attention_backward",
    )(info, q, do, ot, logs, k, kt, v)


def rms_scale(values_in):
    return lax.rsqrt(jnp.mean(values_in * values_in, axis=-1, keepdims=True) + EPSILON)


def rotary_tables(where_at):
    half = HEAD // 2
    frequency = THETA ** (-(jnp.arange(half, dtype=F32) * 2.0) / HEAD)
    angles = where_at.astype(F32)[:, None] * frequency[None, :]
    cosine, sine = jnp.cos(angles), jnp.sin(angles)
    cosine = jnp.concatenate([cosine, cosine], axis=-1)[:, None, :]
    sine = jnp.concatenate([sine, sine], axis=-1)[:, None, :]
    return cosine, sine


def rotate_forward(u, cosine, sine):
    half = HEAD // 2
    turned = jnp.concatenate([-u[..., half:], u[..., :half]], axis=-1)
    return u * cosine + turned * sine


def rotate_back(w, cosine, sine):
    half = HEAD // 2
    shifted = w * sine
    turned = jnp.concatenate([shifted[..., half:], -shifted[..., :half]], axis=-1)
    return w * cosine + turned


def norm_back(grad, unit, scale):
    return scale * (grad - unit * jnp.mean(grad * unit, axis=-1, keepdims=True))


def over_rows(left, right):
    return lax.dot_general(left, right, (((0,), (0,)), ((), ())), preferred_element_type=F32)


def dot(left, right):
    return jnp.dot(left, right, preferred_element_type=F32)


def exchange_heads(value):
    return lax.all_to_all(value, ("z", "xh"), split_axis=0, concat_axis=0, tiled=True)


def exchange_y(value):
    return lax.all_to_all(value, "y", split_axis=0, concat_axis=0, tiled=True)


def column_groups(value, co):
    rows, cols = value.shape
    split = value.reshape(rows, 2, 2, cols // 4)
    mine = pick(split, co, 2)
    other = pick(split, 1 - co, 2)
    return mine.reshape(rows, cols // 2), other.reshape(rows, cols // 2)


def both_cores(value):
    return jnp.concatenate([value, core_swap(value)], axis=0)


def both_cores_columns(value, co):
    mine, other = column_groups(value, co)
    return jnp.concatenate([mine, core_swap(other)], axis=0)


def local(
    tokens,
    positions,
    attn_gain,
    w_query,
    w_key,
    w_value,
    query_gain,
    key_gain,
    w_out,
    ffn_gain,
    w_gate,
    w_up,
    w_down,
    cotangent,
):
    xl = lax.axis_index("xl")
    co = lax.axis_index("co")
    y = lax.axis_index("y")
    block = lax.axis_index("z") * 8 + y * 2 + lax.axis_index("xh")

    gains = jnp.concatenate([attn_gain, ffn_gain, query_gain, key_gain])
    gains = jnp.concatenate([gains, jnp.zeros((1024 - 576,), LOW)]).reshape(1, 8, 128)
    pair = jnp.concatenate([gains, x_pair(gains)], axis=0)
    pair = jnp.where(xl == 0, pair, pair[::-1])
    swapped = core_swap(pair)
    quad = jnp.where(co == 0, jnp.stack([pair, swapped], 1), jnp.stack([swapped, pair], 1))
    quad = quad.reshape(4, 1024).astype(F32)
    gain_one = quad[:, :256].reshape(1024)
    gain_two = quad[:, 256:512].reshape(1024)
    gain_query = quad[:, 512:544].reshape(128)
    gain_key = quad[:, 544:576].reshape(128)

    qkv_full, arrived = gather_weight(jnp.concatenate([w_query, w_key, w_value], axis=1))
    w_out, w_down, w_gate, w_up, _, _ = lax.optimization_barrier(
        (w_out, w_down, w_gate, w_up) + arrived
    )
    out_full, _ = gather_weight(w_out)
    gate_up_full, _ = gather_weight(jnp.concatenate([w_gate, w_up], axis=1))
    down_full, _ = gather_weight(w_down)

    start = block * ROWS + ROWS - 1 - positions[ROWS - 1]
    info = jnp.stack([start, y]).astype(jnp.int32)
    cosine, sine = rotary_tables(positions)
    inputs = tokens.astype(F32)
    scale_one = rms_scale(inputs)
    normal_one = inputs * scale_one
    normed_one = (normal_one * gain_one).astype(LOW)
    qkv = dot(normed_one, qkv_full)
    query_raw = qkv[:, :2048].reshape(ROWS, 16, HEAD)
    key_raw = qkv[:, 2048:3072].reshape(ROWS, 8, HEAD)
    value = qkv[:, 3072:].astype(LOW).reshape(ROWS, 8, HEAD)
    scale_q = rms_scale(query_raw)
    unit_q = query_raw * scale_q
    query = rotate_forward(unit_q * gain_query, cosine, sine).astype(LOW)
    scale_k = rms_scale(key_raw)
    unit_k = key_raw * scale_k
    key = rotate_forward(unit_k * gain_key, cosine, sine).astype(LOW)

    kv_send = jnp.transpose(jnp.concatenate([key, value], axis=-1), (1, 0, 2))
    kv = exchange_heads(kv_send)
    kv = exchange_y(jnp.broadcast_to(kv[None], (4,) + kv.shape))
    kv = jnp.transpose(kv.reshape(4, 4, 2, ROWS, 2 * HEAD), (1, 0, 2, 3, 4)).reshape(-1, 2 * HEAD)
    k_all, v_all = kv[:, :HEAD], kv[:, HEAD:]
    chunks = k_all.shape[0] // CHUNK
    kt_all = jnp.transpose(k_all.reshape(chunks, CHUNK, HEAD), (0, 2, 1))
    vt_all = jnp.transpose(v_all.reshape(chunks, CHUNK, HEAD), (0, 2, 1))
    q_send = jnp.transpose(query.reshape(ROWS, 8, 2, HEAD), (1, 2, 0, 3)).reshape(8, 2 * ROWS, HEAD)
    q_all = exchange_heads(q_send)
    mixed_t, logs = attention_forward(info, q_all, k_all, vt_all)

    o_send = jnp.transpose(mixed_t, (0, 2, 1)).astype(LOW)
    merged = exchange_heads(o_send).reshape(8, 2, ROWS, HEAD)
    merged = jnp.transpose(merged, (2, 0, 1, 3)).reshape(ROWS, 2048)

    middle = inputs + dot(merged, out_full)
    scale_two = rms_scale(middle)
    normal_two = middle * scale_two
    normed_two = (normal_two * gain_two).astype(LOW)
    gate_up = dot(normed_two, gate_up_full)
    gate_value, up_value = gate_up[:, :3072], gate_up[:, 3072:]
    gate_sigmoid = jax.nn.sigmoid(gate_value)
    swish = gate_value * gate_sigmoid
    hidden = (swish * up_value).astype(LOW)
    output = (middle + dot(hidden, down_full)).astype(LOW)
    grad_hidden = dot_t(cotangent, down_full)
    grad_gate = (
        grad_hidden * up_value * gate_sigmoid * (1.0 + gate_value * (1.0 - gate_sigmoid))
    ).astype(LOW)
    grad_up = (grad_hidden * swish).astype(LOW)
    feed_grads = jnp.concatenate([grad_gate, grad_up], axis=1)
    grad_normed_two = dot_t(feed_grads, gate_up_full)
    gain_two_term = jnp.sum(grad_normed_two * normal_two, axis=0)
    grad_middle = cotangent.astype(F32) + norm_back(
        grad_normed_two * gain_two, normal_two, scale_two
    )
    grad_branch = grad_middle.astype(LOW)
    grad_merged = dot_t(grad_branch, out_full).astype(LOW)

    left_two = both_cores_columns(normed_two, co)
    left_hidden = both_cores_columns(hidden, co).reshape(2 * ROWS, 2, 3, 256)
    left_merged = both_cores_columns(merged, co).reshape(2 * ROWS, 2, 2, 256)
    right_feed = both_cores(feed_grads)
    right_cot = both_cores(cotangent)
    right_branch = both_cores(grad_branch)
    pieces = [over_rows(left_two, right_feed).astype(LOW)]
    for g in range(3):
        pieces.append(over_rows(left_hidden[:, :, g].reshape(2 * ROWS, 512), right_cot).astype(LOW))
    for g in range(2):
        pieces.append(
            over_rows(left_merged[:, :, g].reshape(2 * ROWS, 512), right_branch).astype(LOW)
        )
    feed_first, feed_second = sum_everywhere(jnp.concatenate(pieces, axis=1))

    do_send = jnp.transpose(grad_merged.reshape(ROWS, 8, 2, HEAD), (1, 2, 0, 3))
    do_all = exchange_heads(do_send.reshape(8, 2 * ROWS, HEAD))
    dq_all, dkv_all = attention_backward(
        info, q_all, do_all, mixed_t, logs, k_all, kt_all, v_all
    )
    dkv = jnp.transpose(dkv_all.reshape(4, 4, 2, ROWS, 2 * HEAD), (1, 0, 2, 3, 4))
    dkv = exchange_y(dkv.reshape(4, 8, ROWS, 2 * HEAD))
    dkv = jnp.sum(dkv.astype(F32), axis=0).astype(LOW)
    dq_send = jnp.transpose(dq_all.reshape(8, 2, ROWS, HEAD), (0, 2, 1, 3))
    back = exchange_heads(
        jnp.concatenate([dq_send.reshape(8, ROWS, 2 * HEAD), dkv], axis=-1)
    )
    back = jnp.transpose(back, (1, 0, 2))
    grad_q = back[:, :, : 2 * HEAD].reshape(ROWS, 16, HEAD).astype(F32)
    grad_k = back[:, :, 2 * HEAD : 3 * HEAD].astype(F32)
    grad_value = back[:, :, 3 * HEAD :].reshape(ROWS, 1024)

    grad_scaled_q = rotate_back(grad_q, cosine, sine)
    query_gain_term = jnp.sum(grad_scaled_q * unit_q, axis=(0, 1))
    grad_query = norm_back(grad_scaled_q * gain_query, unit_q, scale_q).reshape(ROWS, 2048)
    grad_scaled_k = rotate_back(grad_k, cosine, sine)
    key_gain_term = jnp.sum(grad_scaled_k * unit_k, axis=(0, 1))
    grad_key = norm_back(grad_scaled_k * gain_key, unit_k, scale_k).reshape(ROWS, 1024)
    attention_grads = jnp.concatenate(
        [grad_query.astype(LOW), grad_key.astype(LOW), grad_value], axis=1
    )
    grad_normed_one = dot_t(attention_grads, qkv_full)
    gain_one_term = jnp.sum(grad_normed_one * normal_one, axis=0)
    grad_tokens = grad_middle + norm_back(grad_normed_one * gain_one, normal_one, scale_one)

    gain_terms = jnp.concatenate([gain_one_term, gain_two_term, query_gain_term, key_gain_term])
    gain_terms = gain_terms.reshape(18, 128)
    gain_terms = gain_terms + core_swap(gain_terms)
    gain_terms = jnp.pad(gain_terms, ((0, 238), (0, 128))).astype(LOW)
    gain_terms = jnp.concatenate([gain_terms, gain_terms], axis=0)
    left_one = both_cores_columns(normed_one, co)
    right_attention = both_cores(attention_grads)
    attention_part = jnp.concatenate(
        [over_rows(left_one, right_attention).astype(LOW), gain_terms], axis=1
    )
    qkv_first, qkv_second = sum_everywhere(attention_part)

    feed = jnp.concatenate([feed_first, feed_second], axis=1)
    grad_down = jnp.concatenate([feed[:, 6144 + 1024 * g : 7168 + 1024 * g] for g in range(3)], axis=0)
    grad_out = jnp.concatenate([feed[:, 9216 + 1024 * g : 10240 + 1024 * g] for g in range(2)], axis=0)
    wide = jnp.concatenate([qkv_first, qkv_second], axis=1)
    shard = xl * 2 + co
    gain_all = wide[:18, 4096:4224].reshape(2304)
    return (
        output,
        grad_tokens,
        lax.dynamic_slice_in_dim(gain_all, shard * 256, 256),
        wide[:, :2048],
        wide[:, 2048:3072],
        wide[:, 3072:4096],
        lax.dynamic_slice_in_dim(gain_all, 2048 + shard * 32, 32),
        lax.dynamic_slice_in_dim(gain_all, 2176 + shard * 32, 32),
        grad_out,
        lax.dynamic_slice_in_dim(gain_all, 1024 + shard * 256, 256),
        feed[:, :3072],
        feed[:, 3072:6144],
        grad_down,
    )


def x_pair(value):
    return lax.ppermute(value, "xl", [(0, 1), (1, 0)])


def solution(mesh):
    axes = ("xl", "co", "z", "y", "xh")
    fine = Mesh(mesh.devices.reshape(2, 2, 4, 4, 2), axes)
    rows = P(axes, None)
    shard = P(("xl", "co"), None)
    vector = P(("xl", "co"))
    in_specs = (
        rows,
        P(axes),
        vector,
        shard,
        shard,
        shard,
        vector,
        vector,
        shard,
        vector,
        shard,
        shard,
        shard,
        rows,
    )
    out_specs = (
        rows,
        rows,
        vector,
        shard,
        shard,
        shard,
        vector,
        vector,
        shard,
        vector,
        shard,
        shard,
        shard,
    )
    return jax.shard_map(local, mesh=fine, in_specs=in_specs, out_specs=out_specs, check_vma=False)
```

```python
import jax
import jax.numpy as jnp
from jax import lax
from jax.experimental import pallas as pl
from jax.experimental.pallas import tpu as pltpu
from jax.sharding import Mesh
from jax.sharding import PartitionSpec as P

EPSILON = 1e-06
THETA = 1000000.0
HEAD = 128
ROWS = 128
CHUNK = 512
SCORE_SCALE = HEAD ** (-0.5)
LOG2_E = 1.4426950408889634
EXP_SCALE = SCORE_SCALE * LOG2_E
LOW = jnp.bfloat16
FEED_CUTS = ((0, 256), (1408, 1664), (256, 1408), (1664, 2816))
F32 = jnp.float32


def x_shift(value, step):
    pairs = []
    for x in range(4):
        to = (x + step) % 4
        pairs.append(((x % 2) * 2 + x // 2, (to % 2) * 2 + to // 2))
    return lax.ppermute(value, ("xl", "xh"), pairs)


def shift(value, axis, step):
    if axis == "x":
        return x_shift(value, step)
    return lax.ppermute(value, axis, [(i, (i + step) % 4) for i in range(4)])


def core_swap(value):
    return lax.ppermute(value, "co", [(0, 1), (1, 0)])


def place_on(axis):
    if axis == "x":
        return lax.axis_index("xh") * 2 + lax.axis_index("xl")
    return lax.axis_index(axis)


def pick(value, index, dim):
    return lax.dynamic_index_in_dim(value, index, dim, keepdims=False)


def send_parts(value, axis, dim):
    me = place_on(axis)
    got = [shift(pick(value, (me + step) % 4, dim), axis, step) for step in (1, 3, 2)]
    return [pick(value, me, dim)] + got


def add_parts(parts):
    total = parts[0].astype(F32)
    for part in parts[1:]:
        total = total + part.astype(F32)
    return total.astype(LOW)


def reduce_over(value, axis, dim):
    return add_parts(send_parts(value, axis, dim))


def gather_over(value, axis, dim, dtype=LOW):
    me = place_on(axis)
    shape = value.shape[:dim] + (4,) + value.shape[dim:]
    out = jnp.zeros(shape, dtype)
    out = lax.dynamic_update_index_in_dim(out, value.astype(dtype), me, dim)
    for step in (1, 3, 2):
        got = shift(value, axis, step).astype(dtype)
        out = lax.dynamic_update_index_in_dim(out, got, (me - step) % 4, dim)
    return out


def reduce_zy(grads):
    return lax.psum_scatter(grads, ("z", "y"), scatter_dimension=0, tiled=True)


def exchange_zy(grads):
    parts = grads.reshape(16, 32, grads.shape[-1])
    parts = lax.all_to_all(parts, ("z", "y"), split_axis=0, concat_axis=0, tiled=True)
    return jnp.sum(parts.astype(F32), axis=0).astype(LOW)


def reduce_x_gather(part):
    half = part.shape[-1] // 2
    both = jnp.stack([part[:, :half], part[:, half:]], axis=0)
    mine = reduce_over(both.reshape(4, 16, half), "x", 0)
    xh = lax.axis_index("xh")
    other = lax.ppermute(mine, "xh", [(0, 1), (1, 0)])
    first = jnp.where(xh == 0, mine, other)
    second = jnp.where(xh == 0, other, mine)
    first = gather_over(first, "z", 0)
    second = gather_over(second, "y", 0)
    first = gather_over(first, "y", 0, F32).reshape(256, half)
    second = gather_over(second, "z", 1, F32).reshape(256, half)
    return jnp.concatenate([first, second], axis=1)


def gather_weight(shard):
    half = shard.shape[0] // 2
    up = x_shift(shard[:half], 1)
    down = x_shift(shard[half:], -1)
    return [shard, up, down, core_swap(shard), core_swap(up), core_swap(down)]


def dot_t(left, right):
    return lax.dot_general(left, right, (((1,), (1,)), ((), ())), preferred_element_type=F32)


def dot_n(left, right):
    return lax.dot_general(left, right, (((1,), (0,)), ((), ())), preferred_element_type=F32)


def dot_r(left, right):
    return lax.dot_general(left, right, (((0,), (0,)), ((), ())), preferred_element_type=F32)


def whole(shape):
    return pl.BlockSpec(shape, lambda *_: (0,) * len(shape))


def per_block(shape):
    return pl.BlockSpec((1,) + shape, lambda i: (i,) + (0,) * len(shape))


def smem():
    return pl.BlockSpec(memory_space=pltpu.SMEM)


def anywhere():
    return pl.BlockSpec(memory_space=pl.ANY)


def shaped(shape, dtype):
    return jax.ShapeDtypeStruct(shape, dtype)


def fetch(shards, pieces, full, sems):
    rows = pieces[0].shape[0]
    half = rows // 2
    at = [
        shards[0] * rows,
        shards[1] * rows,
        shards[1] * rows + half,
        shards[2] * rows,
        shards[3] * rows,
        shards[3] * rows + half,
    ]
    copies = []
    for n, (piece, where) in enumerate(zip(pieces, at)):
        where = pl.multiple_of(where, half)
        copy = pltpu.make_async_copy(
            piece, full.at[pl.ds(where, piece.shape[0]), :], sems.at[n]
        )
        copy.start()
        copies.append(copy)
    return copies


def fetch_feed(shards, pieces, w_out, w_gu, w_down, sems):
    groups = ([], [], [])
    n = 0
    for s in range(4):
        for part, (first, end) in enumerate(FEED_CUTS):
            piece = pieces[len(FEED_CUTS) * s + part]
            at = 0
            while first + at < end:
                block, off = divmod(first + at, 256)
                size = min(256 - off, end - first - at)
                src = piece.at[pl.ds(at, size), :]
                if block < 6:
                    where = pl.multiple_of(shards[s] * 256 + off, 128)
                    dst = w_gu.at[pl.ds(where, size), pl.ds(block * 1024, 1024)]
                    group = 1
                elif block < 8:
                    where = pl.multiple_of(shards[s] * 512 + (block - 6) * 256 + off, 128)
                    dst = w_out.at[pl.ds(where, size), :]
                    group = 0
                else:
                    where = pl.multiple_of(shards[s] * 768 + (block - 8) * 256 + off, 128)
                    dst = w_down.at[pl.ds(where, size), :]
                    group = 2
                groups[group].append(pltpu.make_async_copy(src, dst, sems.at[n]))
                n += 1
                at += size
    for group in groups:
        for copy in group:
            copy.start()
    return groups


def settle(copies):
    for copy in copies:
        copy.wait()


def scale_of(value):
    return lax.rsqrt(jnp.mean(value * value, axis=-1, keepdims=True) + EPSILON)


def turn(value):
    return jnp.concatenate([value[:, HEAD // 2 :], value[:, : HEAD // 2]], axis=1)


def project_kernel(
    shards, x_ref, gain_ref, gq_ref, gk_ref, cos_ref, sin_ref, *rest
):
    pieces, (q_ref, kv_ref, raw_ref, left_ref, w, sems) = rest[:6], rest[6:]
    copies = fetch(shards, pieces, w, sems)
    x = x_ref[...].astype(F32)
    h = (x * scale_of(x) * gain_ref[...]).astype(LOW)
    for f in range(4):
        left_ref[f % 2, :, (f // 2) * 256 : (f // 2) * 256 + 256] = h[:, f * 256 : f * 256 + 256]
    cosine, sine = cos_ref[...], sin_ref[...]
    settle(copies)
    for tile in range(8):
        product = dot_n(h, w[:, tile * 512 : tile * 512 + 512])
        for part in range(4):
            n = tile * 4 + part
            raw = product[:, part * HEAD : part * HEAD + HEAD]
            if n >= 24:
                kv_ref[n - 24, 1] = raw.astype(LOW)
                continue
            raw_ref[n] = raw
            gain = gq_ref[...] if n < 16 else gk_ref[...]
            u = raw * scale_of(raw) * gain
            u = (u * cosine + turn(u) * sine).astype(LOW)
            if n < 16:
                q_ref[n] = u
            else:
                kv_ref[n - 16, 0] = u


def project(shards, x, gain, gain_q, gain_k, cosine, sine, pieces):
    return pl.pallas_call(
        project_kernel,
        in_specs=[smem()] + [pl.BlockSpec(memory_space=pltpu.VMEM)] * 6 + [anywhere()] * 6,
        out_shape=[
            shaped((16, ROWS, HEAD), LOW),
            shaped((8, 2, ROWS, HEAD), LOW),
            shaped((24, ROWS, HEAD), F32),
            shaped((2, ROWS, 512), LOW),
        ],
        scratch_shapes=[pltpu.VMEM((1024, 4096), LOW), pltpu.SemaphoreType.DMA((6,))],
        compiler_params=pltpu.CompilerParams(vmem_limit_bytes=32 * 2**20),
        cost_estimate=pl.CostEstimate(
            flops=10**9, bytes_accessed=12 * 2**20, transcendentals=10**4
        ),
        name="project",
    )(shards, x, gain, gain_q, gain_k, cosine, sine, *pieces)


def feed_kernel(shards, o_ref, x_ref, cot_ref, gain_ref, *rest):
    (y_ref, mid_ref, left_ref, right_ref, do_ref, term_ref) = rest[16:22]
    (w_out, w_gu, w_down, merged, sems) = rest[22:]
    out_copies, gu_copies, down_copies = fetch_feed(shards, rest[:16], w_out, w_gu, w_down, sems)
    for n in range(16):
        merged[:, n * HEAD : n * HEAD + HEAD] = o_ref[n]
    for f in range(4):
        for g in range(2):
            at = f * 512 + g * 256
            left_ref[f % 2, 4 + g, :, (f // 2) * 256 : (f // 2) * 256 + 256] = merged[:, at : at + 256]
    cot = cot_ref[...]
    gain = gain_ref[...]
    settle(out_copies)
    middle = x_ref[...].astype(F32) + dot_n(merged[...], w_out[...])
    scale = scale_of(middle)
    normal = middle * scale
    h = (normal * gain).astype(LOW)
    for f in range(4):
        left_ref[f % 2, 0, :, (f // 2) * 256 : (f // 2) * 256 + 256] = h[:, f * 256 : f * 256 + 256]
    settle(gu_copies)
    settle(down_copies)
    total = middle
    dh = jnp.zeros_like(middle)
    for tile in range(6):
        at = tile * 512
        gate = dot_n(h, w_gu[:, at : at + 512])
        up = dot_n(h, w_gu[:, 3072 + at : 3072 + at + 512])
        sg = 1.0 / (1.0 + jnp.exp(-gate))
        swish = gate * sg
        hidden = (swish * up).astype(LOW)
        for part in range(2):
            f, g = divmod(tile * 2 + part, 3)
            left_ref[f % 2, 1 + g, :, (f // 2) * 256 : (f // 2) * 256 + 256] = hidden[
                :, part * 256 : part * 256 + 256
            ]
        total = total + dot_n(hidden, w_down[at : at + 512, :])
        dhidden = dot_t(cot, w_down[at : at + 512, :])
        dgate = (dhidden * up * sg * (1.0 + gate * (1.0 - sg))).astype(LOW)
        dup = (dhidden * swish).astype(LOW)
        right_ref[:, at : at + 512] = dgate
        right_ref[:, 3072 + at : 3072 + at + 512] = dup
        dh = dh + dot_t(dgate, w_gu[:, at : at + 512])
        dh = dh + dot_t(dup, w_gu[:, 3072 + at : 3072 + at + 512])
    y_ref[...] = total.astype(LOW)
    term_ref[...] = jnp.sum(dh * normal, axis=0, keepdims=True)
    dn = dh * gain
    dmid = cot.astype(F32) + scale * (dn - normal * jnp.mean(dn * normal, axis=-1, keepdims=True))
    mid_ref[...] = dmid
    da = dmid.astype(LOW)
    right_ref[:, 6144:7168] = cot
    right_ref[:, 7168:8192] = da
    for tile in range(4):
        back = dot_t(da, w_out[tile * 512 : tile * 512 + 512, :]).astype(LOW)
        for part in range(4):
            do_ref[tile * 4 + part] = back[:, part * HEAD : part * HEAD + HEAD]


def feed(shards, o, x, cot, gain, pieces):
    return pl.pallas_call(
        feed_kernel,
        in_specs=[smem()] + [pl.BlockSpec(memory_space=pltpu.VMEM)] * 4 + [anywhere()] * 16,
        out_shape=[
            shaped((ROWS, 1024), LOW),
            shaped((ROWS, 1024), F32),
            shaped((2, 6, ROWS, 512), LOW),
            shaped((ROWS, 8192), LOW),
            shaped((16, ROWS, HEAD), LOW),
            shaped((1, 1024), F32),
        ],
        scratch_shapes=[
            pltpu.VMEM((2048, 1024), LOW),
            pltpu.VMEM((1024, 6144), LOW),
            pltpu.VMEM((3072, 1024), LOW),
            pltpu.VMEM((ROWS, 2048), LOW),
            pltpu.SemaphoreType.DMA((52,)),
        ],
        compiler_params=pltpu.CompilerParams(vmem_limit_bytes=48 * 2**20),
        cost_estimate=pl.CostEstimate(
            flops=7 * 10**9, bytes_accessed=30 * 2**20, transcendentals=10**6
        ),
        name="feed",
    )(shards, o, x, cot, gain, *pieces)


def lay_left(left_t, half, left):
    columns = left.astype(F32).T.astype(LOW)
    for xl in range(2):
        for y in range(4):
            for z in range(4):
                to, at = ((z * 4 + y) * 2 + xl) * 16, ((xl * 4 + y) * 4 + z) * 16
                left_t[to : to + 16, half * ROWS : half * ROWS + ROWS] = columns[at : at + 16, :]


def weight_kernel(mine_ref, other_ref, right_ref, other_right_ref, out_ref, left_t, right):
    t = pl.program_id(0)

    @pl.when((t == 0) | (t >= 6))
    def _():
        lay_left(left_t, 0, mine_ref[0])
        lay_left(left_t, 1, other_ref[0])

    right[:ROWS, :] = right_ref[...]
    right[ROWS:, :] = other_right_ref[...]
    out_ref[...] = dot_n(left_t[...], right[...]).astype(LOW)


def feed_weight_grads(mine, other, right, other_right):
    def group(t):
        return jnp.maximum(t - 5, 0)

    def column(t):
        return jnp.where(t < 6, t, jnp.where(t < 9, 6, 7))

    left = pl.BlockSpec((1, ROWS, 512), lambda t: (group(t), 0, 0))
    wide = pl.BlockSpec((ROWS, 1024), lambda t: (0, column(t)))
    return pl.pallas_call(
        weight_kernel,
        grid=(11,),
        in_specs=[left, left, wide, wide],
        out_specs=pl.BlockSpec((512, 1024), lambda t: (0, t)),
        out_shape=shaped((512, 11264), LOW),
        scratch_shapes=[pltpu.VMEM((512, 2 * ROWS), LOW), pltpu.VMEM((2 * ROWS, 1024), LOW)],
        compiler_params=pltpu.CompilerParams(vmem_limit_bytes=16 * 2**20),
        cost_estimate=pl.CostEstimate(
            flops=3 * 10**9, bytes_accessed=16 * 2**20, transcendentals=0
        ),
        name="feed_weight_grads",
    )(mine, other, right, other_right)


def attention_weight_kernel(
    mine_ref, other_ref, right_ref, other_right_ref, term_ref, out_ref, left_t, right
):
    t = pl.program_id(0)

    @pl.when(t == 0)
    def _():
        lay_left(left_t, 0, mine_ref[...])
        lay_left(left_t, 1, other_ref[...])

    @pl.when(t < 16)
    def _():
        right[:ROWS, :] = right_ref[...]
        right[ROWS:, :] = other_right_ref[...]
        out_ref[...] = dot_n(left_t[...], right[...]).astype(LOW)

    @pl.when(t == 16)
    def _():
        out_ref[...] = jnp.zeros_like(out_ref)
        for xl in range(2):
            for z in range(2):
                at = (z * 8 + xl) * 16
                out_ref[at : at + 16, :HEAD] = term_ref[z * 16 : z * 16 + 16, :].astype(LOW)


def attention_weight_grads(mine, other, right, other_right, terms):
    wide = pl.BlockSpec((ROWS, 256), lambda t: (0, jnp.minimum(t, 15)))
    left = whole((ROWS, 512))
    return pl.pallas_call(
        attention_weight_kernel,
        grid=(17,),
        in_specs=[left, left, wide, wide, whole((32, HEAD))],
        out_specs=pl.BlockSpec((512, 256), lambda t: (0, t)),
        out_shape=shaped((512, 4352), LOW),
        scratch_shapes=[pltpu.VMEM((512, 2 * ROWS), LOW), pltpu.VMEM((2 * ROWS, 256), LOW)],
        compiler_params=pltpu.CompilerParams(vmem_limit_bytes=16 * 2**20),
        cost_estimate=pl.CostEstimate(flops=10**9, bytes_accessed=6 * 2**20, transcendentals=0),
        name="attention_weight_grads",
    )(mine, other, right, other_right, terms)


def tail_kernel(
    shards, back_ref, raw_ref, x_ref, mid_ref, gain_ref, gq_ref, gk_ref, cos_ref, sin_ref, *rest
):
    pieces, (grad_ref, right_ref, term_ref, w, sems) = rest[:6], rest[6:]
    copies = fetch(shards, pieces, w, sems)
    cosine, sine = cos_ref[...], sin_ref[...]
    term_ref[...] = jnp.zeros_like(term_ref)
    for heads, first, place, gain_ref_ in ((16, 0, 1024, gq_ref), (8, 16, 1152, gk_ref)):
        gain = gain_ref_[...]
        term = jnp.zeros((ROWS, HEAD), F32)
        for n in range(heads):
            grad = back_ref[n // 2, n % 2] if first == 0 else back_ref[n, 2]
            grad = grad.astype(F32)
            raw = raw_ref[first + n]
            scale = scale_of(raw)
            unit = raw * scale
            grad = grad * cosine - turn(grad) * sine
            term = term + grad * unit
            grad = grad * gain
            grad = scale * (grad - unit * jnp.mean(grad * unit, axis=-1, keepdims=True))
            at = (first + n) * HEAD
            right_ref[:, at : at + HEAD] = grad.astype(LOW)
        term_ref[:, place : place + HEAD] = jnp.sum(term, axis=0, keepdims=True)
    for n in range(8):
        at = 3072 + n * HEAD
        right_ref[:, at : at + HEAD] = back_ref[n, 3]
    x = x_ref[...].astype(F32)
    scale = scale_of(x)
    normal = x * scale
    settle(copies)
    dh = dot_t(right_ref[...], w[...])
    term_ref[:, :1024] = jnp.sum(dh * normal, axis=0, keepdims=True)
    dn = dh * gain_ref[...]
    grad_ref[...] = mid_ref[...] + scale * (
        dn - normal * jnp.mean(dn * normal, axis=-1, keepdims=True)
    )


def tail(shards, back, raw, x, mid, gain, gain_q, gain_k, cosine, sine, pieces):
    return pl.pallas_call(
        tail_kernel,
        in_specs=[smem()] + [pl.BlockSpec(memory_space=pltpu.VMEM)] * 9 + [anywhere()] * 6,
        out_shape=[
            shaped((ROWS, 1024), F32),
            shaped((ROWS, 4096), LOW),
            shaped((1, 1280), F32),
        ],
        scratch_shapes=[pltpu.VMEM((1024, 4096), LOW), pltpu.SemaphoreType.DMA((6,))],
        compiler_params=pltpu.CompilerParams(vmem_limit_bytes=32 * 2**20),
        cost_estimate=pl.CostEstimate(
            flops=10**9, bytes_accessed=12 * 2**20, transcendentals=10**4
        ),
        name="tail",
    )(shards, back, raw, x, mid, gain, gain_q, gain_k, cosine, sine, *pieces)


def visible(first_key, query_block, start):
    key = first_key + lax.broadcasted_iota(jnp.int32, (CHUNK, 2 * ROWS), 0)
    query = query_block * ROWS + (lax.broadcasted_iota(jnp.int32, (CHUNK, 2 * ROWS), 1) & (ROWS - 1))
    return (key <= query) & ((key >= start) | (query < start))


def block_of(info):
    i = pl.program_id(0)
    return (i // 2) * 8 + info[1] * 2 + i % 2


def columns_of(value):
    return value.astype(F32).T.astype(LOW)


def forward_kernel(info, q_ref, kv0, kv1, kv2, kv3, o_ref, ot_ref, l_ref, k_ref, v_ref, vt):
    block = block_of(info)
    start = info[0]
    last = block // (CHUNK // ROWS)

    @pl.when(pl.program_id(0) == 0)
    def _():
        for back, piece in enumerate((kv0, kv1, kv2, kv3)):
            owner = lax.rem(info[1] + 4 - back, 4)
            for z in range(4):
                at = pl.ds(pl.multiple_of((z * 4 + owner) * 256, 256), 256)
                k_ref[at, :] = piece[2 * z : 2 * z + 2, 0].reshape(256, HEAD)
                v_ref[at, :] = piece[2 * z : 2 * z + 2, 1].reshape(256, HEAD)
        for c in range(vt.shape[0]):
            vt[c] = columns_of(v_ref[c * CHUNK : (c + 1) * CHUNK, :])

    q = q_ref[0]

    def step(c, carry, masked):
        total, mixed = carry
        keys = k_ref[pl.ds(pl.multiple_of(c * CHUNK, CHUNK), CHUNK), :]
        p = jnp.exp2(dot_t(keys, q) * EXP_SCALE)
        if masked:
            p = jnp.where(visible(c * CHUNK, block, start), p, 0.0)
        total = total + jnp.sum(p.reshape(CHUNK // 8, 8, 2 * ROWS), axis=0)
        mixed = mixed + dot_n(vt[c], p.astype(LOW))
        return total, mixed

    carry = (jnp.zeros((8, 2 * ROWS), F32), jnp.zeros((HEAD, 2 * ROWS), F32))
    carry = step(last, carry, True)
    carry = lax.fori_loop(0, jnp.minimum(last, 1), lambda c, x: step(c, x, True), carry)
    carry = lax.fori_loop(1, last, lambda c, x: step(c, x, False), carry)
    total = jnp.sum(carry[0], axis=0, keepdims=True)
    mixed = carry[1] / total
    ot_ref[0] = mixed
    o_ref[0] = mixed.T.astype(LOW)
    l_ref[0] = jnp.log2(total)


def backward_kernel(
    info, q_ref, do_ref, ot_ref, l_ref, k_ref, v_ref, dq_ref, dkv_ref, kt, dk_acc, dv_acc
):
    i = pl.program_id(0)
    block = block_of(info)
    start = info[0]
    q = q_ref[0]
    do = do_ref[0]
    last = block // (CHUNK // ROWS)

    @pl.when(i == 0)
    def _():
        dk_acc[...] = jnp.zeros_like(dk_acc)
        dv_acc[...] = jnp.zeros_like(dv_acc)
        for c in range(kt.shape[0]):
            kt[c] = columns_of(k_ref[c * CHUNK : (c + 1) * CHUNK, :])

    delta = jnp.sum(do.astype(F32).T * ot_ref[0], axis=0, keepdims=True)
    logs = l_ref[0]

    def step(c, dqt, masked):
        at = pl.ds(pl.multiple_of(c * CHUNK, CHUNK), CHUNK)
        p = jnp.exp2(dot_t(k_ref[at, :], q) * EXP_SCALE - logs)
        if masked:
            p = jnp.where(visible(c * CHUNK, block, start), p, 0.0)
        dp = dot_t(v_ref[at, :], do)
        ds = (p * (dp - delta)).astype(LOW)
        dv_acc[at, :] += dot_n(p.astype(LOW), do)
        dk_acc[at, :] += dot_n(ds, q)
        return dqt + dot_n(kt[c], ds)

    dqt = step(last, jnp.zeros((HEAD, 2 * ROWS), F32), True)
    dqt = lax.fori_loop(0, jnp.minimum(last, 1), lambda c, x: step(c, x, True), dqt)
    dqt = lax.fori_loop(1, last, lambda c, x: step(c, x, False), dqt)
    dq_ref[0] = (dqt * SCORE_SCALE).T.astype(LOW)

    @pl.when(i == pl.num_programs(0) - 1)
    def _():
        for z in range(4):
            for y in range(4):
                at = (z * 4 + y) * 256
                part = (dk_acc[at : at + 256, :] * SCORE_SCALE).astype(LOW)
                dkv_ref[y, 2 * z : 2 * z + 2, 0] = part.reshape(2, ROWS, HEAD)
                part = dv_acc[at : at + 256, :].astype(LOW)
                dkv_ref[y, 2 * z : 2 * z + 2, 1] = part.reshape(2, ROWS, HEAD)


def attention_forward(info, q, pieces):
    length = 32 * ROWS
    return pl.pallas_call(
        forward_kernel,
        grid=(8,),
        in_specs=[smem(), per_block((2 * ROWS, HEAD))] + [whole((8, 2, ROWS, HEAD))] * 4,
        out_specs=[
            per_block((2 * ROWS, HEAD)),
            per_block((HEAD, 2 * ROWS)),
            per_block((1, 2 * ROWS)),
            whole((length, HEAD)),
            whole((length, HEAD)),
        ],
        out_shape=[
            shaped((8, 2 * ROWS, HEAD), LOW),
            shaped((8, HEAD, 2 * ROWS), F32),
            shaped((8, 1, 2 * ROWS), F32),
            shaped((length, HEAD), LOW),
            shaped((length, HEAD), LOW),
        ],
        scratch_shapes=[pltpu.VMEM((length // CHUNK, HEAD, CHUNK), LOW)],
        compiler_params=pltpu.CompilerParams(vmem_limit_bytes=32 * 2**20),
        cost_estimate=pl.CostEstimate(
            flops=3 * 10**9, bytes_accessed=7 * 2**20, transcendentals=5 * 10**6
        ),
        name="attention_forward",
    )(info, q, *pieces)


def attention_backward(info, q, do, ot, logs, k, v):
    length = k.shape[0]
    return pl.pallas_call(
        backward_kernel,
        grid=(8,),
        in_specs=[
            smem(),
            per_block((2 * ROWS, HEAD)),
            per_block((2 * ROWS, HEAD)),
            per_block((HEAD, 2 * ROWS)),
            per_block((1, 2 * ROWS)),
            whole((length, HEAD)),
            whole((length, HEAD)),
        ],
        out_specs=[per_block((2 * ROWS, HEAD)), whole((4, 8, 2, ROWS, HEAD))],
        out_shape=[
            shaped((8, 2 * ROWS, HEAD), LOW),
            shaped((4, 8, 2, ROWS, HEAD), LOW),
        ],
        scratch_shapes=[
            pltpu.VMEM((length // CHUNK, HEAD, CHUNK), LOW),
            pltpu.VMEM((length, HEAD), F32),
            pltpu.VMEM((length, HEAD), F32),
        ],
        compiler_params=pltpu.CompilerParams(vmem_limit_bytes=32 * 2**20),
        cost_estimate=pl.CostEstimate(
            flops=8 * 10**9, bytes_accessed=10 * 2**20, transcendentals=5 * 10**6
        ),
        name="attention_backward",
    )(info, q, do, ot, logs, k, v)


def rotary_tables(where_at):
    half = HEAD // 2
    frequency = THETA ** (-(jnp.arange(half, dtype=F32) * 2.0) / HEAD)
    angles = where_at.astype(F32)[:, None] * frequency[None, :]
    cosine, sine = jnp.cos(angles), jnp.sin(angles)
    return jnp.concatenate([cosine, cosine], axis=-1), jnp.concatenate([-sine, sine], axis=-1)


def exchange_heads(value):
    return lax.all_to_all(value, ("z", "xh"), split_axis=0, concat_axis=0, tiled=True)


def pack_feed(w_gate, w_up, w_out, w_down):
    blocks = [w[:, n * 1024 : n * 1024 + 1024] for w in (w_gate, w_up) for n in range(3)]
    blocks += [w[n : n + 256] for w in (w_out, w_down) for n in range(0, w.shape[0], 256)]
    parts = []
    for first, end in FEED_CUTS:
        rows = []
        while first < end:
            block, off = divmod(first, 256)
            size = min(256 - off, end - first)
            rows.append(blocks[block][off : off + size])
            first += size
        parts.append(jnp.concatenate(rows, axis=0))
    return parts


def x_pair(value):
    return lax.ppermute(value, "xl", [(0, 1), (1, 0)])


def local(
    tokens,
    positions,
    attn_gain,
    w_query,
    w_key,
    w_value,
    query_gain,
    key_gain,
    w_out,
    ffn_gain,
    w_gate,
    w_up,
    w_down,
    cotangent,
):
    xl = lax.axis_index("xl")
    co = lax.axis_index("co")
    y = lax.axis_index("y")
    block = lax.axis_index("z") * 8 + y * 2 + lax.axis_index("xh")
    shard = xl * 2 + co
    shards = jnp.stack([shard, 2 * (1 - xl) + co, 2 * xl + 1 - co, 2 * (1 - xl) + 1 - co])
    shards = shards.astype(jnp.int32)

    qkv_pieces = gather_weight(jnp.concatenate([w_query, w_key, w_value], axis=1))

    gains = jnp.concatenate([attn_gain, ffn_gain, query_gain, key_gain])
    gains = jnp.concatenate([gains, jnp.zeros((1024 - 576,), LOW)]).reshape(1, 8, 128)
    pair = jnp.concatenate([gains, x_pair(gains)], axis=0)
    pair = jnp.where(xl == 0, pair, pair[::-1])
    swapped = core_swap(pair)
    quad = jnp.where(co == 0, jnp.stack([pair, swapped], 1), jnp.stack([swapped, pair], 1))
    quad = quad.reshape(4, 1024).astype(F32)
    gain_one = quad[:, :256].reshape(1, 1024)
    gain_two = quad[:, 256:512].reshape(1, 1024)
    gain_query = quad[:, 512:544].reshape(1, 128)
    gain_key = quad[:, 544:576].reshape(1, 128)

    packed = pack_feed(w_gate, w_up, w_out, w_down)
    feed_across = [x_shift(packed[0], 1), x_shift(packed[1], -1)]

    start = block * ROWS + ROWS - 1 - positions[ROWS - 1]
    info = jnp.stack([start, y]).astype(jnp.int32)
    cosine, sine = rotary_tables(positions)
    query, kv_send, raw, left_one = project(
        shards, tokens, gain_one, gain_query, gain_key, cosine, sine, qkv_pieces
    )

    heads_send = jnp.concatenate([query.reshape(8, 2, ROWS, HEAD), kv_send], axis=1)
    heads_send, feed_across[0], feed_across[1] = lax.optimization_barrier(
        (heads_send, feed_across[0], feed_across[1])
    )
    heads = exchange_heads(heads_send)
    heads, packed[2], packed[3] = lax.optimization_barrier((heads, packed[2], packed[3]))
    kv = heads[:, 2:]
    q_all = heads[:, :2].reshape(8, 2 * ROWS, HEAD)
    kv_pieces = [kv, shift(kv, "y", 1), shift(kv, "y", 2), shift(kv, "y", 3)]
    feed_across += [x_shift(packed[2], 1), x_shift(packed[3], -1)]
    o_send, mixed_t, logs, k_all, v_all = attention_forward(info, q_all, kv_pieces)
    o_send, feed_across[2], feed_across[3] = lax.optimization_barrier(
        (o_send, feed_across[2], feed_across[3])
    )
    feed_pieces = packed + feed_across
    feed_pieces = feed_pieces + [core_swap(piece) for piece in feed_pieces]
    merged = exchange_heads(o_send).reshape(16, ROWS, HEAD)

    output, grad_middle, lefts, right, grad_merged, gain_two_term = feed(
        shards, merged, tokens, cotangent, gain_two, feed_pieces
    )

    feed_part = feed_weight_grads(
        pick(lefts, co, 0), core_swap(pick(lefts, 1 - co, 0)), right, core_swap(right)
    )

    do_all = exchange_heads(grad_merged.reshape(8, 2 * ROWS, HEAD))
    do_all, feed_part = lax.optimization_barrier((do_all, feed_part))
    feed_part = reduce_zy(feed_part)
    dq_all, dkv_all = attention_backward(info, q_all, do_all, mixed_t, logs, k_all, v_all)
    dkv = reduce_over(dkv_all, "y", 0)
    back = exchange_heads(jnp.concatenate([dq_all.reshape(8, 2, ROWS, HEAD), dkv], axis=1))

    grad_tokens, attention_grads, terms = tail(
        shards,
        back,
        raw,
        tokens,
        grad_middle,
        gain_one,
        gain_query,
        gain_key,
        cosine,
        sine,
        qkv_pieces,
    )
    terms = jnp.concatenate([terms[:, :1024], gain_two_term, terms[:, 1024:]], axis=1)
    terms = jnp.pad(terms.reshape(18, 128), ((0, 14), (0, 0)))
    terms = terms + core_swap(terms)
    attention_part = attention_weight_grads(
        pick(left_one, co, 0),
        core_swap(pick(left_one, 1 - co, 0)),
        attention_grads,
        core_swap(attention_grads),
        terms,
    )
    attention_part, feed_part = lax.optimization_barrier((attention_part, feed_part))
    attention_part = exchange_zy(attention_part)
    feed_sum = reduce_x_gather(feed_part)
    wide = reduce_x_gather(attention_part)
    grad_down = jnp.concatenate(
        [feed_sum[:, 6144 + 1024 * g : 7168 + 1024 * g] for g in range(3)], axis=0
    )
    grad_out = jnp.concatenate(
        [feed_sum[:, 9216 + 1024 * g : 10240 + 1024 * g] for g in range(2)], axis=0
    )
    gain_all = wide[:18, 4096:4224].reshape(2304)
    return (
        output,
        grad_tokens,
        lax.dynamic_slice_in_dim(gain_all, shard * 256, 256),
        wide[:, :2048],
        wide[:, 2048:3072],
        wide[:, 3072:4096],
        lax.dynamic_slice_in_dim(gain_all, 2048 + shard * 32, 32),
        lax.dynamic_slice_in_dim(gain_all, 2176 + shard * 32, 32),
        grad_out,
        lax.dynamic_slice_in_dim(gain_all, 1024 + shard * 256, 256),
        feed_sum[:, :3072],
        feed_sum[:, 3072:6144],
        grad_down,
    )


def solution(mesh):
    axes = ("xl", "co", "z", "y", "xh")
    fine = Mesh(mesh.devices.reshape(2, 2, 4, 4, 2), axes)
    rows = P(axes, None)
    shard = P(("xl", "co"), None)
    vector = P(("xl", "co"))
    in_specs = (
        rows,
        P(axes),
        vector,
        shard,
        shard,
        shard,
        vector,
        vector,
        shard,
        vector,
        shard,
        shard,
        shard,
        rows,
    )
    out_specs = (
        rows,
        rows,
        vector,
        shard,
        shard,
        shard,
        vector,
        vector,
        shard,
        vector,
        shard,
        shard,
        shard,
    )
    return jax.shard_map(local, mesh=fine, in_specs=in_specs, out_specs=out_specs, check_vma=False)
```

```python
import jax
import jax.numpy as jnp
from jax import lax
from jax.experimental import pallas as pl
from jax.experimental.pallas import tpu as pltpu
from jax.sharding import Mesh
from jax.sharding import PartitionSpec as P

EPSILON = 1e-06
THETA = 1000000.0
HEAD = 128
ROWS = 128
CHUNK = 512
SCORE_SCALE = HEAD ** (-0.5)
LOG2_E = 1.4426950408889634
EXP_SCALE = SCORE_SCALE * LOG2_E
LOW = jnp.bfloat16
FEED_CUTS = ((0, 256), (1408, 1664), (256, 1408), (1664, 2816))
F32 = jnp.float32


def x_shift(value, step):
    pairs = []
    for x in range(4):
        to = (x + step) % 4
        pairs.append(((x % 2) * 2 + x // 2, (to % 2) * 2 + to // 2))
    return lax.ppermute(value, ("xl", "xh"), pairs)


def shift(value, axis, step):
    if axis == "x":
        return x_shift(value, step)
    return lax.ppermute(value, axis, [(i, (i + step) % 4) for i in range(4)])


def core_swap(value):
    return lax.ppermute(value, "co", [(0, 1), (1, 0)])


def place_on(axis):
    if axis == "x":
        return lax.axis_index("xh") * 2 + lax.axis_index("xl")
    return lax.axis_index(axis)


def pick(value, index, dim):
    return lax.dynamic_index_in_dim(value, index, dim, keepdims=False)


def send_parts(value, axis, dim):
    me = place_on(axis)
    got = [shift(pick(value, (me + step) % 4, dim), axis, step) for step in (1, 3, 2)]
    return [pick(value, me, dim)] + got


def add_parts(parts):
    total = parts[0].astype(F32)
    for part in parts[1:]:
        total = total + part.astype(F32)
    return total.astype(LOW)


def reduce_over(value, axis, dim):
    return add_parts(send_parts(value, axis, dim))


def gather_over(value, axis, dim, dtype=LOW):
    me = place_on(axis)
    shape = value.shape[:dim] + (4,) + value.shape[dim:]
    out = jnp.zeros(shape, dtype)
    out = lax.dynamic_update_index_in_dim(out, value.astype(dtype), me, dim)
    for step in (1, 3, 2):
        got = shift(value, axis, step).astype(dtype)
        out = lax.dynamic_update_index_in_dim(out, got, (me - step) % 4, dim)
    return out


def gather_both_ways(value, axis, dim):
    me = place_on(axis)
    half = value.shape[0] // 2
    before = shift(value, axis, 1)
    after = shift(value, axis, -1)
    across = [shift(before[:half], axis, 1), shift(after[half:], axis, -1)]
    out = jnp.zeros(value.shape[:dim] + (4,) + value.shape[dim:], F32)
    for part, step in ((value, 0), (before, 1), (after, 3), (jnp.concatenate(across), 2)):
        out = lax.dynamic_update_index_in_dim(out, part.astype(F32), (me - step) % 4, dim)
    return out


def exchange_y(value):
    return lax.all_to_all(value, "y", split_axis=0, concat_axis=0, tiled=True)


def send_first(first, second):
    first = exchange_y(first.reshape(4, 64, first.shape[-1]))
    return first, send_parts(second.reshape(4, 64, second.shape[-1]), "z", 0)


def add_first(first, second):
    return jnp.sum(first.astype(F32), axis=0).astype(LOW), add_parts(second)


def reduce_second(first, second):
    second = exchange_y(second.reshape(4, 16, second.shape[-1]))
    first = reduce_over(first.reshape(4, 16, first.shape[-1]), "z", 0)
    return first, jnp.sum(second.astype(F32), axis=0).astype(LOW)


def add_xh(part):
    other = lax.ppermute(part, "xh", [(0, 1), (1, 0)])
    return (part.astype(F32) + other.astype(F32)).astype(LOW)


def gather_weight(shard):
    half = shard.shape[0] // 2
    up = x_shift(shard[:half], 1)
    down = x_shift(shard[half:], -1)
    return [shard, up, down, core_swap(shard), core_swap(up), core_swap(down)]


def dot_t(left, right):
    return lax.dot_general(left, right, (((1,), (1,)), ((), ())), preferred_element_type=F32)


def dot_n(left, right):
    return lax.dot_general(left, right, (((1,), (0,)), ((), ())), preferred_element_type=F32)


def dot_r(left, right):
    return lax.dot_general(left, right, (((0,), (0,)), ((), ())), preferred_element_type=F32)


def whole(shape):
    return pl.BlockSpec(shape, lambda *_: (0,) * len(shape))


def per_block(shape):
    return pl.BlockSpec((1,) + shape, lambda i: (i,) + (0,) * len(shape))


def smem():
    return pl.BlockSpec(memory_space=pltpu.SMEM)


def anywhere():
    return pl.BlockSpec(memory_space=pl.ANY)


def shaped(shape, dtype):
    return pltpu.HBM(shape, dtype)


def held(arrays):
    return [pltpu.with_memory_space_constraint(array, pltpu.HBM) for array in arrays]


def fetch(shards, pieces, full, sems):
    rows = pieces[0].shape[0]
    half = rows // 2
    at = [
        shards[0] * rows,
        shards[1] * rows,
        shards[1] * rows + half,
        shards[2] * rows,
        shards[3] * rows,
        shards[3] * rows + half,
    ]
    copies = []
    for n, (piece, where) in enumerate(zip(pieces, at)):
        where = pl.multiple_of(where, half)
        copy = pltpu.make_async_copy(
            piece, full.at[pl.ds(where, piece.shape[0]), :], sems.at[n]
        )
        copy.start()
        copies.append(copy)
    return copies


def fetch_feed(shards, pieces, w_out, w_gu, w_down, sems):
    groups = ([], [], [], [], [])
    n = 0
    for s in range(4):
        for part, (first, end) in enumerate(FEED_CUTS):
            piece = pieces[len(FEED_CUTS) * s + part]
            at = 0
            while first + at < end:
                block, off = divmod(first + at, 256)
                size = min(256 - off, end - first - at)
                src = piece.at[pl.ds(at, size), :]
                if block < 6:
                    where = pl.multiple_of(shards[s] * 256 + off, 128)
                    dst = w_gu.at[pl.ds(where, size), pl.ds(block * 1024, 1024)]
                    group = (1, 3, 4)[block % 3]
                elif block < 8:
                    where = pl.multiple_of(shards[s] * 512 + (block - 6) * 256 + off, 128)
                    dst = w_out.at[pl.ds(where, size), :]
                    group = 0
                else:
                    where = pl.multiple_of(shards[s] * 768 + (block - 8) * 256 + off, 128)
                    dst = w_down.at[pl.ds(where, size), :]
                    group = 2
                groups[group].append(pltpu.make_async_copy(src, dst, sems.at[n]))
                n += 1
                at += size
    for group in groups:
        for copy in group:
            copy.start()
    return groups


def settle(copies):
    for copy in copies:
        copy.wait()


def scale_of(value):
    return lax.rsqrt(jnp.mean(value * value, axis=-1, keepdims=True) + EPSILON)


def turn(value):
    return jnp.concatenate([value[:, HEAD // 2 :], value[:, : HEAD // 2]], axis=1)


def project_kernel(
    shards, x_ref, gain_ref, gq_ref, gk_ref, cos_ref, sin_ref, *rest
):
    pieces, (q_ref, kv_ref, raw_ref, left_ref, w, sems) = rest[:6], rest[6:]
    copies = fetch(shards, pieces, w, sems)
    x = x_ref[...].astype(F32)
    h = (x * scale_of(x) * gain_ref[...]).astype(LOW)
    for f in range(4):
        left_ref[f // 2, f % 2] = h[:, f * 256 : f * 256 + 256]
    cosine, sine = cos_ref[...], sin_ref[...]
    settle(copies)
    for tile in range(8):
        product = dot_n(h, w[:, tile * 512 : tile * 512 + 512])
        for part in range(4):
            n = tile * 4 + part
            raw = product[:, part * HEAD : part * HEAD + HEAD]
            if n >= 24:
                kv_ref[n - 24, 1] = raw.astype(LOW)
                continue
            raw_ref[n] = raw
            gain = gq_ref[...] if n < 16 else gk_ref[...]
            u = raw * scale_of(raw) * gain
            u = (u * cosine + turn(u) * sine).astype(LOW)
            if n < 16:
                q_ref[n] = u
            else:
                kv_ref[n - 16, 0] = u


def project(shards, x, gain, gain_q, gain_k, cosine, sine, pieces):
    return pl.pallas_call(
        project_kernel,
        in_specs=[smem()] + [pl.BlockSpec(memory_space=pltpu.VMEM)] * 6 + [anywhere()] * 6,
        out_shape=[
            shaped((16, ROWS, HEAD), LOW),
            shaped((8, 2, ROWS, HEAD), LOW),
            shaped((24, ROWS, HEAD), F32),
            shaped((2, 2, ROWS, 256), LOW),
        ],
        scratch_shapes=[pltpu.VMEM((1024, 4096), LOW), pltpu.SemaphoreType.DMA((6,))],
        compiler_params=pltpu.CompilerParams(vmem_limit_bytes=32 * 2**20),
        cost_estimate=pl.CostEstimate(
            flops=10**9, bytes_accessed=12 * 2**20, transcendentals=10**4
        ),
        name="project",
    )(shards, *held([x, gain, gain_q, gain_k, cosine, sine, *pieces]))


def feed_kernel(shards, o_ref, x_ref, cot_ref, gain_ref, *rest):
    (y_ref, mid_ref, left_ref, right_ref, do_ref, term_ref) = rest[16:22]
    (w_out, w_gu, w_down, merged, sems) = rest[22:]
    out_copies, gu_copies, down_copies, gu_next, gu_last = fetch_feed(shards, rest[:16], w_out, w_gu, w_down, sems)
    for n in range(16):
        merged[:, n * HEAD : n * HEAD + HEAD] = o_ref[n]
    for f in range(4):
        for g in range(2):
            at = f * 512 + g * 256
            left_ref[f // 2, f % 2, 4 + g] = merged[:, at : at + 256]
    cot = cot_ref[...]
    gain = gain_ref[...]
    settle(out_copies)
    middle = x_ref[...].astype(F32) + dot_n(merged[...], w_out[...])
    scale = scale_of(middle)
    normal = middle * scale
    h = (normal * gain).astype(LOW)
    for f in range(4):
        left_ref[f // 2, f % 2, 0] = h[:, f * 256 : f * 256 + 256]
    settle(gu_copies)
    settle(down_copies)
    total = middle
    dh = jnp.zeros_like(middle)
    for tile in range(6):
        if tile == 2:
            settle(gu_next)
        if tile == 4:
            settle(gu_last)
        at = tile * 512
        gate = dot_n(h, w_gu[:, at : at + 512])
        up = dot_n(h, w_gu[:, 3072 + at : 3072 + at + 512])
        sg = 1.0 / (1.0 + jnp.exp(-gate))
        swish = gate * sg
        hidden = (swish * up).astype(LOW)
        for part in range(2):
            f, g = divmod(tile * 2 + part, 3)
            left_ref[f // 2, f % 2, 1 + g] = hidden[:, part * 256 : part * 256 + 256]
        total = total + dot_n(hidden, w_down[at : at + 512, :])
        dhidden = dot_t(cot, w_down[at : at + 512, :])
        dgate = (dhidden * up * sg * (1.0 + gate * (1.0 - sg))).astype(LOW)
        dup = (dhidden * swish).astype(LOW)
        right_ref[:, at : at + 512] = dgate
        right_ref[:, 3072 + at : 3072 + at + 512] = dup
        dh = dh + dot_t(dgate, w_gu[:, at : at + 512])
        dh = dh + dot_t(dup, w_gu[:, 3072 + at : 3072 + at + 512])
    y_ref[...] = total.astype(LOW)
    term_ref[...] = jnp.sum(dh * normal, axis=0, keepdims=True)
    dn = dh * gain
    dmid = cot.astype(F32) + scale * (dn - normal * jnp.mean(dn * normal, axis=-1, keepdims=True))
    mid_ref[...] = dmid
    da = dmid.astype(LOW)
    right_ref[:, 6144:] = da
    for tile in range(4):
        back = dot_t(da, w_out[tile * 512 : tile * 512 + 512, :]).astype(LOW)
        for part in range(4):
            do_ref[tile * 4 + part] = back[:, part * HEAD : part * HEAD + HEAD]


def feed(shards, o, x, cot, gain, pieces):
    return pl.pallas_call(
        feed_kernel,
        in_specs=[smem()] + [pl.BlockSpec(memory_space=pltpu.VMEM)] * 4 + [anywhere()] * 16,
        out_shape=[
            shaped((ROWS, 1024), LOW),
            shaped((ROWS, 1024), F32),
            shaped((2, 2, 6, ROWS, 256), LOW),
            shaped((ROWS, 7168), LOW),
            shaped((16, ROWS, HEAD), LOW),
            shaped((1, 1024), F32),
        ],
        scratch_shapes=[
            pltpu.VMEM((2048, 1024), LOW),
            pltpu.VMEM((1024, 6144), LOW),
            pltpu.VMEM((3072, 1024), LOW),
            pltpu.VMEM((ROWS, 2048), LOW),
            pltpu.SemaphoreType.DMA((52,)),
        ],
        compiler_params=pltpu.CompilerParams(vmem_limit_bytes=48 * 2**20),
        cost_estimate=pl.CostEstimate(
            flops=7 * 10**9, bytes_accessed=30 * 2**20, transcendentals=10**6
        ),
        name="feed",
    )(shards, *held([o, x, cot, gain, *pieces]))


def lay_left(left_t, part, left, turned):
    columns = left.astype(F32).T.astype(LOW)
    at = slice(part * ROWS, part * ROWS + ROWS)
    if not turned:
        left_t[:, at] = columns
        return
    for y in range(4):
        for z in range(4):
            to, row = (z * 4 + y) * 16, (y * 4 + z) * 16
            left_t[to : to + 16, at] = columns[row : row + 16, :]


def weight_kernel(*refs):
    lefts, rights, cots, (first_ref, second_ref, left_t, right) = (
        refs[:4],
        refs[4:8],
        refs[8:12],
        refs[12:],
    )
    t = pl.program_id(0)

    @pl.when(t == 0)
    def _():
        for part in range(4):
            lay_left(left_t, part, lefts[part][0], False)

    @pl.when(t >= 6)
    def _():
        for part in range(4):
            lay_left(left_t, part, lefts[part][0], True)

    @pl.when((t < 6) | (t >= 9))
    def _():
        for part in range(4):
            right[part * ROWS : part * ROWS + ROWS, :] = rights[part][...]

    @pl.when(t == 6)
    def _():
        for part in range(4):
            right[part * ROWS : part * ROWS + ROWS, :] = cots[part][...]

    @pl.when(t < 6)
    def _():
        first_ref[...] = dot_n(left_t[...], right[...]).astype(LOW)

    @pl.when(t >= 6)
    def _():
        second_ref[...] = dot_n(left_t[...], right[...]).astype(LOW)


def feed_weight_grads(lefts, rights, cots):
    left = pl.BlockSpec((1, ROWS, 256), lambda t: (jnp.maximum(t - 5, 0), 0, 0))
    wide = pl.BlockSpec((ROWS, 1024), lambda t: (0, jnp.where(t < 6, t, jnp.where(t < 9, 5, 6))))
    return pl.pallas_call(
        weight_kernel,
        grid=(11,),
        in_specs=[left] * 4 + [wide] * 4 + [whole((ROWS, 1024))] * 4,
        out_specs=[
            pl.BlockSpec((256, 1024), lambda t: (0, jnp.minimum(t, 5))),
            pl.BlockSpec((256, 1024), lambda t: (0, jnp.maximum(t - 6, 0))),
        ],
        out_shape=[shaped((256, 6144), LOW), shaped((256, 5120), LOW)],
        scratch_shapes=[pltpu.VMEM((256, 4 * ROWS), LOW), pltpu.VMEM((4 * ROWS, 1024), LOW)],
        compiler_params=pltpu.CompilerParams(vmem_limit_bytes=24 * 2**20),
        cost_estimate=pl.CostEstimate(
            flops=3 * 10**9, bytes_accessed=16 * 2**20, transcendentals=0
        ),
        name="feed_weight_grads",
    )(*held([*lefts, *rights, *cots]))


def attention_weight_kernel(*refs):
    lefts, rights, (term_ref, first_ref, second_ref, left_t, right) = refs[:4], refs[4:8], refs[8:]
    t = pl.program_id(0)

    @pl.when(t == 0)
    def _():
        for part in range(4):
            lay_left(left_t, part, lefts[part][...], False)

    @pl.when(t == 4)
    def _():
        for part in range(4):
            lay_left(left_t, part, lefts[part][...], True)

    for part in range(4):
        right[part * ROWS : part * ROWS + ROWS, :] = rights[part][...]

    @pl.when(t < 4)
    def _():
        first_ref[...] = dot_n(left_t[...], right[...]).astype(LOW)

    @pl.when((t >= 4) & (t < 8))
    def _():
        second_ref[...] = dot_n(left_t[...], right[...]).astype(LOW)

    @pl.when(t == 8)
    def _():
        second_ref[...] = jnp.zeros_like(second_ref)
        for z in range(2):
            at = z * 64
            second_ref[at : at + 16, :HEAD] = term_ref[z * 16 : z * 16 + 16, :].astype(LOW)


def attention_weight_grads(lefts, rights, terms):
    wide = pl.BlockSpec((ROWS, 512), lambda t: (0, jnp.minimum(t, 7)))
    return pl.pallas_call(
        attention_weight_kernel,
        grid=(9,),
        in_specs=[whole((ROWS, 256))] * 4 + [wide] * 4 + [whole((32, HEAD))],
        out_specs=[
            pl.BlockSpec((256, 512), lambda t: (0, jnp.minimum(t, 3))),
            pl.BlockSpec((256, 512), lambda t: (0, jnp.maximum(t - 4, 0))),
        ],
        out_shape=[shaped((256, 2048), LOW), shaped((256, 2560), LOW)],
        scratch_shapes=[pltpu.VMEM((256, 4 * ROWS), LOW), pltpu.VMEM((4 * ROWS, 512), LOW)],
        compiler_params=pltpu.CompilerParams(vmem_limit_bytes=16 * 2**20),
        cost_estimate=pl.CostEstimate(flops=10**9, bytes_accessed=6 * 2**20, transcendentals=0),
        name="attention_weight_grads",
    )(*held([*lefts, *rights, terms]))


def raw_grads_kernel(back_ref, raw_ref, gq_ref, gk_ref, cos_ref, sin_ref, right_ref, term_ref):
    cosine, sine = cos_ref[...], sin_ref[...]
    for heads, first, place, gain_ref in ((16, 0, 0, gq_ref), (8, 16, HEAD, gk_ref)):
        gain = gain_ref[...]
        term = jnp.zeros((ROWS, HEAD), F32)
        for n in range(heads):
            grad = back_ref[n // 2, n % 2] if first == 0 else back_ref[n, 2]
            grad = grad.astype(F32)
            raw = raw_ref[first + n]
            scale = scale_of(raw)
            unit = raw * scale
            grad = grad * cosine - turn(grad) * sine
            term = term + grad * unit
            grad = grad * gain
            grad = scale * (grad - unit * jnp.mean(grad * unit, axis=-1, keepdims=True))
            at = (first + n) * HEAD
            right_ref[:, at : at + HEAD] = grad.astype(LOW)
        term_ref[:, place : place + HEAD] = jnp.sum(term, axis=0, keepdims=True)
    for n in range(8):
        at = 3072 + n * HEAD
        right_ref[:, at : at + HEAD] = back_ref[n, 3]


def raw_grads(back, raw, gain_q, gain_k, cosine, sine):
    return pl.pallas_call(
        raw_grads_kernel,
        in_specs=[pl.BlockSpec(memory_space=pltpu.VMEM)] * 6,
        out_shape=[shaped((ROWS, 4096), LOW), shaped((1, 2 * HEAD), F32)],
        compiler_params=pltpu.CompilerParams(vmem_limit_bytes=16 * 2**20),
        cost_estimate=pl.CostEstimate(
            flops=10**7, bytes_accessed=4 * 2**20, transcendentals=10**4
        ),
        name="raw_grads",
    )(*held([back, raw, gain_q, gain_k, cosine, sine]))


def token_grads_kernel(shards, right_ref, x_ref, mid_ref, gain_ref, *rest):
    pieces, (grad_ref, term_ref, w, sems) = rest[:6], rest[6:]
    copies = fetch(shards, pieces, w, sems)
    x = x_ref[...].astype(F32)
    scale = scale_of(x)
    normal = x * scale
    settle(copies)
    dh = dot_t(right_ref[...], w[...])
    term_ref[...] = jnp.sum(dh * normal, axis=0, keepdims=True)
    dn = dh * gain_ref[...]
    grad_ref[...] = mid_ref[...] + scale * (
        dn - normal * jnp.mean(dn * normal, axis=-1, keepdims=True)
    )


def token_grads(shards, right, x, mid, gain, pieces):
    return pl.pallas_call(
        token_grads_kernel,
        in_specs=[smem()] + [pl.BlockSpec(memory_space=pltpu.VMEM)] * 4 + [anywhere()] * 6,
        out_shape=[shaped((ROWS, 1024), F32), shaped((1, 1024), F32)],
        scratch_shapes=[pltpu.VMEM((1024, 4096), LOW), pltpu.SemaphoreType.DMA((6,))],
        compiler_params=pltpu.CompilerParams(vmem_limit_bytes=32 * 2**20),
        cost_estimate=pl.CostEstimate(
            flops=10**9, bytes_accessed=12 * 2**20, transcendentals=10**4
        ),
        name="token_grads",
    )(shards, *held([right, x, mid, gain, *pieces]))


def visible(first_key, query_block, start):
    key = first_key + lax.broadcasted_iota(jnp.int32, (CHUNK, 2 * ROWS), 0)
    query = query_block * ROWS + (lax.broadcasted_iota(jnp.int32, (CHUNK, 2 * ROWS), 1) & (ROWS - 1))
    return (key <= query) & ((key >= start) | (query < start))


def block_of(info):
    i = pl.program_id(0)
    return (i // 2) * 8 + info[1] * 2 + i % 2


def columns_of(value):
    return value.astype(F32).T.astype(LOW)


def forward_kernel(info, q_ref, kv0, kv1, kv2, kv3, o_ref, ot_ref, l_ref, k_ref, v_ref, vt):
    block = block_of(info)
    start = info[0]
    last = block // (CHUNK // ROWS)

    @pl.when(pl.program_id(0) == 0)
    def _():
        for back, piece in enumerate((kv0, kv1, kv2, kv3)):
            owner = lax.rem(info[1] + 4 - back, 4)
            for z in range(4):
                at = pl.ds(pl.multiple_of((z * 4 + owner) * 256, 256), 256)
                k_ref[at, :] = piece[2 * z : 2 * z + 2, 0].reshape(256, HEAD)
                v_ref[at, :] = piece[2 * z : 2 * z + 2, 1].reshape(256, HEAD)
        for c in range(vt.shape[0]):
            vt[c] = columns_of(v_ref[c * CHUNK : (c + 1) * CHUNK, :])

    q = q_ref[0]

    def step(c, carry, masked):
        total, mixed = carry
        keys = k_ref[pl.ds(pl.multiple_of(c * CHUNK, CHUNK), CHUNK), :]
        p = jnp.exp2(dot_t(keys, q) * EXP_SCALE)
        if masked:
            p = jnp.where(visible(c * CHUNK, block, start), p, 0.0)
        total = total + jnp.sum(p.reshape(CHUNK // 8, 8, 2 * ROWS), axis=0)
        mixed = mixed + dot_n(vt[c], p.astype(LOW))
        return total, mixed

    carry = (jnp.zeros((8, 2 * ROWS), F32), jnp.zeros((HEAD, 2 * ROWS), F32))
    carry = step(last, carry, True)
    carry = lax.fori_loop(0, jnp.minimum(last, 1), lambda c, x: step(c, x, True), carry)
    pairs = jnp.maximum(last - 1, 0) // 2
    carry = lax.fori_loop(
        0, pairs, lambda n, x: step(2 * n + 2, step(2 * n + 1, x, False), False), carry
    )
    carry = lax.fori_loop(2 * pairs + 1, last, lambda c, x: step(c, x, False), carry)
    total = jnp.sum(carry[0], axis=0, keepdims=True)
    mixed = carry[1] / total
    ot_ref[0] = mixed
    o_ref[0] = mixed.T.astype(LOW)
    l_ref[0] = jnp.log2(total)


def backward_kernel(
    info, q_ref, do_ref, ot_ref, l_ref, k_ref, v_ref, dq_ref, dkv_ref, kt, dk_acc, dv_acc
):
    i = pl.program_id(0)
    block = block_of(info)
    start = info[0]
    q = q_ref[0]
    do = do_ref[0]
    last = block // (CHUNK // ROWS)

    @pl.when(i == 0)
    def _():
        dk_acc[...] = jnp.zeros_like(dk_acc)
        dv_acc[...] = jnp.zeros_like(dv_acc)
        for c in range(kt.shape[0]):
            kt[c] = columns_of(k_ref[c * CHUNK : (c + 1) * CHUNK, :])

    delta = jnp.sum(do.astype(F32).T * ot_ref[0], axis=0, keepdims=True)
    logs = l_ref[0]

    def step(c, dqt, masked):
        at = pl.ds(pl.multiple_of(c * CHUNK, CHUNK), CHUNK)
        p = jnp.exp2(dot_t(k_ref[at, :], q) * EXP_SCALE - logs)
        if masked:
            p = jnp.where(visible(c * CHUNK, block, start), p, 0.0)
        dp = dot_t(v_ref[at, :], do)
        ds = (p * (dp - delta)).astype(LOW)
        dv_acc[at, :] += dot_n(p.astype(LOW), do)
        dk_acc[at, :] += dot_n(ds, q)
        return dqt + dot_n(kt[c], ds)

    dqt = step(last, jnp.zeros((HEAD, 2 * ROWS), F32), True)
    dqt = lax.fori_loop(0, jnp.minimum(last, 1), lambda c, x: step(c, x, True), dqt)
    pairs = jnp.maximum(last - 1, 0) // 2
    dqt = lax.fori_loop(
        0, pairs, lambda n, x: step(2 * n + 2, step(2 * n + 1, x, False), False), dqt
    )
    dqt = lax.fori_loop(2 * pairs + 1, last, lambda c, x: step(c, x, False), dqt)
    dq_ref[0] = (dqt * SCORE_SCALE).T.astype(LOW)

    @pl.when(i == pl.num_programs(0) - 1)
    def _():
        for z in range(4):
            for y in range(4):
                at = (z * 4 + y) * 256
                part = (dk_acc[at : at + 256, :] * SCORE_SCALE).astype(LOW)
                dkv_ref[y, 2 * z : 2 * z + 2, 0] = part.reshape(2, ROWS, HEAD)
                part = dv_acc[at : at + 256, :].astype(LOW)
                dkv_ref[y, 2 * z : 2 * z + 2, 1] = part.reshape(2, ROWS, HEAD)


def attention_forward(info, q, pieces):
    length = 32 * ROWS
    return pl.pallas_call(
        forward_kernel,
        grid=(8,),
        in_specs=[smem(), per_block((2 * ROWS, HEAD))] + [whole((8, 2, ROWS, HEAD))] * 4,
        out_specs=[
            per_block((2 * ROWS, HEAD)),
            per_block((HEAD, 2 * ROWS)),
            per_block((1, 2 * ROWS)),
            whole((length, HEAD)),
            whole((length, HEAD)),
        ],
        out_shape=[
            shaped((8, 2 * ROWS, HEAD), LOW),
            shaped((8, HEAD, 2 * ROWS), F32),
            shaped((8, 1, 2 * ROWS), F32),
            shaped((length, HEAD), LOW),
            shaped((length, HEAD), LOW),
        ],
        scratch_shapes=[pltpu.VMEM((length // CHUNK, HEAD, CHUNK), LOW)],
        compiler_params=pltpu.CompilerParams(vmem_limit_bytes=32 * 2**20),
        cost_estimate=pl.CostEstimate(
            flops=3 * 10**9, bytes_accessed=7 * 2**20, transcendentals=5 * 10**6
        ),
        name="attention_forward",
    )(info, *held([q, *pieces]))


def attention_backward(info, q, do, ot, logs, k, v):
    length = k.shape[0]
    return pl.pallas_call(
        backward_kernel,
        grid=(8,),
        in_specs=[
            smem(),
            per_block((2 * ROWS, HEAD)),
            per_block((2 * ROWS, HEAD)),
            per_block((HEAD, 2 * ROWS)),
            per_block((1, 2 * ROWS)),
            whole((length, HEAD)),
            whole((length, HEAD)),
        ],
        out_specs=[per_block((2 * ROWS, HEAD)), whole((4, 8, 2, ROWS, HEAD))],
        out_shape=[
            shaped((8, 2 * ROWS, HEAD), LOW),
            shaped((4, 8, 2, ROWS, HEAD), LOW),
        ],
        scratch_shapes=[
            pltpu.VMEM((length // CHUNK, HEAD, CHUNK), LOW),
            pltpu.VMEM((length, HEAD), F32),
            pltpu.VMEM((length, HEAD), F32),
        ],
        compiler_params=pltpu.CompilerParams(vmem_limit_bytes=32 * 2**20),
        cost_estimate=pl.CostEstimate(
            flops=8 * 10**9, bytes_accessed=10 * 2**20, transcendentals=5 * 10**6
        ),
        name="attention_backward",
    )(info, *held([q, do, ot, logs, k, v]))


def rotary_tables(where_at):
    half = HEAD // 2
    frequency = THETA ** (-(jnp.arange(half, dtype=F32) * 2.0) / HEAD)
    angles = where_at.astype(F32)[:, None] * frequency[None, :]
    cosine, sine = jnp.cos(angles), jnp.sin(angles)
    return jnp.concatenate([cosine, cosine], axis=-1), jnp.concatenate([-sine, sine], axis=-1)


def exchange_heads(value):
    return lax.all_to_all(value, ("z", "xh"), split_axis=0, concat_axis=0, tiled=True)


def pack_feed(w_gate, w_up, w_out, w_down):
    blocks = [w[:, n * 1024 : n * 1024 + 1024] for w in (w_gate, w_up) for n in range(3)]
    blocks += [w[n : n + 256] for w in (w_out, w_down) for n in range(0, w.shape[0], 256)]
    parts = []
    for first, end in FEED_CUTS:
        rows = []
        while first < end:
            block, off = divmod(first, 256)
            size = min(256 - off, end - first)
            rows.append(blocks[block][off : off + size])
            first += size
        parts.append(jnp.concatenate(rows, axis=0))
    return parts


def spread(value, across):
    return [value, core_swap(value), across, core_swap(across)]


def spread_columns(here, across, co):
    return [
        pick(here, co, 0),
        core_swap(pick(here, 1 - co, 0)),
        pick(across, co, 0),
        core_swap(pick(across, 1 - co, 0)),
    ]


def x_pair(value):
    return lax.ppermute(value, "xl", [(0, 1), (1, 0)])


def local(
    tokens,
    positions,
    attn_gain,
    w_query,
    w_key,
    w_value,
    query_gain,
    key_gain,
    w_out,
    ffn_gain,
    w_gate,
    w_up,
    w_down,
    cotangent,
):
    xl = lax.axis_index("xl")
    co = lax.axis_index("co")
    y = lax.axis_index("y")
    block = lax.axis_index("z") * 8 + y * 2 + lax.axis_index("xh")
    shard = xl * 2 + co
    shards = jnp.stack([shard, 2 * (1 - xl) + co, 2 * xl + 1 - co, 2 * (1 - xl) + 1 - co])
    shards = shards.astype(jnp.int32)
    cots = spread(cotangent, x_pair(cotangent))


    qkv_pieces = gather_weight(jnp.concatenate([w_query, w_key, w_value], axis=1))

    gains = jnp.concatenate([attn_gain, ffn_gain, query_gain, key_gain])
    gains = jnp.concatenate([gains, jnp.zeros((1024 - 576,), LOW)]).reshape(1, 8, 128)
    pair = jnp.concatenate([gains, x_pair(gains)], axis=0)
    pair = jnp.where(xl == 0, pair, pair[::-1])
    swapped = core_swap(pair)
    quad = jnp.where(co == 0, jnp.stack([pair, swapped], 1), jnp.stack([swapped, pair], 1))
    quad = quad.reshape(4, 1024).astype(F32)
    gain_one = quad[:, :256].reshape(1, 1024)
    gain_two = quad[:, 256:512].reshape(1, 1024)
    gain_query = quad[:, 512:544].reshape(1, 128)
    gain_key = quad[:, 544:576].reshape(1, 128)

    packed = pack_feed(w_gate, w_up, w_out, w_down)
    feed_across = [x_shift(packed[0], 1), x_shift(packed[1], -1)]

    start = block * ROWS + ROWS - 1 - positions[ROWS - 1]
    info = jnp.stack([start, y]).astype(jnp.int32)
    cosine, sine = rotary_tables(positions)
    query, kv_send, raw, left_one = project(
        shards, tokens, gain_one, gain_query, gain_key, cosine, sine, qkv_pieces
    )

    heads_send = jnp.concatenate([query.reshape(8, 2, ROWS, HEAD), kv_send], axis=1)
    heads_send, feed_across[0], feed_across[1] = lax.optimization_barrier(
        (heads_send, feed_across[0], feed_across[1])
    )
    heads = exchange_heads(heads_send)
    heads, packed[2], packed[3] = lax.optimization_barrier((heads, packed[2], packed[3]))
    kv = heads[:, 2:]
    q_all = heads[:, :2].reshape(8, 2 * ROWS, HEAD)
    kv_pieces = [kv, shift(kv, "y", 1), shift(kv, "y", 2), shift(kv, "y", 3)]
    feed_across += [x_shift(packed[2], 1), x_shift(packed[3], -1)]
    o_send, mixed_t, logs, k_all, v_all = attention_forward(info, q_all, kv_pieces)
    o_send, feed_across[2], feed_across[3] = lax.optimization_barrier(
        (o_send, feed_across[2], feed_across[3])
    )
    feed_pieces = packed + feed_across
    feed_pieces = feed_pieces + [core_swap(piece) for piece in feed_pieces]
    merged = exchange_heads(o_send).reshape(16, ROWS, HEAD)

    output, grad_middle, lefts, right, grad_merged, gain_two_term = feed(
        shards, merged, tokens, cotangent, gain_two, feed_pieces
    )

    do_all = exchange_heads(grad_merged.reshape(8, 2 * ROWS, HEAD))
    left_parts = spread_columns(pick(left_one, xl, 0), x_pair(pick(left_one, 1 - xl, 0)), co)
    do_all, lefts, right, left_parts, cots = lax.optimization_barrier(
        (do_all, lefts, right, left_parts, cots)
    )
    right_across = x_pair(right)
    lefts_across = x_pair(pick(lefts, 1 - xl, 0))

    dq_all, dkv_all = attention_backward(info, q_all, do_all, mixed_t, logs, k_all, v_all)
    dkv = reduce_over(dkv_all, "y", 0)
    back = jnp.concatenate([dq_all.reshape(8, 2, ROWS, HEAD), dkv], axis=1)
    back, right_across, lefts_across = lax.optimization_barrier((back, right_across, lefts_across))
    back = exchange_heads(back)
    feed_part = feed_weight_grads(
        spread_columns(pick(lefts, xl, 0), lefts_across, co), spread(right, right_across), cots
    )
    back, feed_part = lax.optimization_barrier((back, feed_part))
    feed_first = exchange_y(feed_part[0].reshape(4, 64, 6144))
    feed_second = lax.psum_scatter(feed_part[1], "z", scatter_dimension=0, tiled=True)

    attention_grads, head_terms = raw_grads(back, raw, gain_query, gain_key, cosine, sine)
    attention_across = x_pair(attention_grads)
    grad_tokens, gain_one_term = token_grads(
        shards, attention_grads, tokens, grad_middle, gain_one, qkv_pieces
    )
    terms = jnp.concatenate([gain_one_term, gain_two_term, head_terms], axis=1)
    terms = jnp.pad(terms.reshape(18, 128), ((0, 14), (0, 0)))
    terms = terms + core_swap(terms)
    terms = terms + x_pair(terms)
    attention_across, terms = lax.optimization_barrier((attention_across, terms))
    attention_part = attention_weight_grads(
        left_parts, spread(attention_grads, attention_across), terms
    )
    attention_part, feed_first, feed_second = lax.optimization_barrier(
        (attention_part, feed_first, feed_second)
    )
    attention_parts = send_first(*attention_part)
    feed_first = jnp.sum(feed_first.astype(F32), axis=0).astype(LOW)
    first, second = add_first(*attention_parts)
    first, second = reduce_second(
        jnp.concatenate([feed_first, first], axis=-1),
        jnp.concatenate([feed_second, second], axis=-1),
    )
    both = add_xh(jnp.concatenate([first, second], axis=-1))
    first = gather_over(both[:, :8192], "z", 0)
    second = gather_over(both[:, 8192:], "y", 0)
    first = gather_both_ways(first, "y", 0).reshape(256, 8192)
    second = gather_both_ways(second, "z", 1).reshape(256, 7680)
    grad_down = jnp.concatenate([second[:, 1024 * g : 1024 * g + 1024] for g in range(3)], axis=0)
    grad_out = jnp.concatenate([second[:, 1024 * g : 1024 * g + 1024] for g in (3, 4)], axis=0)
    gain_all = second[:18, 7168:7296].reshape(2304)
    return (
        output,
        grad_tokens,
        lax.dynamic_slice_in_dim(gain_all, shard * 256, 256),
        first[:, 6144:],
        second[:, 5120:6144],
        second[:, 6144:7168],
        lax.dynamic_slice_in_dim(gain_all, 2048 + shard * 32, 32),
        lax.dynamic_slice_in_dim(gain_all, 2176 + shard * 32, 32),
        grad_out,
        lax.dynamic_slice_in_dim(gain_all, 1024 + shard * 256, 256),
        first[:, :3072],
        first[:, 3072:6144],
        grad_down,
    )


def solution(mesh):
    axes = ("xl", "co", "z", "y", "xh")
    fine = Mesh(mesh.devices.reshape(2, 2, 4, 4, 2), axes)
    rows = P(axes, None)
    shard = P(("xl", "co"), None)
    vector = P(("xl", "co"))
    in_specs = (
        rows,
        P(axes),
        vector,
        shard,
        shard,
        shard,
        vector,
        vector,
        shard,
        vector,
        shard,
        shard,
        shard,
        rows,
    )
    out_specs = (
        rows,
        rows,
        vector,
        shard,
        shard,
        shard,
        vector,
        vector,
        shard,
        vector,
        shard,
        shard,
        shard,
    )
    return jax.shard_map(local, mesh=fine, in_specs=in_specs, out_specs=out_specs, check_vma=False)
```

```python
import jax
import jax.numpy as jnp
from jax import lax
from jax.experimental import pallas as pl
from jax.experimental.pallas import tpu as pltpu
from jax.sharding import Mesh
from jax.sharding import PartitionSpec as P

EPSILON = 1e-06
THETA = 1000000.0
HEAD = 128
ROWS = 128
CHUNK = 512
SCORE_SCALE = HEAD ** (-0.5)
LOG2_E = 1.4426950408889634
EXP_SCALE = SCORE_SCALE * LOG2_E
LOW = jnp.bfloat16
FEED_CUTS = ((0, 256), (1408, 1664), (256, 1408), (1664, 2816))
F32 = jnp.float32


def x_shift(value, step):
    pairs = []
    for x in range(4):
        to = (x + step) % 4
        pairs.append(((x % 2) * 2 + x // 2, (to % 2) * 2 + to // 2))
    return lax.ppermute(value, ("xl", "xh"), pairs)


def shift(value, axis, step):
    if axis == "x":
        return x_shift(value, step)
    return lax.ppermute(value, axis, [(i, (i + step) % 4) for i in range(4)])


def core_swap(value):
    return lax.ppermute(value, "co", [(0, 1), (1, 0)])


def place_on(axis):
    if axis == "x":
        return lax.axis_index("xh") * 2 + lax.axis_index("xl")
    return lax.axis_index(axis)


def pick(value, index, dim):
    return lax.dynamic_index_in_dim(value, index, dim, keepdims=False)


def send_parts(value, axis, dim):
    me = place_on(axis)
    got = [shift(pick(value, (me + step) % 4, dim), axis, step) for step in (1, 3, 2)]
    return [pick(value, me, dim)] + got


def add_parts(parts):
    total = parts[0].astype(F32)
    for part in parts[1:]:
        total = total + part.astype(F32)
    return total.astype(LOW)


def reduce_over(value, axis, dim):
    return add_parts(send_parts(value, axis, dim))


def gather_over(value, axis, dim, dtype=LOW):
    me = place_on(axis)
    shape = value.shape[:dim] + (4,) + value.shape[dim:]
    out = jnp.zeros(shape, dtype)
    out = lax.dynamic_update_index_in_dim(out, value.astype(dtype), me, dim)
    for step in (1, 3, 2):
        got = shift(value, axis, step).astype(dtype)
        out = lax.dynamic_update_index_in_dim(out, got, (me - step) % 4, dim)
    return out


def both_ways(value, axis):
    before = shift(value, axis, 1)
    after = shift(value, axis, -1)
    across = (shift(before[:2], axis, 1), shift(after[2:], axis, -1))
    return [(value, 0, 0), (before, 1, 0), (after, 3, 0), (across[0], 2, 0), (across[1], 2, 2)]


def lay_out(parts, axis, columns):
    me = place_on(axis)
    width = columns[0][1] - columns[0][0]
    out = jnp.zeros((len(columns), 4, 4, 16, width), F32)
    for part, back, first in parts:
        owner = (me - back) % 4
        piece = jnp.stack([part[..., a:b] for a, b in columns]).astype(F32)
        if axis == "y":
            at, piece = (owner, first), piece[:, None]
        else:
            at, piece = (first, owner), piece[:, :, None]
        out = lax.dynamic_update_slice(out, piece, (0, *at, 0, 0))
    return out.reshape(len(columns) * 256, width)


def exchange_y(value):
    return lax.all_to_all(value, "y", split_axis=0, concat_axis=0, tiled=True)


def send_first(first, second):
    first = exchange_y(first.reshape(4, 64, first.shape[-1]))
    return first, send_parts(second.reshape(4, 64, second.shape[-1]), "z", 0)


def add_first(first, second):
    return jnp.sum(first.astype(F32), axis=0).astype(LOW), add_parts(second)


def reduce_second(first, second):
    second = exchange_y(second.reshape(4, 16, second.shape[-1]))
    first = reduce_over(first.reshape(4, 16, first.shape[-1]), "z", 0)
    return first, jnp.sum(second.astype(F32), axis=0).astype(LOW)


def add_xh(part):
    other = lax.ppermute(part, "xh", [(0, 1), (1, 0)])
    return (part.astype(F32) + other.astype(F32)).astype(LOW)


def gather_weight(shard):
    half = shard.shape[0] // 2
    up = x_shift(shard[:half], 1)
    down = x_shift(shard[half:], -1)
    return [shard, up, down, core_swap(shard), core_swap(up), core_swap(down)]


def dot_t(left, right):
    return lax.dot_general(left, right, (((1,), (1,)), ((), ())), preferred_element_type=F32)


def dot_n(left, right):
    return lax.dot_general(left, right, (((1,), (0,)), ((), ())), preferred_element_type=F32)


def dot_r(left, right):
    return lax.dot_general(left, right, (((0,), (0,)), ((), ())), preferred_element_type=F32)


def whole(shape):
    return pl.BlockSpec(shape, lambda *_: (0,) * len(shape))


def per_block(shape):
    return pl.BlockSpec((1,) + shape, lambda i: (i,) + (0,) * len(shape))


def smem():
    return pl.BlockSpec(memory_space=pltpu.SMEM)


def anywhere():
    return pl.BlockSpec(memory_space=pl.ANY)


def shaped(shape, dtype):
    return pltpu.HBM(shape, dtype)


def held(arrays):
    return [pltpu.with_memory_space_constraint(array, pltpu.HBM) for array in arrays]


def fetch(shards, pieces, full, sems):
    rows = pieces[0].shape[0]
    half = rows // 2
    at = [
        shards[0] * rows,
        shards[1] * rows,
        shards[1] * rows + half,
        shards[2] * rows,
        shards[3] * rows,
        shards[3] * rows + half,
    ]
    copies = []
    for n, (piece, where) in enumerate(zip(pieces, at)):
        where = pl.multiple_of(where, half)
        copy = pltpu.make_async_copy(
            piece, full.at[pl.ds(where, piece.shape[0]), :], sems.at[n]
        )
        copy.start()
        copies.append(copy)
    return copies


def fetch_feed(shards, pieces, w_out, w_gu, w_down, sems):
    groups = ([], [], [], [], [])
    n = 0
    for s in range(4):
        for part, (first, end) in enumerate(FEED_CUTS):
            piece = pieces[len(FEED_CUTS) * s + part]
            at = 0
            while first + at < end:
                block, off = divmod(first + at, 256)
                size = min(256 - off, end - first - at)
                src = piece.at[pl.ds(at, size), :]
                if block < 6:
                    where = pl.multiple_of(shards[s] * 256 + off, 128)
                    dst = w_gu.at[pl.ds(where, size), pl.ds(block * 1024, 1024)]
                    group = (1, 3, 4)[block % 3]
                elif block < 8:
                    where = pl.multiple_of(shards[s] * 512 + (block - 6) * 256 + off, 128)
                    dst = w_out.at[pl.ds(where, size), :]
                    group = 0
                else:
                    where = pl.multiple_of(shards[s] * 768 + (block - 8) * 256 + off, 128)
                    dst = w_down.at[pl.ds(where, size), :]
                    group = 2
                groups[group].append(pltpu.make_async_copy(src, dst, sems.at[n]))
                n += 1
                at += size
    for group in groups:
        for copy in group:
            copy.start()
    return groups


def settle(copies):
    for copy in copies:
        copy.wait()


def scale_of(value):
    return lax.rsqrt(jnp.mean(value * value, axis=-1, keepdims=True) + EPSILON)


def turn(value):
    return jnp.concatenate([value[:, HEAD // 2 :], value[:, : HEAD // 2]], axis=1)


def project_kernel(
    shards, x_ref, gain_ref, gq_ref, gk_ref, cos_ref, sin_ref, *rest
):
    pieces, (q_ref, kv_ref, raw_ref, left_ref, w, sems) = rest[:6], rest[6:]
    copies = fetch(shards, pieces, w, sems)
    x = x_ref[...].astype(F32)
    h = (x * scale_of(x) * gain_ref[...]).astype(LOW)
    for f in range(4):
        left_ref[f // 2, f % 2] = h[:, f * 256 : f * 256 + 256]
    cosine, sine = cos_ref[...], sin_ref[...]
    settle(copies)
    for tile in range(8):
        product = dot_n(h, w[:, tile * 512 : tile * 512 + 512])
        for part in range(4):
            n = tile * 4 + part
            raw = product[:, part * HEAD : part * HEAD + HEAD]
            if n >= 24:
                kv_ref[n - 24, 1] = raw.astype(LOW)
                continue
            raw_ref[n] = raw
            gain = gq_ref[...] if n < 16 else gk_ref[...]
            u = raw * scale_of(raw) * gain
            u = (u * cosine + turn(u) * sine).astype(LOW)
            if n < 16:
                q_ref[n] = u
            else:
                kv_ref[n - 16, 0] = u


def project(shards, x, gain, gain_q, gain_k, cosine, sine, pieces):
    return pl.pallas_call(
        project_kernel,
        in_specs=[smem()] + [pl.BlockSpec(memory_space=pltpu.VMEM)] * 6 + [anywhere()] * 6,
        out_shape=[
            shaped((16, ROWS, HEAD), LOW),
            shaped((8, 2, ROWS, HEAD), LOW),
            shaped((24, ROWS, HEAD), F32),
            shaped((2, 2, ROWS, 256), LOW),
        ],
        scratch_shapes=[pltpu.VMEM((1024, 4096), LOW), pltpu.SemaphoreType.DMA((6,))],
        compiler_params=pltpu.CompilerParams(vmem_limit_bytes=32 * 2**20),
        cost_estimate=pl.CostEstimate(
            flops=10**9, bytes_accessed=12 * 2**20, transcendentals=10**4
        ),
        name="project",
    )(shards, x, gain, gain_q, gain_k, cosine, sine, *held(pieces))


def feed_kernel(shards, o_ref, x_ref, cot_ref, gain_ref, *rest):
    (y_ref, mid_ref, left_ref, right_ref, do_ref, term_ref) = rest[16:22]
    (w_out, w_gu, w_down, merged, sems) = rest[22:]
    out_copies, gu_copies, down_copies, gu_next, gu_last = fetch_feed(shards, rest[:16], w_out, w_gu, w_down, sems)
    for n in range(16):
        merged[:, n * HEAD : n * HEAD + HEAD] = o_ref[n]
    cot = cot_ref[...]
    gain = gain_ref[...]
    settle(out_copies)
    middle = x_ref[...].astype(F32) + dot_n(merged[...], w_out[...])
    scale = scale_of(middle)
    normal = middle * scale
    h = (normal * gain).astype(LOW)
    for f in range(4):
        left_ref[f // 2, f % 2, 0] = h[:, f * 256 : f * 256 + 256]
    settle(gu_copies)
    settle(down_copies)
    total = middle
    dh = jnp.zeros_like(middle)
    for tile in range(6):
        if tile == 2:
            settle(gu_next)
        if tile == 4:
            settle(gu_last)
        at = tile * 512
        gate = dot_n(h, w_gu[:, at : at + 512])
        up = dot_n(h, w_gu[:, 3072 + at : 3072 + at + 512])
        sg = 1.0 / (1.0 + jnp.exp(-gate))
        swish = gate * sg
        hidden = (swish * up).astype(LOW)
        for part in range(2):
            f, g = divmod(tile * 2 + part, 3)
            left_ref[f // 2, f % 2, 1 + g] = hidden[:, part * 256 : part * 256 + 256]
        total = total + dot_n(hidden, w_down[at : at + 512, :])
        dhidden = dot_t(cot, w_down[at : at + 512, :])
        dgate = (dhidden * up * sg * (1.0 + gate * (1.0 - sg))).astype(LOW)
        dup = (dhidden * swish).astype(LOW)
        right_ref[:, at : at + 512] = dgate
        right_ref[:, 3072 + at : 3072 + at + 512] = dup
        dh = dh + dot_t(dgate, w_gu[:, at : at + 512])
        dh = dh + dot_t(dup, w_gu[:, 3072 + at : 3072 + at + 512])
    y_ref[...] = total.astype(LOW)
    term_ref[...] = jnp.sum(dh * normal, axis=0, keepdims=True)
    dn = dh * gain
    dmid = cot.astype(F32) + scale * (dn - normal * jnp.mean(dn * normal, axis=-1, keepdims=True))
    mid_ref[...] = dmid
    da = dmid.astype(LOW)
    right_ref[:, 6144:] = da
    for tile in range(4):
        back = dot_t(da, w_out[tile * 512 : tile * 512 + 512, :]).astype(LOW)
        for part in range(4):
            do_ref[tile * 4 + part] = back[:, part * HEAD : part * HEAD + HEAD]


def feed(shards, o, x, cot, gain, pieces):
    return pl.pallas_call(
        feed_kernel,
        in_specs=[smem()] + [pl.BlockSpec(memory_space=pltpu.VMEM)] * 4 + [anywhere()] * 16,
        out_shape=[
            shaped((ROWS, 1024), LOW),
            shaped((ROWS, 1024), F32),
            shaped((2, 2, 4, ROWS, 256), LOW),
            shaped((ROWS, 7168), LOW),
            shaped((16, ROWS, HEAD), LOW),
            shaped((1, 1024), F32),
        ],
        scratch_shapes=[
            pltpu.VMEM((2048, 1024), LOW),
            pltpu.VMEM((1024, 6144), LOW),
            pltpu.VMEM((3072, 1024), LOW),
            pltpu.VMEM((ROWS, 2048), LOW),
            pltpu.SemaphoreType.DMA((52,)),
        ],
        compiler_params=pltpu.CompilerParams(vmem_limit_bytes=48 * 2**20),
        cost_estimate=pl.CostEstimate(
            flops=7 * 10**9, bytes_accessed=30 * 2**20, transcendentals=10**6
        ),
        name="feed",
    )(shards, *held([o, x, cot, gain, *pieces]))


def columns_of(value):
    return value.astype(F32).T.astype(LOW)


def lay_left(left_t, part, left, turned):
    columns = columns_of(left)
    at = slice(part * ROWS, part * ROWS + ROWS)
    if not turned:
        left_t[:, at] = columns
        return
    for y in range(4):
        for z in range(4):
            to, row = (z * 4 + y) * 16, (y * 4 + z) * 16
            left_t[to : to + 16, at] = columns[row : row + 16, :]


def weight_kernel(*refs):
    lefts, heads, rights, cots = refs[:4], refs[4:8], refs[8:12], refs[12:16]
    first_ref, second_ref, left_t, right = refs[16:]
    t = pl.program_id(0)

    @pl.when(t == 0)
    def _():
        for part in range(4):
            lay_left(left_t, part, lefts[part][0], False)

    @pl.when((t >= 6) & (t < 9))
    def _():
        for part in range(4):
            lay_left(left_t, part, lefts[part][0], True)

    for group in range(2):

        @pl.when(t == 9 + group)
        def _():
            for part in range(4):
                pair = [heads[part][2 * group], heads[part][2 * group + 1]]
                lay_left(left_t, part, jnp.concatenate(pair, axis=1), True)

    @pl.when((t < 6) | (t >= 9))
    def _():
        for part in range(4):
            right[part * ROWS : part * ROWS + ROWS, :] = rights[part][...]

    @pl.when(t == 6)
    def _():
        for part in range(4):
            right[part * ROWS : part * ROWS + ROWS, :] = cots[part][...]

    @pl.when(t < 6)
    def _():
        first_ref[...] = dot_n(left_t[...], right[...]).astype(LOW)

    @pl.when(t >= 6)
    def _():
        second_ref[...] = dot_n(left_t[...], right[...]).astype(LOW)


def feed_weight_grads(lefts, heads, rights, cots):
    left = pl.BlockSpec((1, ROWS, 256), lambda t: (jnp.clip(t - 5, 0, 3), 0, 0))
    wide = pl.BlockSpec((ROWS, 1024), lambda t: (0, jnp.where(t < 6, t, jnp.where(t < 9, 5, 6))))
    return pl.pallas_call(
        weight_kernel,
        grid=(11,),
        in_specs=[left] * 4 + [whole((4, ROWS, HEAD))] * 4 + [wide] * 4 + [whole((ROWS, 1024))] * 4,
        out_specs=[
            pl.BlockSpec((256, 1024), lambda t: (0, jnp.minimum(t, 5))),
            pl.BlockSpec((256, 1024), lambda t: (0, jnp.maximum(t - 6, 0))),
        ],
        out_shape=[shaped((256, 6144), LOW), shaped((256, 5120), LOW)],
        scratch_shapes=[pltpu.VMEM((256, 4 * ROWS), LOW), pltpu.VMEM((4 * ROWS, 1024), LOW)],
        compiler_params=pltpu.CompilerParams(vmem_limit_bytes=24 * 2**20),
        cost_estimate=pl.CostEstimate(
            flops=3 * 10**9, bytes_accessed=16 * 2**20, transcendentals=0
        ),
        name="feed_weight_grads",
    )(*held([*lefts, *heads, *rights, *cots]))


def attention_weight_kernel(*refs):
    lefts, rights, (term_ref, first_ref, second_ref, left_t, right) = refs[:4], refs[4:8], refs[8:]
    t = pl.program_id(0)

    @pl.when(t == 0)
    def _():
        for part in range(4):
            lay_left(left_t, part, lefts[part][...], False)

    @pl.when(t == 4)
    def _():
        for part in range(4):
            lay_left(left_t, part, lefts[part][...], True)

    for part in range(4):
        right[part * ROWS : part * ROWS + ROWS, :] = rights[part][...]

    @pl.when(t < 4)
    def _():
        first_ref[...] = dot_n(left_t[...], right[...]).astype(LOW)

    @pl.when((t >= 4) & (t < 8))
    def _():
        second_ref[...] = dot_n(left_t[...], right[...]).astype(LOW)

    @pl.when(t == 8)
    def _():
        second_ref[...] = jnp.zeros_like(second_ref)
        for z in range(2):
            at = z * 64
            second_ref[at : at + 16, :HEAD] = term_ref[z * 16 : z * 16 + 16, :].astype(LOW)


def attention_weight_grads(lefts, rights, terms):
    wide = pl.BlockSpec((ROWS, 512), lambda t: (0, jnp.minimum(t, 7)))
    return pl.pallas_call(
        attention_weight_kernel,
        grid=(9,),
        in_specs=[whole((ROWS, 256))] * 4 + [wide] * 4 + [whole((32, HEAD))],
        out_specs=[
            pl.BlockSpec((256, 512), lambda t: (0, jnp.minimum(t, 3))),
            pl.BlockSpec((256, 512), lambda t: (0, jnp.maximum(t - 4, 0))),
        ],
        out_shape=[shaped((256, 2048), LOW), shaped((256, 2560), LOW)],
        scratch_shapes=[pltpu.VMEM((256, 4 * ROWS), LOW), pltpu.VMEM((4 * ROWS, 512), LOW)],
        compiler_params=pltpu.CompilerParams(vmem_limit_bytes=16 * 2**20),
        cost_estimate=pl.CostEstimate(flops=10**9, bytes_accessed=6 * 2**20, transcendentals=0),
        name="attention_weight_grads",
    )(*held([*lefts, *rights, terms]))


def raw_grads_kernel(back_ref, raw_ref, gq_ref, gk_ref, cos_ref, sin_ref, right_ref, term_ref):
    cosine, sine = cos_ref[...], sin_ref[...]
    for heads, first, place, gain_ref in ((16, 0, 0, gq_ref), (8, 16, HEAD, gk_ref)):
        gain = gain_ref[...]
        term = jnp.zeros((ROWS, HEAD), F32)
        for n in range(heads):
            grad = back_ref[n // 2, n % 2] if first == 0 else back_ref[n, 2]
            grad = grad.astype(F32)
            raw = raw_ref[first + n]
            scale = scale_of(raw)
            unit = raw * scale
            grad = grad * cosine - turn(grad) * sine
            term = term + grad * unit
            grad = grad * gain
            grad = scale * (grad - unit * jnp.mean(grad * unit, axis=-1, keepdims=True))
            at = (first + n) * HEAD
            right_ref[:, at : at + HEAD] = grad.astype(LOW)
        term_ref[:, place : place + HEAD] = jnp.sum(term, axis=0, keepdims=True)
    for n in range(8):
        at = 3072 + n * HEAD
        right_ref[:, at : at + HEAD] = back_ref[n, 3]


def raw_grads(back, raw, gain_q, gain_k, cosine, sine):
    return pl.pallas_call(
        raw_grads_kernel,
        in_specs=[pl.BlockSpec(memory_space=pltpu.VMEM)] * 6,
        out_shape=[shaped((ROWS, 4096), LOW), shaped((1, 2 * HEAD), F32)],
        compiler_params=pltpu.CompilerParams(vmem_limit_bytes=16 * 2**20),
        cost_estimate=pl.CostEstimate(
            flops=10**7, bytes_accessed=4 * 2**20, transcendentals=10**4
        ),
        name="raw_grads",
    )(*held([back, raw, gain_q, gain_k, cosine, sine]))


def token_grads_kernel(shards, right_ref, x_ref, mid_ref, gain_ref, *rest):
    pieces, (grad_ref, term_ref, w, sems) = rest[:6], rest[6:]
    copies = fetch(shards, pieces, w, sems)
    x = x_ref[...].astype(F32)
    scale = scale_of(x)
    normal = x * scale
    settle(copies)
    dh = dot_t(right_ref[...], w[...])
    term_ref[...] = jnp.sum(dh * normal, axis=0, keepdims=True)
    dn = dh * gain_ref[...]
    grad_ref[...] = mid_ref[...] + scale * (
        dn - normal * jnp.mean(dn * normal, axis=-1, keepdims=True)
    )


def token_grads(shards, right, x, mid, gain, pieces):
    return pl.pallas_call(
        token_grads_kernel,
        in_specs=[smem()] + [pl.BlockSpec(memory_space=pltpu.VMEM)] * 4 + [anywhere()] * 6,
        out_shape=[shaped((ROWS, 1024), F32), shaped((1, 1024), F32)],
        scratch_shapes=[pltpu.VMEM((1024, 4096), LOW), pltpu.SemaphoreType.DMA((6,))],
        compiler_params=pltpu.CompilerParams(vmem_limit_bytes=32 * 2**20),
        cost_estimate=pl.CostEstimate(
            flops=10**9, bytes_accessed=12 * 2**20, transcendentals=10**4
        ),
        name="token_grads",
    )(shards, *held([right, x, mid, gain, *pieces]))


def visible(first_key, query_block, start):
    key = first_key + lax.broadcasted_iota(jnp.int32, (CHUNK, 2 * ROWS), 0)
    query = query_block * ROWS + (lax.broadcasted_iota(jnp.int32, (CHUNK, 2 * ROWS), 1) & (ROWS - 1))
    return (key <= query) & ((key >= start) | (query < start))


def block_of(info):
    i = pl.program_id(0)
    return (i // 2) * 8 + info[1] * 2 + i % 2


def forward_kernel(info, q_ref, kv0, kv1, kv2, kv3, o_ref, ot_ref, l_ref, k_ref, v_ref, vt):
    block = block_of(info)
    start = info[0]
    last = block // (CHUNK // ROWS)

    @pl.when(pl.program_id(0) == 0)
    def _():
        for back, piece in enumerate((kv0, kv1, kv2, kv3)):
            owner = lax.rem(info[1] + 4 - back, 4)
            for z in range(4):
                at = pl.ds(pl.multiple_of((z * 4 + owner) * 256, 256), 256)
                k_ref[at, :] = piece[2 * z : 2 * z + 2, 0].reshape(256, HEAD)
                v_ref[at, :] = piece[2 * z : 2 * z + 2, 1].reshape(256, HEAD)
        for c in range(vt.shape[0]):
            vt[c] = columns_of(v_ref[c * CHUNK : (c + 1) * CHUNK, :])

    q = q_ref[0]

    def step(c, carry, masked):
        total, mixed = carry
        keys = k_ref[pl.ds(pl.multiple_of(c * CHUNK, CHUNK), CHUNK), :]
        p = jnp.exp2(dot_t(keys, q) * EXP_SCALE)
        if masked:
            p = jnp.where(visible(c * CHUNK, block, start), p, 0.0)
        total = total + jnp.sum(p.reshape(CHUNK // 8, 8, 2 * ROWS), axis=0)
        mixed = mixed + dot_n(vt[c], p.astype(LOW))
        return total, mixed

    carry = (jnp.zeros((8, 2 * ROWS), F32), jnp.zeros((HEAD, 2 * ROWS), F32))
    carry = step(last, carry, True)
    carry = lax.fori_loop(0, jnp.minimum(last, 1), lambda c, x: step(c, x, True), carry)
    pairs = jnp.maximum(last - 1, 0) // 2
    carry = lax.fori_loop(
        0, pairs, lambda n, x: step(2 * n + 2, step(2 * n + 1, x, False), False), carry
    )
    carry = lax.fori_loop(2 * pairs + 1, last, lambda c, x: step(c, x, False), carry)
    total = jnp.sum(carry[0], axis=0, keepdims=True)
    mixed = carry[1] / total
    ot_ref[0] = mixed
    o_ref[0] = mixed.T.astype(LOW)
    l_ref[0] = jnp.log2(total)


def backward_kernel(
    info, q_ref, do_ref, ot_ref, l_ref, k_ref, v_ref, dq_ref, dkv_ref, kt, dk_acc, dv_acc
):
    i = pl.program_id(0)
    block = block_of(info)
    start = info[0]
    q = q_ref[0]
    do = do_ref[0]
    last = block // (CHUNK // ROWS)

    @pl.when(i == 0)
    def _():
        dk_acc[...] = jnp.zeros_like(dk_acc)
        dv_acc[...] = jnp.zeros_like(dv_acc)
        for c in range(kt.shape[0]):
            kt[c] = columns_of(k_ref[c * CHUNK : (c + 1) * CHUNK, :])

    delta = jnp.sum(do.astype(F32).T * ot_ref[0], axis=0, keepdims=True)
    logs = l_ref[0]

    def step(c, dqt, masked):
        at = pl.ds(pl.multiple_of(c * CHUNK, CHUNK), CHUNK)
        p = jnp.exp2(dot_t(k_ref[at, :], q) * EXP_SCALE - logs)
        if masked:
            p = jnp.where(visible(c * CHUNK, block, start), p, 0.0)
        dp = dot_t(v_ref[at, :], do)
        ds = (p * (dp - delta)).astype(LOW)
        dv_acc[at, :] += dot_n(p.astype(LOW), do)
        dk_acc[at, :] += dot_n(ds, q)
        return dqt + dot_n(kt[c], ds)

    dqt = step(last, jnp.zeros((HEAD, 2 * ROWS), F32), True)
    dqt = lax.fori_loop(0, jnp.minimum(last, 1), lambda c, x: step(c, x, True), dqt)
    pairs = jnp.maximum(last - 1, 0) // 2
    dqt = lax.fori_loop(
        0, pairs, lambda n, x: step(2 * n + 2, step(2 * n + 1, x, False), False), dqt
    )
    dqt = lax.fori_loop(2 * pairs + 1, last, lambda c, x: step(c, x, False), dqt)
    dq_ref[0] = (dqt * SCORE_SCALE).T.astype(LOW)

    @pl.when(i == pl.num_programs(0) - 1)
    def _():
        for z in range(4):
            for y in range(4):
                at = (z * 4 + y) * 256
                part = (dk_acc[at : at + 256, :] * SCORE_SCALE).astype(LOW)
                dkv_ref[y, 2 * z : 2 * z + 2, 0] = part.reshape(2, ROWS, HEAD)
                part = dv_acc[at : at + 256, :].astype(LOW)
                dkv_ref[y, 2 * z : 2 * z + 2, 1] = part.reshape(2, ROWS, HEAD)


def attention_forward(info, q, pieces):
    length = 32 * ROWS
    return pl.pallas_call(
        forward_kernel,
        grid=(8,),
        in_specs=[smem(), per_block((2 * ROWS, HEAD))] + [whole((8, 2, ROWS, HEAD))] * 4,
        out_specs=[
            per_block((2 * ROWS, HEAD)),
            per_block((HEAD, 2 * ROWS)),
            per_block((1, 2 * ROWS)),
            whole((length, HEAD)),
            whole((length, HEAD)),
        ],
        out_shape=[
            shaped((8, 2 * ROWS, HEAD), LOW),
            shaped((8, HEAD, 2 * ROWS), F32),
            shaped((8, 1, 2 * ROWS), F32),
            shaped((length, HEAD), LOW),
            shaped((length, HEAD), LOW),
        ],
        scratch_shapes=[pltpu.VMEM((length // CHUNK, HEAD, CHUNK), LOW)],
        compiler_params=pltpu.CompilerParams(vmem_limit_bytes=32 * 2**20),
        cost_estimate=pl.CostEstimate(
            flops=3 * 10**9, bytes_accessed=7 * 2**20, transcendentals=5 * 10**6
        ),
        name="attention_forward",
    )(info, *held([q, *pieces]))


def attention_backward(info, q, do, ot, logs, k, v):
    length = k.shape[0]
    return pl.pallas_call(
        backward_kernel,
        grid=(8,),
        in_specs=[
            smem(),
            per_block((2 * ROWS, HEAD)),
            per_block((2 * ROWS, HEAD)),
            per_block((HEAD, 2 * ROWS)),
            per_block((1, 2 * ROWS)),
            whole((length, HEAD)),
            whole((length, HEAD)),
        ],
        out_specs=[per_block((2 * ROWS, HEAD)), whole((4, 8, 2, ROWS, HEAD))],
        out_shape=[
            shaped((8, 2 * ROWS, HEAD), LOW),
            shaped((4, 8, 2, ROWS, HEAD), LOW),
        ],
        scratch_shapes=[
            pltpu.VMEM((length // CHUNK, HEAD, CHUNK), LOW),
            pltpu.VMEM((length, HEAD), F32),
            pltpu.VMEM((length, HEAD), F32),
        ],
        compiler_params=pltpu.CompilerParams(vmem_limit_bytes=32 * 2**20),
        cost_estimate=pl.CostEstimate(
            flops=8 * 10**9, bytes_accessed=10 * 2**20, transcendentals=5 * 10**6
        ),
        name="attention_backward",
    )(info, *held([q, do, ot, logs, k, v]))


def rotary_tables(where_at):
    half = HEAD // 2
    frequency = THETA ** (-(jnp.arange(half, dtype=F32) * 2.0) / HEAD)
    angles = where_at.astype(F32)[:, None] * frequency[None, :]
    cosine, sine = jnp.cos(angles), jnp.sin(angles)
    return jnp.concatenate([cosine, cosine], axis=-1), jnp.concatenate([-sine, sine], axis=-1)


def exchange_heads(value):
    return lax.all_to_all(value, ("z", "xh"), split_axis=0, concat_axis=0, tiled=True)


def pack_feed(w_gate, w_up, w_out, w_down):
    blocks = [w[:, n * 1024 : n * 1024 + 1024] for w in (w_gate, w_up) for n in range(3)]
    blocks += [w[n : n + 256] for w in (w_out, w_down) for n in range(0, w.shape[0], 256)]
    parts = []
    for first, end in FEED_CUTS:
        rows = []
        while first < end:
            block, off = divmod(first, 256)
            size = min(256 - off, end - first)
            rows.append(blocks[block][off : off + size])
            first += size
        parts.append(jnp.concatenate(rows, axis=0))
    return parts


def spread(value, across):
    return [value, core_swap(value), across, core_swap(across)]


def spread_columns(here, across, co):
    return [
        pick(here, co, 0),
        core_swap(pick(here, 1 - co, 0)),
        pick(across, co, 0),
        core_swap(pick(across, 1 - co, 0)),
    ]


def x_pair(value):
    return lax.ppermute(value, "xl", [(0, 1), (1, 0)])


def local(
    tokens,
    positions,
    attn_gain,
    w_query,
    w_key,
    w_value,
    query_gain,
    key_gain,
    w_out,
    ffn_gain,
    w_gate,
    w_up,
    w_down,
    cotangent,
):
    xl = lax.axis_index("xl")
    co = lax.axis_index("co")
    y = lax.axis_index("y")
    block = lax.axis_index("z") * 8 + y * 2 + lax.axis_index("xh")
    shard = xl * 2 + co
    shards = jnp.stack([shard, 2 * (1 - xl) + co, 2 * xl + 1 - co, 2 * (1 - xl) + 1 - co])
    shards = shards.astype(jnp.int32)
    cots = spread(cotangent, x_pair(cotangent))


    qkv_pieces = gather_weight(jnp.concatenate([w_query, w_key, w_value], axis=1))

    gains = jnp.concatenate([attn_gain, ffn_gain, query_gain, key_gain])
    gains = jnp.concatenate([gains, jnp.zeros((1024 - 576,), LOW)]).reshape(1, 8, 128)
    pair = jnp.concatenate([gains, x_pair(gains)], axis=0)
    pair = jnp.where(xl == 0, pair, pair[::-1])
    swapped = core_swap(pair)
    quad = jnp.where(co == 0, jnp.stack([pair, swapped], 1), jnp.stack([swapped, pair], 1))
    quad = quad.reshape(4, 1024).astype(F32)
    gain_one = quad[:, :256].reshape(1, 1024)
    gain_two = quad[:, 256:512].reshape(1, 1024)
    gain_query = quad[:, 512:544].reshape(1, 128)
    gain_key = quad[:, 544:576].reshape(1, 128)

    packed = pack_feed(w_gate, w_up, w_out, w_down)
    feed_across = [x_shift(packed[0], 1), x_shift(packed[1], -1)]

    start = block * ROWS + ROWS - 1 - positions[ROWS - 1]
    info = jnp.stack([start, y]).astype(jnp.int32)
    cosine, sine = rotary_tables(positions)
    query, kv_send, raw, left_one = project(
        shards, tokens, gain_one, gain_query, gain_key, cosine, sine, qkv_pieces
    )

    heads_send = jnp.concatenate([query.reshape(8, 2, ROWS, HEAD), kv_send], axis=1)
    heads_send, feed_across[0], feed_across[1] = lax.optimization_barrier(
        (heads_send, feed_across[0], feed_across[1])
    )
    heads = exchange_heads(heads_send)
    heads, packed[2], packed[3] = lax.optimization_barrier((heads, packed[2], packed[3]))
    kv = heads[:, 2:]
    q_all = heads[:, :2].reshape(8, 2 * ROWS, HEAD)
    kv_pieces = [kv, shift(kv, "y", 1), shift(kv, "y", 2), shift(kv, "y", 3)]
    feed_across += [x_shift(packed[2], 1), x_shift(packed[3], -1)]
    o_send, mixed_t, logs, k_all, v_all = attention_forward(info, q_all, kv_pieces)
    o_send, feed_across[2], feed_across[3] = lax.optimization_barrier(
        (o_send, feed_across[2], feed_across[3])
    )
    feed_pieces = packed + feed_across
    feed_pieces = feed_pieces + [core_swap(piece) for piece in feed_pieces]
    merged = exchange_heads(o_send).reshape(16, ROWS, HEAD)

    output, grad_middle, lefts, right, grad_merged, gain_two_term = feed(
        shards, merged, tokens, cotangent, gain_two, feed_pieces
    )

    do_all = exchange_heads(grad_merged.reshape(8, 2 * ROWS, HEAD))
    left_parts = spread_columns(pick(left_one, xl, 0), x_pair(pick(left_one, 1 - xl, 0)), co)
    head_parts = merged.reshape(2, 2, 4, ROWS, HEAD)
    head_parts = spread_columns(pick(head_parts, xl, 0), x_pair(pick(head_parts, 1 - xl, 0)), co)
    do_all, left_parts, head_parts, cots = lax.optimization_barrier(
        (do_all, left_parts, head_parts, cots)
    )
    right_across = x_pair(right)
    lefts_across = x_pair(pick(lefts, 1 - xl, 0))

    dq_all, dkv_all = attention_backward(info, q_all, do_all, mixed_t, logs, k_all, v_all)
    dkv = reduce_over(dkv_all, "y", 0)
    back = jnp.concatenate([dq_all.reshape(8, 2, ROWS, HEAD), dkv], axis=1)
    back, right_across, lefts_across = lax.optimization_barrier((back, right_across, lefts_across))
    back = exchange_heads(back)
    feed_part = feed_weight_grads(
        spread_columns(pick(lefts, xl, 0), lefts_across, co),
        head_parts,
        spread(right, right_across),
        cots,
    )
    back, feed_part = lax.optimization_barrier((back, feed_part))
    feed_first = exchange_y(feed_part[0].reshape(4, 64, 6144))
    feed_second = lax.psum_scatter(feed_part[1], "z", scatter_dimension=0, tiled=True)

    attention_grads, head_terms = raw_grads(back, raw, gain_query, gain_key, cosine, sine)
    attention_across = x_pair(attention_grads)
    grad_tokens, gain_one_term = token_grads(
        shards, attention_grads, tokens, grad_middle, gain_one, qkv_pieces
    )
    terms = jnp.concatenate([gain_one_term, gain_two_term, head_terms], axis=1)
    terms = jnp.pad(terms.reshape(18, 128), ((0, 14), (0, 0)))
    terms = terms + core_swap(terms)
    terms = terms + x_pair(terms)
    attention_across, terms = lax.optimization_barrier((attention_across, terms))
    attention_part = attention_weight_grads(
        left_parts, spread(attention_grads, attention_across), terms
    )
    attention_part, feed_first, feed_second = lax.optimization_barrier(
        (attention_part, feed_first, feed_second)
    )
    attention_parts = send_first(*attention_part)
    feed_first = jnp.sum(feed_first.astype(F32), axis=0).astype(LOW)
    first, second = add_first(*attention_parts)
    first, second = reduce_second(
        jnp.concatenate([feed_first, first], axis=-1),
        jnp.concatenate([feed_second, second], axis=-1),
    )
    both = add_xh(jnp.concatenate([first, second], axis=-1))
    first = gather_over(both[:, :8192], "z", 0)
    second = gather_over(both[:, 8192:], "y", 0)
    first = both_ways(first, "y")
    second = both_ways(second, "z")
    gain_all = lay_out(second, "z", [(7168, 7296)])[:18].reshape(2304)
    return (
        output,
        grad_tokens,
        lax.dynamic_slice_in_dim(gain_all, shard * 256, 256),
        lay_out(first, "y", [(6144, 8192)]),
        lay_out(second, "z", [(5120, 6144)]),
        lay_out(second, "z", [(6144, 7168)]),
        lax.dynamic_slice_in_dim(gain_all, 2048 + shard * 32, 32),
        lax.dynamic_slice_in_dim(gain_all, 2176 + shard * 32, 32),
        lay_out(second, "z", [(3072, 4096), (4096, 5120)]),
        lax.dynamic_slice_in_dim(gain_all, 1024 + shard * 256, 256),
        lay_out(first, "y", [(0, 3072)]),
        lay_out(first, "y", [(3072, 6144)]),
        lay_out(second, "z", [(0, 1024), (1024, 2048), (2048, 3072)]),
    )


def solution(mesh):
    axes = ("xl", "co", "z", "y", "xh")
    fine = Mesh(mesh.devices.reshape(2, 2, 4, 4, 2), axes)
    rows = P(axes, None)
    shard = P(("xl", "co"), None)
    vector = P(("xl", "co"))
    in_specs = (
        rows,
        P(axes),
        vector,
        shard,
        shard,
        shard,
        vector,
        vector,
        shard,
        vector,
        shard,
        shard,
        shard,
        rows,
    )
    out_specs = (
        rows,
        rows,
        vector,
        shard,
        shard,
        shard,
        vector,
        vector,
        shard,
        vector,
        shard,
        shard,
        shard,
    )
    return jax.shard_map(local, mesh=fine, in_specs=in_specs, out_specs=out_specs, check_vma=False)
```

```python
import jax
import jax.numpy as jnp
from jax import lax
from jax.experimental import pallas as pl
from jax.experimental.pallas import tpu as pltpu
from jax.sharding import Mesh
from jax.sharding import PartitionSpec as P

EPSILON = 1e-06
THETA = 1000000.0
HEAD = 128
ROWS = 128
CHUNK = 512
SCORE_SCALE = HEAD ** (-0.5)
LOG2_E = 1.4426950408889634
EXP_SCALE = SCORE_SCALE * LOG2_E
LOW = jnp.bfloat16
FEED_CUTS = ((0, 256), (1408, 1664), (256, 1408), (1664, 2816))
F32 = jnp.float32


def x_shift(value, step):
    pairs = []
    for x in range(4):
        to = (x + step) % 4
        pairs.append(((x % 2) * 2 + x // 2, (to % 2) * 2 + to // 2))
    return lax.ppermute(value, ("xl", "xh"), pairs)


def shift(value, axis, step):
    if axis == "x":
        return x_shift(value, step)
    return lax.ppermute(value, axis, [(i, (i + step) % 4) for i in range(4)])


def core_swap(value):
    return lax.ppermute(value, "co", [(0, 1), (1, 0)])


def place_on(axis):
    if axis == "x":
        return lax.axis_index("xh") * 2 + lax.axis_index("xl")
    return lax.axis_index(axis)


def pick(value, index, dim):
    return lax.dynamic_index_in_dim(value, index, dim, keepdims=False)


def send_parts(value, axis, dim):
    me = place_on(axis)
    got = [shift(pick(value, (me + step) % 4, dim), axis, step) for step in (1, 3, 2)]
    return [pick(value, me, dim)] + got


def add_parts(parts):
    total = parts[0].astype(F32)
    for part in parts[1:]:
        total = total + part.astype(F32)
    return total.astype(LOW)


def reduce_over(value, axis, dim):
    return add_parts(send_parts(value, axis, dim))


def gather_over(value, axis, dim, dtype=LOW):
    me = place_on(axis)
    shape = value.shape[:dim] + (4,) + value.shape[dim:]
    out = jnp.zeros(shape, dtype)
    out = lax.dynamic_update_index_in_dim(out, value.astype(dtype), me, dim)
    for step in (1, 3, 2):
        got = shift(value, axis, step).astype(dtype)
        out = lax.dynamic_update_index_in_dim(out, got, (me - step) % 4, dim)
    return out


def both_ways(value, axis):
    before = shift(value, axis, 1)
    after = shift(value, axis, -1)
    across = (shift(before[:2], axis, 1), shift(after[2:], axis, -1))
    return [(value, 0, 0), (before, 1, 0), (after, 3, 0), (across[0], 2, 0), (across[1], 2, 2)]


def lay_out(parts, axis, columns):
    me = place_on(axis)
    width = columns[0][1] - columns[0][0]
    out = jnp.zeros((len(columns), 4, 4, 16, width), F32)
    for part, back, first in parts:
        owner = (me - back) % 4
        piece = jnp.stack([part[..., a:b] for a, b in columns]).astype(F32)
        if axis == "y":
            at, piece = (owner, first), piece[:, None]
        else:
            at, piece = (first, owner), piece[:, :, None]
        out = lax.dynamic_update_slice(out, piece, (0, *at, 0, 0))
    return out.reshape(len(columns) * 256, width)


def exchange_y(value):
    return lax.all_to_all(value, "y", split_axis=0, concat_axis=0, tiled=True)


def send_first(first, second):
    first = exchange_y(first.reshape(4, 64, first.shape[-1]))
    return first, send_parts(second.reshape(4, 64, second.shape[-1]), "z", 0)


def add_first(first, second):
    return jnp.sum(first.astype(F32), axis=0).astype(LOW), add_parts(second)


def reduce_second(first, second):
    second = exchange_y(second.reshape(4, 16, second.shape[-1]))
    first = reduce_over(first.reshape(4, 16, first.shape[-1]), "z", 0)
    return first, jnp.sum(second.astype(F32), axis=0).astype(LOW)


def add_xh(part):
    other = lax.ppermute(part, "xh", [(0, 1), (1, 0)])
    return (part.astype(F32) + other.astype(F32)).astype(LOW)


def gather_weight(shard):
    half = shard.shape[0] // 2
    up = x_shift(shard[:half], 1)
    down = x_shift(shard[half:], -1)
    return [shard, up, down, core_swap(shard), core_swap(up), core_swap(down)]


def dot_t(left, right):
    return lax.dot_general(left, right, (((1,), (1,)), ((), ())), preferred_element_type=F32)


def dot_n(left, right):
    return lax.dot_general(left, right, (((1,), (0,)), ((), ())), preferred_element_type=F32)


def dot_r(left, right):
    return lax.dot_general(left, right, (((0,), (0,)), ((), ())), preferred_element_type=F32)


def whole(shape):
    return pl.BlockSpec(shape, lambda *_: (0,) * len(shape))


def per_block(shape):
    return pl.BlockSpec((1,) + shape, lambda i: (i,) + (0,) * len(shape))


def smem():
    return pl.BlockSpec(memory_space=pltpu.SMEM)


def anywhere():
    return pl.BlockSpec(memory_space=pl.ANY)


def shaped(shape, dtype):
    return pltpu.HBM(shape, dtype)


def held(arrays):
    return [pltpu.with_memory_space_constraint(array, pltpu.HBM) for array in arrays]


def fetch(shards, pieces, full, sems):
    rows = pieces[0].shape[0]
    half = rows // 2
    at = [
        shards[0] * rows,
        shards[1] * rows,
        shards[1] * rows + half,
        shards[2] * rows,
        shards[3] * rows,
        shards[3] * rows + half,
    ]
    copies = []
    for n, (piece, where) in enumerate(zip(pieces, at)):
        where = pl.multiple_of(where, half)
        copy = pltpu.make_async_copy(
            piece, full.at[pl.ds(where, piece.shape[0]), :], sems.at[n]
        )
        copy.start()
        copies.append(copy)
    return copies


def fetch_feed(shards, pieces, w_out, w_gu, w_down, sems):
    groups = ([], [], [], [], [])
    n = 0
    for s in range(4):
        for part, (first, end) in enumerate(FEED_CUTS):
            piece = pieces[len(FEED_CUTS) * s + part]
            at = 0
            while first + at < end:
                block, off = divmod(first + at, 256)
                size = min(256 - off, end - first - at)
                src = piece.at[pl.ds(at, size), :]
                if block < 6:
                    where = pl.multiple_of(shards[s] * 256 + off, 128)
                    dst = w_gu.at[pl.ds(where, size), pl.ds(block * 1024, 1024)]
                    group = (1, 3, 4)[block % 3]
                elif block < 8:
                    where = pl.multiple_of(shards[s] * 512 + (block - 6) * 256 + off, 128)
                    dst = w_out.at[pl.ds(where, size), :]
                    group = 0
                else:
                    where = pl.multiple_of(shards[s] * 768 + (block - 8) * 256 + off, 128)
                    dst = w_down.at[pl.ds(where, size), :]
                    group = 2
                groups[group].append(pltpu.make_async_copy(src, dst, sems.at[n]))
                n += 1
                at += size
    for group in groups:
        for copy in group:
            copy.start()
    return groups


def settle(copies):
    for copy in copies:
        copy.wait()


def scale_of(value):
    return lax.rsqrt(jnp.mean(value * value, axis=-1, keepdims=True) + EPSILON)


def turn(value):
    return jnp.concatenate([value[:, HEAD // 2 :], value[:, : HEAD // 2]], axis=1)


def project_kernel(
    shards, x_ref, gain_ref, gq_ref, gk_ref, cos_ref, sin_ref, *rest
):
    pieces, (q_ref, kv_ref, raw_ref, left_ref, w, sems) = rest[:6], rest[6:]
    copies = fetch(shards, pieces, w, sems)
    x = x_ref[...].astype(F32)
    h = (x * scale_of(x) * gain_ref[...]).astype(LOW)
    for f in range(4):
        left_ref[f // 2, f % 2] = h[:, f * 256 : f * 256 + 256]
    cosine, sine = cos_ref[...], sin_ref[...]
    settle(copies)
    for tile in range(8):
        product = dot_n(h, w[:, tile * 512 : tile * 512 + 512])
        for part in range(4):
            n = tile * 4 + part
            raw = product[:, part * HEAD : part * HEAD + HEAD]
            if n >= 24:
                kv_ref[n - 24, 1] = raw.astype(LOW)
                continue
            raw_ref[n] = raw
            gain = gq_ref[...] if n < 16 else gk_ref[...]
            u = raw * scale_of(raw) * gain
            u = (u * cosine + turn(u) * sine).astype(LOW)
            if n < 16:
                q_ref[n] = u
            else:
                kv_ref[n - 16, 0] = u


def project(shards, x, gain, gain_q, gain_k, cosine, sine, pieces):
    return pl.pallas_call(
        project_kernel,
        in_specs=[smem()] + [pl.BlockSpec(memory_space=pltpu.VMEM)] * 6 + [anywhere()] * 6,
        out_shape=[
            shaped((16, ROWS, HEAD), LOW),
            shaped((8, 2, ROWS, HEAD), LOW),
            shaped((24, ROWS, HEAD), F32),
            shaped((2, 2, ROWS, 256), LOW),
        ],
        scratch_shapes=[pltpu.VMEM((1024, 4096), LOW), pltpu.SemaphoreType.DMA((6,))],
        compiler_params=pltpu.CompilerParams(vmem_limit_bytes=32 * 2**20),
        cost_estimate=pl.CostEstimate(
            flops=10**9, bytes_accessed=12 * 2**20, transcendentals=10**4
        ),
        name="project",
    )(shards, x, gain, gain_q, gain_k, cosine, sine, *pieces)


def feed_kernel(shards, o_ref, x_ref, cot_ref, gain_ref, *rest):
    (y_ref, mid_ref, left_ref, right_ref, do_ref, term_ref) = rest[16:22]
    (w_out, w_gu, w_down, merged, sems) = rest[22:]
    out_copies, gu_copies, down_copies, gu_next, gu_last = fetch_feed(shards, rest[:16], w_out, w_gu, w_down, sems)
    for n in range(16):
        merged[:, n * HEAD : n * HEAD + HEAD] = o_ref[n]
    cot = cot_ref[...]
    gain = gain_ref[...]
    settle(out_copies)
    middle = x_ref[...].astype(F32) + dot_n(merged[...], w_out[...])
    scale = scale_of(middle)
    normal = middle * scale
    h = (normal * gain).astype(LOW)
    for f in range(4):
        left_ref[f // 2, f % 2, 0] = h[:, f * 256 : f * 256 + 256]
    settle(gu_copies)
    settle(down_copies)
    total = middle
    dh = jnp.zeros_like(middle)
    for tile in range(6):
        if tile == 2:
            settle(gu_next)
        if tile == 4:
            settle(gu_last)
        at = tile * 512
        gate = dot_n(h, w_gu[:, at : at + 512])
        up = dot_n(h, w_gu[:, 3072 + at : 3072 + at + 512])
        sg = 1.0 / (1.0 + jnp.exp(-gate))
        swish = gate * sg
        hidden = (swish * up).astype(LOW)
        for part in range(2):
            f, g = divmod(tile * 2 + part, 3)
            left_ref[f // 2, f % 2, 1 + g] = hidden[:, part * 256 : part * 256 + 256]
        total = total + dot_n(hidden, w_down[at : at + 512, :])
        dhidden = dot_t(cot, w_down[at : at + 512, :])
        dgate = (dhidden * up * sg * (1.0 + gate * (1.0 - sg))).astype(LOW)
        dup = (dhidden * swish).astype(LOW)
        right_ref[:, at : at + 512] = dgate
        right_ref[:, 3072 + at : 3072 + at + 512] = dup
        dh = dh + dot_t(dgate, w_gu[:, at : at + 512])
        dh = dh + dot_t(dup, w_gu[:, 3072 + at : 3072 + at + 512])
    y_ref[...] = total.astype(LOW)
    term_ref[...] = jnp.sum(dh * normal, axis=0, keepdims=True)
    dn = dh * gain
    dmid = cot.astype(F32) + scale * (dn - normal * jnp.mean(dn * normal, axis=-1, keepdims=True))
    mid_ref[...] = dmid
    da = dmid.astype(LOW)
    right_ref[:, 6144:] = da
    for tile in range(4):
        back = dot_t(da, w_out[tile * 512 : tile * 512 + 512, :]).astype(LOW)
        for part in range(4):
            do_ref[tile * 4 + part] = back[:, part * HEAD : part * HEAD + HEAD]


def feed(shards, o, x, cot, gain, pieces):
    return pl.pallas_call(
        feed_kernel,
        in_specs=[smem()] + [pl.BlockSpec(memory_space=pltpu.VMEM)] * 4 + [anywhere()] * 16,
        out_shape=[
            shaped((ROWS, 1024), LOW),
            shaped((ROWS, 1024), F32),
            shaped((2, 2, 4, ROWS, 256), LOW),
            shaped((ROWS, 7168), LOW),
            shaped((16, ROWS, HEAD), LOW),
            shaped((1, 1024), F32),
        ],
        scratch_shapes=[
            pltpu.VMEM((2048, 1024), LOW),
            pltpu.VMEM((1024, 6144), LOW),
            pltpu.VMEM((3072, 1024), LOW),
            pltpu.VMEM((ROWS, 2048), LOW),
            pltpu.SemaphoreType.DMA((52,)),
        ],
        compiler_params=pltpu.CompilerParams(vmem_limit_bytes=48 * 2**20),
        cost_estimate=pl.CostEstimate(
            flops=7 * 10**9, bytes_accessed=30 * 2**20, transcendentals=10**6
        ),
        name="feed",
    )(shards, *held([o, x, cot, gain, *pieces]))


def columns_of(value):
    return value.astype(F32).T.astype(LOW)


def lay_left(left_t, part, left, turned):
    columns = columns_of(left)
    at = slice(part * ROWS, part * ROWS + ROWS)
    if not turned:
        left_t[:, at] = columns
        return
    for y in range(4):
        for z in range(4):
            to, row = (z * 4 + y) * 16, (y * 4 + z) * 16
            left_t[to : to + 16, at] = columns[row : row + 16, :]


def weight_kernel(*refs):
    lefts, heads, rights, cots = refs[:4], refs[4:8], refs[8:12], refs[12:16]
    first_ref, second_ref, left_t, right = refs[16:]
    t = pl.program_id(0)

    @pl.when(t == 0)
    def _():
        for part in range(4):
            lay_left(left_t, part, lefts[part][0], False)

    @pl.when((t >= 6) & (t < 9))
    def _():
        for part in range(4):
            lay_left(left_t, part, lefts[part][0], True)

    for group in range(2):

        @pl.when(t == 9 + group)
        def _():
            for part in range(4):
                pair = [heads[part][2 * group], heads[part][2 * group + 1]]
                lay_left(left_t, part, jnp.concatenate(pair, axis=1), True)

    @pl.when((t < 6) | (t >= 9))
    def _():
        for part in range(4):
            right[part * ROWS : part * ROWS + ROWS, :] = rights[part][...]

    @pl.when(t == 6)
    def _():
        for part in range(4):
            right[part * ROWS : part * ROWS + ROWS, :] = cots[part][...]

    @pl.when(t < 6)
    def _():
        first_ref[...] = dot_n(left_t[...], right[...]).astype(LOW)

    @pl.when(t >= 6)
    def _():
        second_ref[...] = dot_n(left_t[...], right[...]).astype(LOW)


def feed_weight_grads(lefts, heads, rights, cots):
    left = pl.BlockSpec((1, ROWS, 256), lambda t: (jnp.clip(t - 5, 0, 3), 0, 0))
    wide = pl.BlockSpec((ROWS, 1024), lambda t: (0, jnp.where(t < 6, t, jnp.where(t < 9, 5, 6))))
    return pl.pallas_call(
        weight_kernel,
        grid=(11,),
        in_specs=[left] * 4 + [whole((4, ROWS, HEAD))] * 4 + [wide] * 4 + [whole((ROWS, 1024))] * 4,
        out_specs=[
            pl.BlockSpec((256, 1024), lambda t: (0, jnp.minimum(t, 5))),
            pl.BlockSpec((256, 1024), lambda t: (0, jnp.maximum(t - 6, 0))),
        ],
        out_shape=[shaped((256, 6144), LOW), shaped((256, 5120), LOW)],
        scratch_shapes=[pltpu.VMEM((256, 4 * ROWS), LOW), pltpu.VMEM((4 * ROWS, 1024), LOW)],
        compiler_params=pltpu.CompilerParams(vmem_limit_bytes=24 * 2**20),
        cost_estimate=pl.CostEstimate(
            flops=3 * 10**9, bytes_accessed=16 * 2**20, transcendentals=0
        ),
        name="feed_weight_grads",
    )(*held([*lefts, *heads, *rights, *cots]))


def attention_weight_kernel(*refs):
    lefts, rights, (term_ref, first_ref, second_ref, left_t, right) = refs[:4], refs[4:8], refs[8:]
    t = pl.program_id(0)

    @pl.when(t == 0)
    def _():
        for part in range(4):
            lay_left(left_t, part, lefts[part][...], False)

    @pl.when(t == 4)
    def _():
        for part in range(4):
            lay_left(left_t, part, lefts[part][...], True)

    for part in range(4):
        right[part * ROWS : part * ROWS + ROWS, :] = rights[part][...]

    @pl.when(t < 4)
    def _():
        first_ref[...] = dot_n(left_t[...], right[...]).astype(LOW)

    @pl.when((t >= 4) & (t < 8))
    def _():
        second_ref[...] = dot_n(left_t[...], right[...]).astype(LOW)

    @pl.when(t == 8)
    def _():
        second_ref[...] = jnp.zeros_like(second_ref)
        for z in range(2):
            at = z * 64
            second_ref[at : at + 16, :HEAD] = term_ref[z * 16 : z * 16 + 16, :].astype(LOW)


def attention_weight_grads(lefts, rights, terms):
    wide = pl.BlockSpec((ROWS, 512), lambda t: (0, jnp.minimum(t, 7)))
    return pl.pallas_call(
        attention_weight_kernel,
        grid=(9,),
        in_specs=[whole((ROWS, 256))] * 4 + [wide] * 4 + [whole((32, HEAD))],
        out_specs=[
            pl.BlockSpec((256, 512), lambda t: (0, jnp.minimum(t, 3))),
            pl.BlockSpec((256, 512), lambda t: (0, jnp.maximum(t - 4, 0))),
        ],
        out_shape=[shaped((256, 2048), LOW), shaped((256, 2560), LOW)],
        scratch_shapes=[pltpu.VMEM((256, 4 * ROWS), LOW), pltpu.VMEM((4 * ROWS, 512), LOW)],
        compiler_params=pltpu.CompilerParams(vmem_limit_bytes=16 * 2**20),
        cost_estimate=pl.CostEstimate(flops=10**9, bytes_accessed=6 * 2**20, transcendentals=0),
        name="attention_weight_grads",
    )(*held([*lefts, *rights, terms]))


def raw_grads_kernel(
    dq_ref, dkv_ref, raw_ref, gq_ref, gk_ref, cos_ref, sin_ref, right_ref, term_ref
):
    cosine, sine = cos_ref[...], sin_ref[...]
    for heads, first, place, gain_ref in ((16, 0, 0, gq_ref), (8, 16, HEAD, gk_ref)):
        gain = gain_ref[...]
        term = jnp.zeros((ROWS, HEAD), F32)
        for n in range(heads):
            grad = dq_ref[n // 2, n % 2] if first == 0 else dkv_ref[n, 0]
            grad = grad.astype(F32)
            raw = raw_ref[first + n]
            scale = scale_of(raw)
            unit = raw * scale
            grad = grad * cosine - turn(grad) * sine
            term = term + grad * unit
            grad = grad * gain
            grad = scale * (grad - unit * jnp.mean(grad * unit, axis=-1, keepdims=True))
            at = (first + n) * HEAD
            right_ref[:, at : at + HEAD] = grad.astype(LOW)
        term_ref[:, place : place + HEAD] = jnp.sum(term, axis=0, keepdims=True)
    for n in range(8):
        at = 3072 + n * HEAD
        right_ref[:, at : at + HEAD] = dkv_ref[n, 1]


def raw_grads(dq, dkv, raw, gain_q, gain_k, cosine, sine):
    return pl.pallas_call(
        raw_grads_kernel,
        in_specs=[pl.BlockSpec(memory_space=pltpu.VMEM)] * 7,
        out_shape=[shaped((ROWS, 4096), LOW), shaped((1, 2 * HEAD), F32)],
        compiler_params=pltpu.CompilerParams(vmem_limit_bytes=16 * 2**20),
        cost_estimate=pl.CostEstimate(
            flops=10**7, bytes_accessed=4 * 2**20, transcendentals=10**4
        ),
        name="raw_grads",
    )(*held([dq, dkv, raw, gain_q, gain_k, cosine, sine]))


def token_grads_kernel(shards, right_ref, x_ref, mid_ref, gain_ref, *rest):
    pieces, (grad_ref, term_ref, w, sems) = rest[:6], rest[6:]
    copies = fetch(shards, pieces, w, sems)
    x = x_ref[...].astype(F32)
    scale = scale_of(x)
    normal = x * scale
    settle(copies)
    dh = dot_t(right_ref[...], w[...])
    term_ref[...] = jnp.sum(dh * normal, axis=0, keepdims=True)
    dn = dh * gain_ref[...]
    grad_ref[...] = mid_ref[...] + scale * (
        dn - normal * jnp.mean(dn * normal, axis=-1, keepdims=True)
    )


def token_grads(shards, right, x, mid, gain, pieces):
    return pl.pallas_call(
        token_grads_kernel,
        in_specs=[smem()] + [pl.BlockSpec(memory_space=pltpu.VMEM)] * 4 + [anywhere()] * 6,
        out_shape=[shaped((ROWS, 1024), F32), shaped((1, 1024), F32)],
        scratch_shapes=[pltpu.VMEM((1024, 4096), LOW), pltpu.SemaphoreType.DMA((6,))],
        compiler_params=pltpu.CompilerParams(vmem_limit_bytes=32 * 2**20),
        cost_estimate=pl.CostEstimate(
            flops=10**9, bytes_accessed=12 * 2**20, transcendentals=10**4
        ),
        name="token_grads",
    )(shards, *held([right, x, mid, gain, *pieces]))


def visible(first_key, query_block, start):
    key = first_key + lax.broadcasted_iota(jnp.int32, (CHUNK, 2 * ROWS), 0)
    query = query_block * ROWS + (lax.broadcasted_iota(jnp.int32, (CHUNK, 2 * ROWS), 1) & (ROWS - 1))
    return (key <= query) & ((key >= start) | (query < start))


def block_of(info):
    i = pl.program_id(0)
    return (i // 2) * 8 + info[1] * 2 + i % 2


def forward_kernel(info, q_ref, kv0, kv1, kv2, kv3, o_ref, ot_ref, l_ref, k_ref, v_ref, vt):
    block = block_of(info)
    start = info[0]
    last = block // (CHUNK // ROWS)

    @pl.when(pl.program_id(0) == 0)
    def _():
        for back, piece in enumerate((kv0, kv1, kv2, kv3)):
            owner = lax.rem(info[1] + 4 - back, 4)
            for z in range(4):
                at = pl.ds(pl.multiple_of((z * 4 + owner) * 256, 256), 256)
                k_ref[at, :] = piece[2 * z : 2 * z + 2, 0].reshape(256, HEAD)
                v_ref[at, :] = piece[2 * z : 2 * z + 2, 1].reshape(256, HEAD)
        for c in range(vt.shape[0]):
            vt[c] = columns_of(v_ref[c * CHUNK : (c + 1) * CHUNK, :])

    q = q_ref[0]

    def step(c, carry, masked):
        total, mixed = carry
        keys = k_ref[pl.ds(pl.multiple_of(c * CHUNK, CHUNK), CHUNK), :]
        p = jnp.exp2(dot_t(keys, q) * EXP_SCALE)
        if masked:
            p = jnp.where(visible(c * CHUNK, block, start), p, 0.0)
        total = total + jnp.sum(p.reshape(CHUNK // 8, 8, 2 * ROWS), axis=0)
        mixed = mixed + dot_n(vt[c], p.astype(LOW))
        return total, mixed

    carry = (jnp.zeros((8, 2 * ROWS), F32), jnp.zeros((HEAD, 2 * ROWS), F32))
    carry = step(last, carry, True)
    carry = lax.fori_loop(0, jnp.minimum(last, 1), lambda c, x: step(c, x, True), carry)
    pairs = jnp.maximum(last - 1, 0) // 2
    carry = lax.fori_loop(
        0, pairs, lambda n, x: step(2 * n + 2, step(2 * n + 1, x, False), False), carry
    )
    carry = lax.fori_loop(2 * pairs + 1, last, lambda c, x: step(c, x, False), carry)
    total = jnp.sum(carry[0], axis=0, keepdims=True)
    mixed = carry[1] / total
    ot_ref[0] = mixed
    o_ref[0] = mixed.T.astype(LOW)
    l_ref[0] = jnp.log2(total)


def backward_kernel(
    info, q_ref, do_ref, ot_ref, l_ref, k_ref, v_ref, dq_ref, dkv_ref, kt, dk_acc, dv_acc
):
    i = pl.program_id(0)
    block = block_of(info)
    start = info[0]
    q = q_ref[0]
    do = do_ref[0]
    last = block // (CHUNK // ROWS)

    @pl.when(i == 0)
    def _():
        dk_acc[...] = jnp.zeros_like(dk_acc)
        dv_acc[...] = jnp.zeros_like(dv_acc)
        for c in range(kt.shape[0]):
            kt[c] = columns_of(k_ref[c * CHUNK : (c + 1) * CHUNK, :])

    delta = jnp.sum(do.astype(F32).T * ot_ref[0], axis=0, keepdims=True)
    logs = l_ref[0]

    def step(c, dqt, masked):
        at = pl.ds(pl.multiple_of(c * CHUNK, CHUNK), CHUNK)
        p = jnp.exp2(dot_t(k_ref[at, :], q) * EXP_SCALE - logs)
        if masked:
            p = jnp.where(visible(c * CHUNK, block, start), p, 0.0)
        dp = dot_t(v_ref[at, :], do)
        ds = (p * (dp - delta)).astype(LOW)
        dv_acc[at, :] += dot_n(p.astype(LOW), do)
        dk_acc[at, :] += dot_n(ds, q)
        return dqt + dot_n(kt[c], ds)

    dqt = step(last, jnp.zeros((HEAD, 2 * ROWS), F32), True)
    dqt = lax.fori_loop(0, jnp.minimum(last, 1), lambda c, x: step(c, x, True), dqt)
    pairs = jnp.maximum(last - 1, 0) // 2
    dqt = lax.fori_loop(
        0, pairs, lambda n, x: step(2 * n + 2, step(2 * n + 1, x, False), False), dqt
    )
    dqt = lax.fori_loop(2 * pairs + 1, last, lambda c, x: step(c, x, False), dqt)
    dq_ref[0] = (dqt * SCORE_SCALE).T.astype(LOW)

    @pl.when(i == pl.num_programs(0) - 1)
    def _():
        for z in range(4):
            for y in range(4):
                at = (z * 4 + y) * 256
                part = (dk_acc[at : at + 256, :] * SCORE_SCALE).astype(LOW)
                dkv_ref[y, 2 * z : 2 * z + 2, 0] = part.reshape(2, ROWS, HEAD)
                part = dv_acc[at : at + 256, :].astype(LOW)
                dkv_ref[y, 2 * z : 2 * z + 2, 1] = part.reshape(2, ROWS, HEAD)


def attention_forward(info, q, pieces):
    length = 32 * ROWS
    return pl.pallas_call(
        forward_kernel,
        grid=(8,),
        in_specs=[smem(), per_block((2 * ROWS, HEAD))] + [whole((8, 2, ROWS, HEAD))] * 4,
        out_specs=[
            per_block((2 * ROWS, HEAD)),
            per_block((HEAD, 2 * ROWS)),
            per_block((1, 2 * ROWS)),
            whole((length, HEAD)),
            whole((length, HEAD)),
        ],
        out_shape=[
            shaped((8, 2 * ROWS, HEAD), LOW),
            shaped((8, HEAD, 2 * ROWS), F32),
            shaped((8, 1, 2 * ROWS), F32),
            shaped((length, HEAD), LOW),
            shaped((length, HEAD), LOW),
        ],
        scratch_shapes=[pltpu.VMEM((length // CHUNK, HEAD, CHUNK), LOW)],
        compiler_params=pltpu.CompilerParams(vmem_limit_bytes=32 * 2**20),
        cost_estimate=pl.CostEstimate(
            flops=3 * 10**9, bytes_accessed=7 * 2**20, transcendentals=5 * 10**6
        ),
        name="attention_forward",
    )(info, *held([q, *pieces]))


def attention_backward(info, q, do, ot, logs, k, v):
    length = k.shape[0]
    return pl.pallas_call(
        backward_kernel,
        grid=(8,),
        in_specs=[
            smem(),
            per_block((2 * ROWS, HEAD)),
            per_block((2 * ROWS, HEAD)),
            per_block((HEAD, 2 * ROWS)),
            per_block((1, 2 * ROWS)),
            whole((length, HEAD)),
            whole((length, HEAD)),
        ],
        out_specs=[per_block((2 * ROWS, HEAD)), whole((4, 8, 2, ROWS, HEAD))],
        out_shape=[
            shaped((8, 2 * ROWS, HEAD), LOW),
            shaped((4, 8, 2, ROWS, HEAD), LOW),
        ],
        scratch_shapes=[
            pltpu.VMEM((length // CHUNK, HEAD, CHUNK), LOW),
            pltpu.VMEM((length, HEAD), F32),
            pltpu.VMEM((length, HEAD), F32),
        ],
        compiler_params=pltpu.CompilerParams(vmem_limit_bytes=32 * 2**20),
        cost_estimate=pl.CostEstimate(
            flops=8 * 10**9, bytes_accessed=10 * 2**20, transcendentals=5 * 10**6
        ),
        name="attention_backward",
    )(info, *held([q, do, ot, logs, k, v]))


def rotary_tables(where_at):
    half = HEAD // 2
    frequency = THETA ** (-(jnp.arange(half, dtype=F32) * 2.0) / HEAD)
    angles = where_at.astype(F32)[:, None] * frequency[None, :]
    cosine, sine = jnp.cos(angles), jnp.sin(angles)
    return jnp.concatenate([cosine, cosine], axis=-1), jnp.concatenate([-sine, sine], axis=-1)


def exchange_heads(value):
    return lax.all_to_all(value, ("z", "xh"), split_axis=0, concat_axis=0, tiled=True)


def pack_feed(w_gate, w_up, w_out, w_down):
    blocks = [w[:, n * 1024 : n * 1024 + 1024] for w in (w_gate, w_up) for n in range(3)]
    blocks += [w[n : n + 256] for w in (w_out, w_down) for n in range(0, w.shape[0], 256)]
    parts = []
    for first, end in FEED_CUTS:
        rows = []
        while first < end:
            block, off = divmod(first, 256)
            size = min(256 - off, end - first)
            rows.append(blocks[block][off : off + size])
            first += size
        parts.append(jnp.concatenate(rows, axis=0))
    return parts


def spread(value, across):
    return [value, core_swap(value), across, core_swap(across)]


def spread_columns(here, across, co):
    return [
        pick(here, co, 0),
        core_swap(pick(here, 1 - co, 0)),
        pick(across, co, 0),
        core_swap(pick(across, 1 - co, 0)),
    ]


def x_pair(value):
    return lax.ppermute(value, "xl", [(0, 1), (1, 0)])


def local(
    tokens,
    positions,
    attn_gain,
    w_query,
    w_key,
    w_value,
    query_gain,
    key_gain,
    w_out,
    ffn_gain,
    w_gate,
    w_up,
    w_down,
    cotangent,
):
    xl = lax.axis_index("xl")
    co = lax.axis_index("co")
    y = lax.axis_index("y")
    block = lax.axis_index("z") * 8 + y * 2 + lax.axis_index("xh")
    shard = xl * 2 + co
    shards = jnp.stack([shard, 2 * (1 - xl) + co, 2 * xl + 1 - co, 2 * (1 - xl) + 1 - co])
    shards = shards.astype(jnp.int32)
    cots = spread(cotangent, x_pair(cotangent))


    qkv_pieces = gather_weight(jnp.concatenate([w_query, w_key, w_value], axis=1))

    gains = jnp.concatenate([attn_gain, ffn_gain, query_gain, key_gain])
    gains = jnp.concatenate([gains, jnp.zeros((1024 - 576,), LOW)]).reshape(1, 8, 128)
    pair = jnp.concatenate([gains, x_pair(gains)], axis=0)
    pair = jnp.where(xl == 0, pair, pair[::-1])
    swapped = core_swap(pair)
    quad = jnp.where(co == 0, jnp.stack([pair, swapped], 1), jnp.stack([swapped, pair], 1))
    quad = quad.reshape(4, 1024).astype(F32)
    gain_one = quad[:, :256].reshape(1, 1024)
    gain_two = quad[:, 256:512].reshape(1, 1024)
    gain_query = quad[:, 512:544].reshape(1, 128)
    gain_key = quad[:, 544:576].reshape(1, 128)

    packed = pack_feed(w_gate, w_up, w_out, w_down)
    feed_across = [x_shift(packed[0], 1), x_shift(packed[1], -1)]

    start = block * ROWS + ROWS - 1 - positions[ROWS - 1]
    info = jnp.stack([start, y]).astype(jnp.int32)
    cosine, sine = rotary_tables(positions)
    query, kv_send, raw, left_one = project(
        shards, tokens, gain_one, gain_query, gain_key, cosine, sine, qkv_pieces
    )

    heads_send = jnp.concatenate([query.reshape(8, 2, ROWS, HEAD), kv_send], axis=1)
    heads_send, feed_across[0], feed_across[1] = lax.optimization_barrier(
        (heads_send, feed_across[0], feed_across[1])
    )
    heads = exchange_heads(heads_send)
    heads, packed[2], packed[3] = lax.optimization_barrier((heads, packed[2], packed[3]))
    kv = heads[:, 2:]
    q_all = heads[:, :2].reshape(8, 2 * ROWS, HEAD)
    kv_pieces = [kv, shift(kv, "y", 1), shift(kv, "y", 2), shift(kv, "y", 3)]
    feed_across += [x_shift(packed[2], 1), x_shift(packed[3], -1)]
    o_send, mixed_t, logs, k_all, v_all = attention_forward(info, q_all, kv_pieces)
    o_send, feed_across[2], feed_across[3] = lax.optimization_barrier(
        (o_send, feed_across[2], feed_across[3])
    )
    feed_pieces = packed + feed_across
    feed_pieces = feed_pieces + [core_swap(piece) for piece in feed_pieces]
    merged = exchange_heads(o_send).reshape(16, ROWS, HEAD)

    output, grad_middle, lefts, right, grad_merged, gain_two_term = feed(
        shards, merged, tokens, cotangent, gain_two, feed_pieces
    )

    do_all = exchange_heads(grad_merged.reshape(8, 2 * ROWS, HEAD))
    left_parts = spread_columns(pick(left_one, xl, 0), x_pair(pick(left_one, 1 - xl, 0)), co)
    head_parts = merged.reshape(2, 2, 4, ROWS, HEAD)
    head_parts = spread_columns(pick(head_parts, xl, 0), x_pair(pick(head_parts, 1 - xl, 0)), co)
    do_all, left_parts, head_parts, cots = lax.optimization_barrier(
        (do_all, left_parts, head_parts, cots)
    )
    right_across = x_pair(right)
    lefts_across = x_pair(pick(lefts, 1 - xl, 0))

    dq_all, dkv_all = attention_backward(info, q_all, do_all, mixed_t, logs, k_all, v_all)
    dkv = reduce_over(dkv_all, "y", 0)
    dq = exchange_heads(dq_all.reshape(8, 2, ROWS, HEAD))
    dkv, dq, right_across, lefts_across = lax.optimization_barrier(
        (dkv, dq, right_across, lefts_across)
    )
    dkv = exchange_heads(dkv)
    feed_part = feed_weight_grads(
        spread_columns(pick(lefts, xl, 0), lefts_across, co),
        head_parts,
        spread(right, right_across),
        cots,
    )
    dkv, feed_part = lax.optimization_barrier((dkv, feed_part))
    feed_second = lax.psum_scatter(feed_part[1], "z", scatter_dimension=0, tiled=True)

    attention_grads, head_terms = raw_grads(dq, dkv, raw, gain_query, gain_key, cosine, sine)
    attention_across = x_pair(attention_grads)
    head_terms, feed_first = lax.optimization_barrier((head_terms, feed_part[0]))
    feed_first = exchange_y(feed_first.reshape(4, 64, 6144))
    grad_tokens, gain_one_term = token_grads(
        shards, attention_grads, tokens, grad_middle, gain_one, qkv_pieces
    )
    terms = jnp.concatenate([gain_one_term, gain_two_term, head_terms], axis=1)
    terms = jnp.pad(terms.reshape(18, 128), ((0, 14), (0, 0)))
    terms = terms + core_swap(terms)
    terms = terms + x_pair(terms)
    attention_across, _ = lax.optimization_barrier((attention_across, gain_one_term))
    attention_part = attention_weight_grads(
        left_parts, spread(attention_grads, attention_across), terms
    )
    attention_part, feed_first, feed_second = lax.optimization_barrier(
        (attention_part, feed_first, feed_second)
    )
    attention_parts = send_first(*attention_part)
    feed_first = jnp.sum(feed_first.astype(F32), axis=0).astype(LOW)
    first, second = add_first(*attention_parts)
    first, second = reduce_second(
        jnp.concatenate([feed_first, first], axis=-1),
        jnp.concatenate([feed_second, second], axis=-1),
    )
    first = gather_over(add_xh(first), "z", 0)
    second = gather_over(add_xh(second), "y", 0)
    first = both_ways(first, "y")
    second = both_ways(second, "z")
    gain_all = lay_out(second, "z", [(7168, 7296)])[:18].reshape(2304)
    return (
        output,
        grad_tokens,
        lax.dynamic_slice_in_dim(gain_all, shard * 256, 256),
        lay_out(first, "y", [(6144, 8192)]),
        lay_out(second, "z", [(5120, 6144)]),
        lay_out(second, "z", [(6144, 7168)]),
        lax.dynamic_slice_in_dim(gain_all, 2048 + shard * 32, 32),
        lax.dynamic_slice_in_dim(gain_all, 2176 + shard * 32, 32),
        lay_out(second, "z", [(3072, 4096), (4096, 5120)]),
        lax.dynamic_slice_in_dim(gain_all, 1024 + shard * 256, 256),
        lay_out(first, "y", [(0, 3072)]),
        lay_out(first, "y", [(3072, 6144)]),
        lay_out(second, "z", [(0, 1024), (1024, 2048), (2048, 3072)]),
    )


def solution(mesh):
    axes = ("xl", "co", "z", "y", "xh")
    fine = Mesh(mesh.devices.reshape(2, 2, 4, 4, 2), axes)
    rows = P(axes, None)
    shard = P(("xl", "co"), None)
    vector = P(("xl", "co"))
    in_specs = (
        rows,
        P(axes),
        vector,
        shard,
        shard,
        shard,
        vector,
        vector,
        shard,
        vector,
        shard,
        shard,
        shard,
        rows,
    )
    out_specs = (
        rows,
        rows,
        vector,
        shard,
        shard,
        shard,
        vector,
        vector,
        shard,
        vector,
        shard,
        shard,
        shard,
    )
    return jax.shard_map(local, mesh=fine, in_specs=in_specs, out_specs=out_specs, check_vma=False)
```

```python
import jax
import jax.numpy as jnp
from jax import lax
from jax.experimental import pallas as pl
from jax.experimental.pallas import tpu as pltpu
from jax.sharding import Mesh
from jax.sharding import PartitionSpec as P

EPSILON = 1e-06
THETA = 1000000.0
HEAD = 128
ROWS = 128
CHUNK = 512
SCORE_SCALE = HEAD ** (-0.5)
LOG2_E = 1.4426950408889634
EXP_SCALE = SCORE_SCALE * LOG2_E
LOW = jnp.bfloat16
FEED_CUTS = ((0, 256), (1408, 1664), (256, 1408), (1664, 2816))
F32 = jnp.float32


def x_shift(value, step):
    pairs = []
    for x in range(4):
        to = (x + step) % 4
        pairs.append(((x % 2) * 2 + x // 2, (to % 2) * 2 + to // 2))
    return lax.ppermute(value, ("xl", "xh"), pairs)


def shift(value, axis, step):
    if axis == "x":
        return x_shift(value, step)
    return lax.ppermute(value, axis, [(i, (i + step) % 4) for i in range(4)])


def core_swap(value):
    return lax.ppermute(value, "co", [(0, 1), (1, 0)])


def place_on(axis):
    if axis == "x":
        return lax.axis_index("xh") * 2 + lax.axis_index("xl")
    return lax.axis_index(axis)


def pick(value, index, dim):
    return lax.dynamic_index_in_dim(value, index, dim, keepdims=False)


def send_parts(value, axis, dim):
    me = place_on(axis)
    got = [shift(pick(value, (me + step) % 4, dim), axis, step) for step in (1, 3, 2)]
    return [pick(value, me, dim)] + got


def add_parts(parts):
    total = parts[0].astype(F32)
    for part in parts[1:]:
        total = total + part.astype(F32)
    return total.astype(LOW)


def reduce_over(value, axis, dim):
    return add_parts(send_parts(value, axis, dim))


def gather_over(value, axis, dim, dtype=LOW):
    me = place_on(axis)
    shape = value.shape[:dim] + (4,) + value.shape[dim:]
    out = jnp.zeros(shape, dtype)
    out = lax.dynamic_update_index_in_dim(out, value.astype(dtype), me, dim)
    for step in (1, 3, 2):
        got = shift(value, axis, step).astype(dtype)
        out = lax.dynamic_update_index_in_dim(out, got, (me - step) % 4, dim)
    return out


def both_ways(value, axis):
    before = shift(value, axis, 1)
    after = shift(value, axis, -1)
    across = (shift(before[:2], axis, 1), shift(after[2:], axis, -1))
    return [(value, 0, 0), (before, 1, 0), (after, 3, 0), (across[0], 2, 0), (across[1], 2, 2)]


def lay_out(parts, axis, columns):
    me = place_on(axis)
    width = columns[0][1] - columns[0][0]
    out = jnp.zeros((len(columns), 4, 4, 16, width), F32)
    for part, back, first in parts:
        owner = (me - back) % 4
        piece = jnp.stack([part[..., a:b] for a, b in columns]).astype(F32)
        if axis == "y":
            at, piece = (owner, first), piece[:, None]
        else:
            at, piece = (first, owner), piece[:, :, None]
        out = lax.dynamic_update_slice(out, piece, (0, *at, 0, 0))
    return out.reshape(len(columns) * 256, width)


def exchange_y(value):
    return lax.all_to_all(value, "y", split_axis=0, concat_axis=0, tiled=True)


def send_first(first, second):
    first = exchange_y(first.reshape(4, 64, first.shape[-1]))
    return first, send_parts(second.reshape(4, 64, second.shape[-1]), "z", 0)


def add_first(first, second):
    return jnp.sum(first.astype(F32), axis=0).astype(LOW), add_parts(second)


def reduce_second(first, second):
    second = exchange_y(second.reshape(4, 16, second.shape[-1]))
    first = reduce_over(first.reshape(4, 16, first.shape[-1]), "z", 0)
    return first, jnp.sum(second.astype(F32), axis=0).astype(LOW)


def add_xh(part):
    other = lax.ppermute(part, "xh", [(0, 1), (1, 0)])
    return (part.astype(F32) + other.astype(F32)).astype(LOW)


def gather_weight(shard):
    half = shard.shape[0] // 2
    up = x_shift(shard[:half], 1)
    down = x_shift(shard[half:], -1)
    return [shard, up, down, core_swap(shard), core_swap(up), core_swap(down)]


def dot_t(left, right):
    return lax.dot_general(left, right, (((1,), (1,)), ((), ())), preferred_element_type=F32)


def dot_n(left, right):
    return lax.dot_general(left, right, (((1,), (0,)), ((), ())), preferred_element_type=F32)


def dot_r(left, right):
    return lax.dot_general(left, right, (((0,), (0,)), ((), ())), preferred_element_type=F32)


def whole(shape):
    return pl.BlockSpec(shape, lambda *_: (0,) * len(shape))


def per_block(shape):
    return pl.BlockSpec((1,) + shape, lambda i: (i,) + (0,) * len(shape))


def smem():
    return pl.BlockSpec(memory_space=pltpu.SMEM)


def anywhere():
    return pl.BlockSpec(memory_space=pl.ANY)


def shaped(shape, dtype):
    return pltpu.HBM(shape, dtype)


def held(arrays):
    return [pltpu.with_memory_space_constraint(array, pltpu.HBM) for array in arrays]


def fetch(shards, pieces, full, sems):
    rows = pieces[0].shape[0]
    half = rows // 2
    at = [
        shards[0] * rows,
        shards[1] * rows,
        shards[1] * rows + half,
        shards[2] * rows,
        shards[3] * rows,
        shards[3] * rows + half,
    ]
    copies = []
    for n, (piece, where) in enumerate(zip(pieces, at)):
        where = pl.multiple_of(where, half)
        copy = pltpu.make_async_copy(
            piece, full.at[pl.ds(where, piece.shape[0]), :], sems.at[n]
        )
        copy.start()
        copies.append(copy)
    return copies


def fetch_feed(shards, pieces, w_out, w_gu, w_down, sems):
    groups = ([], [], [], [], [])
    n = 0
    for s in range(4):
        for part, (first, end) in enumerate(FEED_CUTS):
            piece = pieces[len(FEED_CUTS) * s + part]
            at = 0
            while first + at < end:
                block, off = divmod(first + at, 256)
                size = min(256 - off, end - first - at)
                src = piece.at[pl.ds(at, size), :]
                if block < 6:
                    where = pl.multiple_of(shards[s] * 256 + off, 128)
                    dst = w_gu.at[pl.ds(where, size), pl.ds(block * 1024, 1024)]
                    group = (1, 3, 4)[block % 3]
                elif block < 8:
                    where = pl.multiple_of(shards[s] * 512 + (block - 6) * 256 + off, 128)
                    dst = w_out.at[pl.ds(where, size), :]
                    group = 0
                else:
                    where = pl.multiple_of(shards[s] * 768 + (block - 8) * 256 + off, 128)
                    dst = w_down.at[pl.ds(where, size), :]
                    group = 2
                groups[group].append(pltpu.make_async_copy(src, dst, sems.at[n]))
                n += 1
                at += size
    for group in groups:
        for copy in group:
            copy.start()
    return groups


def settle(copies):
    for copy in copies:
        copy.wait()


def scale_of(value):
    return lax.rsqrt(jnp.mean(value * value, axis=-1, keepdims=True) + EPSILON)


def turn(value):
    return jnp.concatenate([value[:, HEAD // 2 :], value[:, : HEAD // 2]], axis=1)


def project_kernel(
    shards, x_ref, gain_ref, gq_ref, gk_ref, cos_ref, sin_ref, *rest
):
    pieces, (q_ref, kv_ref, raw_ref, left_ref, w, sems) = rest[:6], rest[6:]
    copies = fetch(shards, pieces, w, sems)
    x = x_ref[...].astype(F32)
    h = (x * scale_of(x) * gain_ref[...]).astype(LOW)
    for f in range(4):
        left_ref[f // 2, f % 2] = h[:, f * 256 : f * 256 + 256]
    cosine, sine = cos_ref[...], sin_ref[...]
    settle(copies)
    for tile in range(8):
        product = dot_n(h, w[:, tile * 512 : tile * 512 + 512])
        for part in range(4):
            n = tile * 4 + part
            raw = product[:, part * HEAD : part * HEAD + HEAD]
            if n >= 24:
                kv_ref[n - 24, 1] = raw.astype(LOW)
                continue
            raw_ref[n] = raw
            gain = gq_ref[...] if n < 16 else gk_ref[...]
            u = raw * scale_of(raw) * gain
            u = (u * cosine + turn(u) * sine).astype(LOW)
            if n < 16:
                q_ref[n] = u
            else:
                kv_ref[n - 16, 0] = u


def project(shards, x, gain, gain_q, gain_k, cosine, sine, pieces):
    return pl.pallas_call(
        project_kernel,
        in_specs=[smem()] + [pl.BlockSpec(memory_space=pltpu.VMEM)] * 6 + [anywhere()] * 6,
        out_shape=[
            shaped((16, ROWS, HEAD), LOW),
            shaped((8, 2, ROWS, HEAD), LOW),
            shaped((24, ROWS, HEAD), F32),
            shaped((2, 2, ROWS, 256), LOW),
        ],
        scratch_shapes=[pltpu.VMEM((1024, 4096), LOW), pltpu.SemaphoreType.DMA((6,))],
        compiler_params=pltpu.CompilerParams(vmem_limit_bytes=32 * 2**20),
        cost_estimate=pl.CostEstimate(
            flops=10**9, bytes_accessed=12 * 2**20, transcendentals=10**4
        ),
        name="project",
    )(shards, x, gain, gain_q, gain_k, cosine, sine, *pieces)


def feed_kernel(shards, o_ref, x_ref, cot_ref, gain_ref, *rest):
    (y_ref, mid_ref, left_ref, right_ref, do_ref, term_ref) = rest[16:22]
    (w_out, w_gu, w_down, merged, sems) = rest[22:]
    out_copies, gu_copies, down_copies, gu_next, gu_last = fetch_feed(shards, rest[:16], w_out, w_gu, w_down, sems)
    for n in range(16):
        merged[:, n * HEAD : n * HEAD + HEAD] = o_ref[n]
    cot = cot_ref[...]
    gain = gain_ref[...]
    settle(out_copies)
    middle = x_ref[...].astype(F32) + dot_n(merged[...], w_out[...])
    scale = scale_of(middle)
    normal = middle * scale
    h = (normal * gain).astype(LOW)
    for f in range(4):
        left_ref[f // 2, f % 2, 0] = h[:, f * 256 : f * 256 + 256]
    settle(gu_copies)
    settle(down_copies)
    total = middle
    dh = jnp.zeros_like(middle)
    for tile in range(6):
        if tile == 2:
            settle(gu_next)
        if tile == 4:
            settle(gu_last)
        at = tile * 512
        gate = dot_n(h, w_gu[:, at : at + 512])
        up = dot_n(h, w_gu[:, 3072 + at : 3072 + at + 512])
        sg = 1.0 / (1.0 + jnp.exp(-gate))
        swish = gate * sg
        hidden = (swish * up).astype(LOW)
        for part in range(2):
            f, g = divmod(tile * 2 + part, 3)
            left_ref[f // 2, f % 2, 1 + g] = hidden[:, part * 256 : part * 256 + 256]
        total = total + dot_n(hidden, w_down[at : at + 512, :])
        dhidden = dot_t(cot, w_down[at : at + 512, :])
        dgate = (dhidden * up * sg * (1.0 + gate * (1.0 - sg))).astype(LOW)
        dup = (dhidden * swish).astype(LOW)
        right_ref[:, at : at + 512] = dgate
        right_ref[:, 3072 + at : 3072 + at + 512] = dup
        dh = dh + dot_t(dgate, w_gu[:, at : at + 512])
        dh = dh + dot_t(dup, w_gu[:, 3072 + at : 3072 + at + 512])
    y_ref[...] = total.astype(LOW)
    term_ref[...] = jnp.sum(dh * normal, axis=0, keepdims=True)
    dn = dh * gain
    dmid = cot.astype(F32) + scale * (dn - normal * jnp.mean(dn * normal, axis=-1, keepdims=True))
    mid_ref[...] = dmid
    da = dmid.astype(LOW)
    right_ref[:, 6144:] = da
    for tile in range(4):
        back = dot_t(da, w_out[tile * 512 : tile * 512 + 512, :]).astype(LOW)
        for part in range(4):
            do_ref[tile * 4 + part] = back[:, part * HEAD : part * HEAD + HEAD]


def feed(shards, o, x, cot, gain, pieces):
    return pl.pallas_call(
        feed_kernel,
        in_specs=[smem()] + [pl.BlockSpec(memory_space=pltpu.VMEM)] * 4 + [anywhere()] * 16,
        out_shape=[
            shaped((ROWS, 1024), LOW),
            shaped((ROWS, 1024), F32),
            shaped((2, 2, 4, ROWS, 256), LOW),
            shaped((ROWS, 7168), LOW),
            shaped((16, ROWS, HEAD), LOW),
            shaped((1, 1024), F32),
        ],
        scratch_shapes=[
            pltpu.VMEM((2048, 1024), LOW),
            pltpu.VMEM((1024, 6144), LOW),
            pltpu.VMEM((3072, 1024), LOW),
            pltpu.VMEM((ROWS, 2048), LOW),
            pltpu.SemaphoreType.DMA((52,)),
        ],
        compiler_params=pltpu.CompilerParams(vmem_limit_bytes=48 * 2**20),
        cost_estimate=pl.CostEstimate(
            flops=7 * 10**9, bytes_accessed=30 * 2**20, transcendentals=10**6
        ),
        name="feed",
    )(shards, *held([o, x, cot, gain, *pieces]))


def columns_of(value):
    return value.astype(F32).T.astype(LOW)


def lay_left(left_t, part, left, turned):
    columns = columns_of(left)
    at = slice(part * ROWS, part * ROWS + ROWS)
    if not turned:
        left_t[:, at] = columns
        return
    for y in range(4):
        for z in range(4):
            to, row = (z * 4 + y) * 16, (y * 4 + z) * 16
            left_t[to : to + 16, at] = columns[row : row + 16, :]


def weight_kernel(*refs):
    lefts, heads, rights, cots = refs[:4], refs[4:8], refs[8:12], refs[12:16]
    first_ref, second_ref, left_t, right = refs[16:]
    t = pl.program_id(0)

    @pl.when(t == 0)
    def _():
        for part in range(4):
            lay_left(left_t, part, lefts[part][0], False)

    @pl.when((t >= 6) & (t < 9))
    def _():
        for part in range(4):
            lay_left(left_t, part, lefts[part][0], True)

    for group in range(2):

        @pl.when(t == 9 + group)
        def _():
            for part in range(4):
                pair = [heads[part][2 * group], heads[part][2 * group + 1]]
                lay_left(left_t, part, jnp.concatenate(pair, axis=1), True)

    @pl.when((t < 6) | (t >= 9))
    def _():
        for part in range(4):
            right[part * ROWS : part * ROWS + ROWS, :] = rights[part][...]

    @pl.when(t == 6)
    def _():
        for part in range(4):
            right[part * ROWS : part * ROWS + ROWS, :] = cots[part][...]

    @pl.when(t < 6)
    def _():
        first_ref[...] = dot_n(left_t[...], right[...]).astype(LOW)

    @pl.when(t >= 6)
    def _():
        second_ref[...] = dot_n(left_t[...], right[...]).astype(LOW)


def feed_weight_grads(lefts, heads, rights, cots):
    left = pl.BlockSpec((1, ROWS, 256), lambda t: (jnp.clip(t - 5, 0, 3), 0, 0))
    wide = pl.BlockSpec((ROWS, 1024), lambda t: (0, jnp.where(t < 6, t, jnp.where(t < 9, 5, 6))))
    return pl.pallas_call(
        weight_kernel,
        grid=(11,),
        in_specs=[left] * 4 + [whole((4, ROWS, HEAD))] * 4 + [wide] * 4 + [whole((ROWS, 1024))] * 4,
        out_specs=[
            pl.BlockSpec((256, 1024), lambda t: (0, jnp.minimum(t, 5))),
            pl.BlockSpec((256, 1024), lambda t: (0, jnp.maximum(t - 6, 0))),
        ],
        out_shape=[shaped((256, 6144), LOW), shaped((256, 5120), LOW)],
        scratch_shapes=[pltpu.VMEM((256, 4 * ROWS), LOW), pltpu.VMEM((4 * ROWS, 1024), LOW)],
        compiler_params=pltpu.CompilerParams(vmem_limit_bytes=24 * 2**20),
        cost_estimate=pl.CostEstimate(
            flops=3 * 10**9, bytes_accessed=16 * 2**20, transcendentals=0
        ),
        name="feed_weight_grads",
    )(*held([*lefts, *heads, *rights, *cots]))


def attention_weight_kernel(*refs):
    lefts, rights, (term_ref, first_ref, second_ref, left_t, right) = refs[:4], refs[4:8], refs[8:]
    t = pl.program_id(0)

    @pl.when(t == 0)
    def _():
        for part in range(4):
            lay_left(left_t, part, lefts[part][...], False)

    @pl.when(t == 4)
    def _():
        for part in range(4):
            lay_left(left_t, part, lefts[part][...], True)

    for part in range(4):
        right[part * ROWS : part * ROWS + ROWS, :] = rights[part][...]

    @pl.when(t < 4)
    def _():
        first_ref[...] = dot_n(left_t[...], right[...]).astype(LOW)

    @pl.when((t >= 4) & (t < 8))
    def _():
        second_ref[...] = dot_n(left_t[...], right[...]).astype(LOW)

    @pl.when(t == 8)
    def _():
        second_ref[...] = jnp.zeros_like(second_ref)
        for z in range(2):
            at = z * 64
            second_ref[at : at + 16, :HEAD] = term_ref[z * 16 : z * 16 + 16, :].astype(LOW)


def attention_weight_grads(lefts, rights, terms):
    wide = pl.BlockSpec((ROWS, 512), lambda t: (0, jnp.minimum(t, 7)))
    return pl.pallas_call(
        attention_weight_kernel,
        grid=(9,),
        in_specs=[whole((ROWS, 256))] * 4 + [wide] * 4 + [whole((32, HEAD))],
        out_specs=[
            pl.BlockSpec((256, 512), lambda t: (0, jnp.minimum(t, 3))),
            pl.BlockSpec((256, 512), lambda t: (0, jnp.maximum(t - 4, 0))),
        ],
        out_shape=[shaped((256, 2048), LOW), shaped((256, 2560), LOW)],
        scratch_shapes=[pltpu.VMEM((256, 4 * ROWS), LOW), pltpu.VMEM((4 * ROWS, 512), LOW)],
        compiler_params=pltpu.CompilerParams(vmem_limit_bytes=16 * 2**20),
        cost_estimate=pl.CostEstimate(flops=10**9, bytes_accessed=6 * 2**20, transcendentals=0),
        name="attention_weight_grads",
    )(*held([*lefts, *rights, terms]))


def raw_grads_kernel(
    dq_ref, dkv_ref, raw_ref, gq_ref, gk_ref, cos_ref, sin_ref, right_ref, term_ref
):
    cosine, sine = cos_ref[...], sin_ref[...]
    for heads, first, place, gain_ref in ((16, 0, 0, gq_ref), (8, 16, HEAD, gk_ref)):
        gain = gain_ref[...]
        term = jnp.zeros((ROWS, HEAD), F32)
        for n in range(heads):
            grad = dq_ref[n // 2, n % 2] if first == 0 else dkv_ref[n, 0]
            grad = grad.astype(F32)
            raw = raw_ref[first + n]
            scale = scale_of(raw)
            unit = raw * scale
            grad = grad * cosine - turn(grad) * sine
            term = term + grad * unit
            grad = grad * gain
            grad = scale * (grad - unit * jnp.mean(grad * unit, axis=-1, keepdims=True))
            at = (first + n) * HEAD
            right_ref[:, at : at + HEAD] = grad.astype(LOW)
        term_ref[:, place : place + HEAD] = jnp.sum(term, axis=0, keepdims=True)
    for n in range(8):
        at = 3072 + n * HEAD
        right_ref[:, at : at + HEAD] = dkv_ref[n, 1]


def raw_grads(dq, dkv, raw, gain_q, gain_k, cosine, sine):
    return pl.pallas_call(
        raw_grads_kernel,
        in_specs=[pl.BlockSpec(memory_space=pltpu.VMEM)] * 7,
        out_shape=[shaped((ROWS, 4096), LOW), shaped((1, 2 * HEAD), F32)],
        compiler_params=pltpu.CompilerParams(vmem_limit_bytes=16 * 2**20),
        cost_estimate=pl.CostEstimate(
            flops=10**7, bytes_accessed=4 * 2**20, transcendentals=10**4
        ),
        name="raw_grads",
    )(*held([dq, dkv, raw, gain_q, gain_k, cosine, sine]))


def token_grads_kernel(shards, right_ref, x_ref, mid_ref, gain_ref, *rest):
    pieces, (grad_ref, term_ref, w, sems) = rest[:6], rest[6:]
    copies = fetch(shards, pieces, w, sems)
    x = x_ref[...].astype(F32)
    scale = scale_of(x)
    normal = x * scale
    settle(copies)
    dh = dot_t(right_ref[...], w[...])
    term_ref[...] = jnp.sum(dh * normal, axis=0, keepdims=True)
    dn = dh * gain_ref[...]
    grad_ref[...] = mid_ref[...] + scale * (
        dn - normal * jnp.mean(dn * normal, axis=-1, keepdims=True)
    )


def token_grads(shards, right, x, mid, gain, pieces):
    return pl.pallas_call(
        token_grads_kernel,
        in_specs=[smem()] + [pl.BlockSpec(memory_space=pltpu.VMEM)] * 4 + [anywhere()] * 6,
        out_shape=[shaped((ROWS, 1024), F32), shaped((1, 1024), F32)],
        scratch_shapes=[pltpu.VMEM((1024, 4096), LOW), pltpu.SemaphoreType.DMA((6,))],
        compiler_params=pltpu.CompilerParams(vmem_limit_bytes=32 * 2**20),
        cost_estimate=pl.CostEstimate(
            flops=10**9, bytes_accessed=12 * 2**20, transcendentals=10**4
        ),
        name="token_grads",
    )(shards, *held([right, x, mid, gain, *pieces]))


def visible(first_key, query_block, start):
    key = first_key + lax.broadcasted_iota(jnp.int32, (CHUNK, 2 * ROWS), 0)
    query = query_block * ROWS + (lax.broadcasted_iota(jnp.int32, (CHUNK, 2 * ROWS), 1) & (ROWS - 1))
    return (key <= query) & ((key >= start) | (query < start))


def block_of(info):
    i = pl.program_id(0)
    return (i // 2) * 8 + info[1] * 2 + i % 2


def forward_kernel(info, q_ref, kv0, kv1, kv2, kv3, o_ref, ot_ref, l_ref, k_ref, v_ref, vt):
    block = block_of(info)
    start = info[0]
    last = block // (CHUNK // ROWS)

    @pl.when(pl.program_id(0) == 0)
    def _():
        for back, piece in enumerate((kv0, kv1, kv2, kv3)):
            owner = lax.rem(info[1] + 4 - back, 4)
            for z in range(4):
                at = pl.ds(pl.multiple_of((z * 4 + owner) * 256, 256), 256)
                k_ref[at, :] = piece[2 * z : 2 * z + 2, 0].reshape(256, HEAD)
                v_ref[at, :] = piece[2 * z : 2 * z + 2, 1].reshape(256, HEAD)
        for c in range(vt.shape[0]):
            vt[c] = columns_of(v_ref[c * CHUNK : (c + 1) * CHUNK, :])

    q = q_ref[0]

    def step(c, carry, masked):
        total, mixed = carry
        keys = k_ref[pl.ds(pl.multiple_of(c * CHUNK, CHUNK), CHUNK), :]
        p = jnp.exp2(dot_t(keys, q) * EXP_SCALE)
        if masked:
            p = jnp.where(visible(c * CHUNK, block, start), p, 0.0)
        total = total + jnp.sum(p.reshape(CHUNK // 8, 8, 2 * ROWS), axis=0)
        mixed = mixed + dot_n(vt[c], p.astype(LOW))
        return total, mixed

    carry = (jnp.zeros((8, 2 * ROWS), F32), jnp.zeros((HEAD, 2 * ROWS), F32))
    carry = step(last, carry, True)
    carry = lax.fori_loop(0, jnp.minimum(last, 1), lambda c, x: step(c, x, True), carry)
    pairs = jnp.maximum(last - 1, 0) // 2
    carry = lax.fori_loop(
        0, pairs, lambda n, x: step(2 * n + 2, step(2 * n + 1, x, False), False), carry
    )
    carry = lax.fori_loop(2 * pairs + 1, last, lambda c, x: step(c, x, False), carry)
    total = jnp.sum(carry[0], axis=0, keepdims=True)
    mixed = carry[1] / total
    ot_ref[0] = mixed
    o_ref[0] = mixed.T.astype(LOW)
    l_ref[0] = jnp.log2(total)


def backward_kernel(
    info, q_ref, do_ref, ot_ref, l_ref, k_ref, v_ref, dq_ref, dkv_ref, kt, dk_acc, dv_acc
):
    i = pl.program_id(0)
    block = block_of(info)
    start = info[0]
    q = q_ref[0]
    do = do_ref[0]
    last = block // (CHUNK // ROWS)

    @pl.when(i == 0)
    def _():
        dk_acc[...] = jnp.zeros_like(dk_acc)
        dv_acc[...] = jnp.zeros_like(dv_acc)
        for c in range(kt.shape[0]):
            kt[c] = columns_of(k_ref[c * CHUNK : (c + 1) * CHUNK, :])

    delta = jnp.sum(do.astype(F32).T * ot_ref[0], axis=0, keepdims=True)
    logs = l_ref[0]

    def step(c, dqt, masked):
        at = pl.ds(pl.multiple_of(c * CHUNK, CHUNK), CHUNK)
        p = jnp.exp2(dot_t(k_ref[at, :], q) * EXP_SCALE - logs)
        if masked:
            p = jnp.where(visible(c * CHUNK, block, start), p, 0.0)
        dp = dot_t(v_ref[at, :], do)
        ds = (p * (dp - delta)).astype(LOW)
        dv_acc[at, :] += dot_n(p.astype(LOW), do)
        dk_acc[at, :] += dot_n(ds, q)
        return dqt + dot_n(kt[c], ds)

    dqt = step(last, jnp.zeros((HEAD, 2 * ROWS), F32), True)
    dqt = lax.fori_loop(0, jnp.minimum(last, 1), lambda c, x: step(c, x, True), dqt)
    pairs = jnp.maximum(last - 1, 0) // 2
    dqt = lax.fori_loop(
        0, pairs, lambda n, x: step(2 * n + 2, step(2 * n + 1, x, False), False), dqt
    )
    dqt = lax.fori_loop(2 * pairs + 1, last, lambda c, x: step(c, x, False), dqt)
    dq_ref[0] = (dqt * SCORE_SCALE).T.astype(LOW)

    @pl.when(i == pl.num_programs(0) - 1)
    def _():
        for z in range(4):
            for y in range(4):
                at = (z * 4 + y) * 256
                part = (dk_acc[at : at + 256, :] * SCORE_SCALE).astype(LOW)
                dkv_ref[y, 2 * z : 2 * z + 2, 0] = part.reshape(2, ROWS, HEAD)
                part = dv_acc[at : at + 256, :].astype(LOW)
                dkv_ref[y, 2 * z : 2 * z + 2, 1] = part.reshape(2, ROWS, HEAD)


def attention_forward(info, q, pieces):
    length = 32 * ROWS
    return pl.pallas_call(
        forward_kernel,
        grid=(8,),
        in_specs=[smem(), per_block((2 * ROWS, HEAD))] + [whole((8, 2, ROWS, HEAD))] * 4,
        out_specs=[
            per_block((2 * ROWS, HEAD)),
            per_block((HEAD, 2 * ROWS)),
            per_block((1, 2 * ROWS)),
            whole((length, HEAD)),
            whole((length, HEAD)),
        ],
        out_shape=[
            shaped((8, 2 * ROWS, HEAD), LOW),
            shaped((8, HEAD, 2 * ROWS), F32),
            shaped((8, 1, 2 * ROWS), F32),
            shaped((length, HEAD), LOW),
            shaped((length, HEAD), LOW),
        ],
        scratch_shapes=[pltpu.VMEM((length // CHUNK, HEAD, CHUNK), LOW)],
        compiler_params=pltpu.CompilerParams(vmem_limit_bytes=32 * 2**20),
        cost_estimate=pl.CostEstimate(
            flops=3 * 10**9, bytes_accessed=7 * 2**20, transcendentals=5 * 10**6
        ),
        name="attention_forward",
    )(info, *held([q, *pieces]))


def attention_backward(info, q, do, ot, logs, k, v):
    length = k.shape[0]
    return pl.pallas_call(
        backward_kernel,
        grid=(8,),
        in_specs=[
            smem(),
            per_block((2 * ROWS, HEAD)),
            per_block((2 * ROWS, HEAD)),
            per_block((HEAD, 2 * ROWS)),
            per_block((1, 2 * ROWS)),
            whole((length, HEAD)),
            whole((length, HEAD)),
        ],
        out_specs=[per_block((2 * ROWS, HEAD)), whole((4, 8, 2, ROWS, HEAD))],
        out_shape=[
            shaped((8, 2 * ROWS, HEAD), LOW),
            shaped((4, 8, 2, ROWS, HEAD), LOW),
        ],
        scratch_shapes=[
            pltpu.VMEM((length // CHUNK, HEAD, CHUNK), LOW),
            pltpu.VMEM((length, HEAD), F32),
            pltpu.VMEM((length, HEAD), F32),
        ],
        compiler_params=pltpu.CompilerParams(vmem_limit_bytes=32 * 2**20),
        cost_estimate=pl.CostEstimate(
            flops=8 * 10**9, bytes_accessed=10 * 2**20, transcendentals=5 * 10**6
        ),
        name="attention_backward",
    )(info, *held([q, do, ot, logs, k, v]))


def rotary_tables(where_at):
    half = HEAD // 2
    frequency = THETA ** (-(jnp.arange(half, dtype=F32) * 2.0) / HEAD)
    angles = where_at.astype(F32)[:, None] * frequency[None, :]
    cosine, sine = jnp.cos(angles), jnp.sin(angles)
    return jnp.concatenate([cosine, cosine], axis=-1), jnp.concatenate([-sine, sine], axis=-1)


def exchange_heads(value):
    return lax.all_to_all(value, ("z", "xh"), split_axis=0, concat_axis=0, tiled=True)


def pack_feed(w_gate, w_up, w_out, w_down):
    blocks = [w[:, n * 1024 : n * 1024 + 1024] for w in (w_gate, w_up) for n in range(3)]
    blocks += [w[n : n + 256] for w in (w_out, w_down) for n in range(0, w.shape[0], 256)]
    parts = []
    for first, end in FEED_CUTS:
        rows = []
        while first < end:
            block, off = divmod(first, 256)
            size = min(256 - off, end - first)
            rows.append(blocks[block][off : off + size])
            first += size
        parts.append(jnp.concatenate(rows, axis=0))
    return parts


def spread(value, across):
    return [value, core_swap(value), across, core_swap(across)]


def spread_columns(here, across, co):
    return [
        pick(here, co, 0),
        core_swap(pick(here, 1 - co, 0)),
        pick(across, co, 0),
        core_swap(pick(across, 1 - co, 0)),
    ]


def x_pair(value):
    return lax.ppermute(value, "xl", [(0, 1), (1, 0)])


def local(
    tokens,
    positions,
    attn_gain,
    w_query,
    w_key,
    w_value,
    query_gain,
    key_gain,
    w_out,
    ffn_gain,
    w_gate,
    w_up,
    w_down,
    cotangent,
):
    xl = lax.axis_index("xl")
    co = lax.axis_index("co")
    y = lax.axis_index("y")
    block = lax.axis_index("z") * 8 + y * 2 + lax.axis_index("xh")
    shard = xl * 2 + co
    shards = jnp.stack([shard, 2 * (1 - xl) + co, 2 * xl + 1 - co, 2 * (1 - xl) + 1 - co])
    shards = shards.astype(jnp.int32)
    cots = spread(cotangent, x_pair(cotangent))


    qkv_pieces = gather_weight(jnp.concatenate([w_query, w_key, w_value], axis=1))

    gains = jnp.concatenate([attn_gain, ffn_gain, query_gain, key_gain])
    gains = jnp.concatenate([gains, jnp.zeros((1024 - 576,), LOW)]).reshape(1, 8, 128)
    pair = jnp.concatenate([gains, x_pair(gains)], axis=0)
    pair = jnp.where(xl == 0, pair, pair[::-1])
    swapped = core_swap(pair)
    quad = jnp.where(co == 0, jnp.stack([pair, swapped], 1), jnp.stack([swapped, pair], 1))
    quad = quad.reshape(4, 1024).astype(F32)
    gain_one = quad[:, :256].reshape(1, 1024)
    gain_two = quad[:, 256:512].reshape(1, 1024)
    gain_query = quad[:, 512:544].reshape(1, 128)
    gain_key = quad[:, 544:576].reshape(1, 128)

    packed = pack_feed(w_gate, w_up, w_out, w_down)
    feed_across = [x_shift(packed[0], 1), x_shift(packed[1], -1)]

    start = block * ROWS + ROWS - 1 - positions[ROWS - 1]
    info = jnp.stack([start, y]).astype(jnp.int32)
    cosine, sine = rotary_tables(positions)
    query, kv_send, raw, left_one = project(
        shards, tokens, gain_one, gain_query, gain_key, cosine, sine, qkv_pieces
    )

    heads_send = jnp.concatenate([query.reshape(8, 2, ROWS, HEAD), kv_send], axis=1)
    heads_send, feed_across[0], feed_across[1] = lax.optimization_barrier(
        (heads_send, feed_across[0], feed_across[1])
    )
    heads = exchange_heads(heads_send)
    heads, packed[2], packed[3] = lax.optimization_barrier((heads, packed[2], packed[3]))
    kv = heads[:, 2:]
    q_all = heads[:, :2].reshape(8, 2 * ROWS, HEAD)
    kv_pieces = [kv, shift(kv, "y", 1), shift(kv, "y", 2), shift(kv, "y", 3)]
    feed_across += [x_shift(packed[2], 1), x_shift(packed[3], -1)]
    o_send, mixed_t, logs, k_all, v_all = attention_forward(info, q_all, kv_pieces)
    merged = exchange_heads(o_send).reshape(16, ROWS, HEAD)
    merged, feed_across[2], feed_across[3] = lax.optimization_barrier(
        (merged, feed_across[2], feed_across[3])
    )
    feed_pieces = packed + feed_across
    feed_pieces = feed_pieces + [core_swap(piece) for piece in feed_pieces]

    output, grad_middle, lefts, right, grad_merged, gain_two_term = feed(
        shards, merged, tokens, cotangent, gain_two, feed_pieces
    )

    do_all = exchange_heads(grad_merged.reshape(8, 2 * ROWS, HEAD))
    left_parts = spread_columns(pick(left_one, xl, 0), x_pair(pick(left_one, 1 - xl, 0)), co)
    head_parts = merged.reshape(2, 2, 4, ROWS, HEAD)
    head_parts = spread_columns(pick(head_parts, xl, 0), x_pair(pick(head_parts, 1 - xl, 0)), co)
    do_all, left_parts, head_parts, cots = lax.optimization_barrier(
        (do_all, left_parts, head_parts, cots)
    )
    right_across = x_pair(right)
    lefts_across = x_pair(pick(lefts, 1 - xl, 0))

    dq_all, dkv_all = attention_backward(info, q_all, do_all, mixed_t, logs, k_all, v_all)
    dkv = reduce_over(dkv_all, "y", 0)
    dq = exchange_heads(dq_all.reshape(8, 2, ROWS, HEAD))
    dkv, dq, right_across, lefts_across = lax.optimization_barrier(
        (dkv, dq, right_across, lefts_across)
    )
    dkv = exchange_heads(dkv)
    feed_part = feed_weight_grads(
        spread_columns(pick(lefts, xl, 0), lefts_across, co),
        head_parts,
        spread(right, right_across),
        cots,
    )
    dkv, feed_part = lax.optimization_barrier((dkv, feed_part))
    feed_second = lax.psum_scatter(feed_part[1], "z", scatter_dimension=0, tiled=True)

    attention_grads, head_terms = raw_grads(dq, dkv, raw, gain_query, gain_key, cosine, sine)
    attention_across = x_pair(attention_grads)
    head_terms, feed_first = lax.optimization_barrier((head_terms, feed_part[0]))
    feed_first = exchange_y(feed_first.reshape(4, 64, 6144))
    grad_tokens, gain_one_term = token_grads(
        shards, attention_grads, tokens, grad_middle, gain_one, qkv_pieces
    )
    terms = jnp.concatenate([gain_one_term, gain_two_term, head_terms], axis=1)
    terms = jnp.pad(terms.reshape(18, 128), ((0, 14), (0, 0)))
    terms = terms + core_swap(terms)
    terms = terms + x_pair(terms)
    attention_across, _ = lax.optimization_barrier((attention_across, gain_one_term))
    attention_part = attention_weight_grads(
        left_parts, spread(attention_grads, attention_across), terms
    )
    attention_part, feed_first, feed_second = lax.optimization_barrier(
        (attention_part, feed_first, feed_second)
    )
    attention_parts = send_first(*attention_part)
    feed_first = jnp.sum(feed_first.astype(F32), axis=0).astype(LOW)
    first, second = add_first(*attention_parts)
    first, second = reduce_second(
        jnp.concatenate([feed_first, first], axis=-1),
        jnp.concatenate([feed_second, second], axis=-1),
    )
    first = gather_over(add_xh(first), "z", 0)
    second = gather_over(add_xh(second), "y", 0)
    first = both_ways(first, "y")
    second = both_ways(second, "z")
    gain_all = lay_out(second, "z", [(7168, 7296)])[:18].reshape(2304)
    return (
        output,
        grad_tokens,
        lax.dynamic_slice_in_dim(gain_all, shard * 256, 256),
        lay_out(first, "y", [(6144, 8192)]),
        lay_out(second, "z", [(5120, 6144)]),
        lay_out(second, "z", [(6144, 7168)]),
        lax.dynamic_slice_in_dim(gain_all, 2048 + shard * 32, 32),
        lax.dynamic_slice_in_dim(gain_all, 2176 + shard * 32, 32),
        lay_out(second, "z", [(3072, 4096), (4096, 5120)]),
        lax.dynamic_slice_in_dim(gain_all, 1024 + shard * 256, 256),
        lay_out(first, "y", [(0, 3072)]),
        lay_out(first, "y", [(3072, 6144)]),
        lay_out(second, "z", [(0, 1024), (1024, 2048), (2048, 3072)]),
    )


def solution(mesh):
    axes = ("xl", "co", "z", "y", "xh")
    fine = Mesh(mesh.devices.reshape(2, 2, 4, 4, 2), axes)
    rows = P(axes, None)
    shard = P(("xl", "co"), None)
    vector = P(("xl", "co"))
    in_specs = (
        rows,
        P(axes),
        vector,
        shard,
        shard,
        shard,
        vector,
        vector,
        shard,
        vector,
        shard,
        shard,
        shard,
        rows,
    )
    out_specs = (
        rows,
        rows,
        vector,
        shard,
        shard,
        shard,
        vector,
        vector,
        shard,
        vector,
        shard,
        shard,
        shard,
    )
    return jax.shard_map(local, mesh=fine, in_specs=in_specs, out_specs=out_specs, check_vma=False)
```
